32 devices in a mesh: groups: 2 (over y), ctx: 4 (over x, core), head: 4 (over z).
Axes of the slice: x: 2, y: 2, z: 4, core: 2. Of those that a mesh axis runs over, the one named last changes fastest.
Arguments:
- features: bfloat16 [4, 3072, 8192], P('groups', 'ctx', 'head'), parts along dimension 0, may hold values from -6 to 6
- gate_in: bfloat16 [4, 3072, 8192], P('groups', 'ctx', 'head'), parts along dimension 0, may hold values from -240 to 240
- state_proj: bfloat16 [2, 4, 128, 3072], P(None, 'groups', 'head', 'ctx'), parts along dimension 1, may hold values from -3 to 3
- step_size: float32 [4, 128, 3072], P('groups', 'head', 'ctx'), parts along dimension 0, may hold values from 0.01 to 0.1
- log_decay: float32 [4, 128, 3072], P('groups', 'head', 'ctx'), parts along dimension 0, may hold values from -1 to 0
- skip_gain: float32 [128], P('head'), may hold values from 0.5 to 2
- norm_gain: float32 [8192], P('head'), may hold values from 0.5 to 1.5
Outputs:
- output: bfloat16 [4, 3072, 8192], P('groups', 'ctx', 'head'), parts along dimension 0
The draws below stay inside these ranges and needn't reach their ends.
There are 2 independent parts, one for each index of `groups`. The reference program is written for one: setup_inputs(seed, part) draws one part's arguments, and reference() takes and returns one part's arrays. A program takes and returns all parts, laid end to end along the dimension named above; an argument that names none is the same for every part. Nothing has to cross between parts.
All inputs are finite; a program needn't handle non-finite values.
Results may differ from the reference program's by a relative error of at most 0.014.
Values may be sent and summed in bfloat16 or wider, within the bound.
No kernel may reach another device: no remote copies, remote signals or barrier semaphores. Data moves between devices by JAX's collectives and lax.ppermute only.
A program may use at most 128 MiB of HBM per device.

```python
import math
import jax
import jax.numpy as jnp
from jax import lax

HEADS = 128
HEAD_DIM = 64
STATE = 128
SPAN = 128
SEQUENCE_COUNT = 2
SEQUENCE_LENGTH = 3072
DI = 8192


def draw_gate_in(key, part):
    key = jax.random.fold_in(key, 5)
    head_pos = jnp.repeat(jnp.arange(HEADS, dtype=jnp.float32), HEAD_DIM) / HEADS
    column = jnp.exp(1.1 * head_pos + jax.random.uniform(jax.random.fold_in(key, 1), (DI,), minval=math.log(0.5), maxval=math.log(2.0)))
    row_scale = jnp.exp(jax.random.uniform(jax.random.fold_in(key, 2), (SEQUENCE_COUNT, SEQUENCE_LENGTH, 1), minval=0.0, maxval=math.log(10.0)))
    values = jnp.clip(jax.random.normal(jax.random.fold_in(key, 4), (SEQUENCE_COUNT, SEQUENCE_LENGTH, DI)), -4.0, 4.0)
    return (values * row_scale * column[None, None, :]).astype(jnp.bfloat16)


def choose_spike_events(key):
    return jax.random.permutation(key, SEQUENCE_LENGTH)[:3].astype(jnp.int32)


def draw_log_decay(key, part):
    key = jax.random.fold_in(key, 11)
    quick_share = 0.4
    strong_count = max(1, HEADS // 16)
    head_order = jax.random.permutation(jax.random.fold_in(key, 7), HEADS)
    strong_heads = head_order < strong_count
    quick_heads = jnp.logical_and(jax.random.uniform(jax.random.fold_in(key, 1), (HEADS,)) < quick_share, jnp.logical_not(strong_heads))
    quick_rate = 1.0 / jax.random.uniform(jax.random.fold_in(key, 2), (HEADS,), minval=14.0, maxval=25.0)
    slow_rate = jax.random.uniform(jax.random.fold_in(key, 3), (HEADS,), minval=0.1, maxval=0.9) / SEQUENCE_LENGTH
    shape = (SEQUENCE_COUNT, HEADS, SEQUENCE_LENGTH)
    slow_jitter = jax.random.uniform(jax.random.fold_in(key, 4), shape, minval=0.5, maxval=1.5)
    quick_jitter = jax.random.uniform(jax.random.fold_in(key, 9), shape, minval=0.0, maxval=2.0)
    strong_values = jax.random.uniform(jax.random.fold_in(key, 8), shape, minval=-1.0, maxval=-0.6)
    slow_values = -slow_rate[None, :, None] * slow_jitter
    quick_values = -quick_rate[None, :, None] * quick_jitter
    baseline_decay = jnp.where(strong_heads[None, :, None], strong_values, jnp.where(quick_heads[None, :, None], quick_values, slow_values))
    spike_random_keys = jax.random.split(jax.random.fold_in(key, 5), SEQUENCE_COUNT)
    spike_positions = jax.vmap(choose_spike_events)(spike_random_keys)
    forgotten_fraction = jax.random.uniform(jax.random.fold_in(key, 6), (SEQUENCE_COUNT, HEADS, 3), minval=0.2, maxval=0.35)
    at_spike_position = jnp.arange(SEQUENCE_LENGTH)[None, None, :] == spike_positions[:, :, None]
    spike_event = jnp.sum(jnp.where(at_spike_position[:, None, :, :], jnp.log(1.0 - forgotten_fraction)[:, :, :, None], 0.0), axis=2)
    return jnp.clip(baseline_decay + spike_event, -1.0, 0.0).astype(jnp.float32)


def shard_levels(stream_key, dims, cuts, low, top_value):
    def one(position, shards_of):
        draws = jax.random.uniform(jax.random.fold_in(jax.random.fold_in(stream_key, 6), position), (shards_of,), jnp.float32, low / len(cuts), top_value / len(cuts))
        return jnp.repeat(jnp.exp(draws), dims[position] // shards_of).reshape((-1,) + (1,) * (len(dims) - position - 1))

    loudness = one(*cuts[0])
    for cut in cuts[1:]:
        loudness = loudness * one(*cut)
    return loudness


def gaussian(key, dims, scale, reach, cuts=(), kind=jnp.bfloat16):
    loudness = shard_levels(key, dims, cuts, -0.22, 0.18) if cuts else 1.0
    values = jax.random.normal(key, dims, jnp.float32) * scale * loudness
    return jnp.minimum(jnp.maximum(values, -reach), reach).astype(kind)


def setup_inputs(seed: int = 0, part: int = 0) -> dict:
    arg_keys = jax.random.split(jax.random.key(seed), 8)
    part_splits = jax.random.split(jax.random.fold_in(arg_keys[7], part), 8)
    features = gaussian(part_splits[0], (SEQUENCE_COUNT, SEQUENCE_LENGTH, DI), 1.0, 6.0, ((1, 4), (2, 4)))
    gate_in = draw_gate_in(jax.random.fold_in(jax.random.fold_in(arg_keys[7], part), 71), part)
    state_proj = gaussian(part_splits[2], (2, SEQUENCE_COUNT, STATE, SEQUENCE_LENGTH), 0.5, 3.0, ((2, 4), (3, 4)))
    step_size = jnp.clip(jnp.exp(math.log(0.1) - 2.3025851 * jax.random.uniform(part_splits[3], (SEQUENCE_COUNT, HEADS, SEQUENCE_LENGTH), jnp.float32) ** shard_levels(part_splits[3], (SEQUENCE_COUNT, HEADS, SEQUENCE_LENGTH), ((1, 4), (2, 4)), -0.2, 0.2)), 0.01, 0.1)
    log_decay = draw_log_decay(jax.random.fold_in(jax.random.fold_in(arg_keys[7], part), 71), part)
    skip_gain = jnp.clip(0.5 + 1.5 * jax.random.uniform(arg_keys[5], (HEADS,), jnp.float32) ** shard_levels(arg_keys[5], (HEADS,), ((0, 4),), -0.2, 0.2), 0.5, 2.0)
    norm_gain = jnp.clip(1.0 + 0.1 * jax.random.normal(arg_keys[6], (DI,), jnp.float32), 0.5, 1.5)
    return {"features": features, "gate_in": gate_in, "state_proj": state_proj, "step_size": step_size, "log_decay": log_decay, "skip_gain": skip_gain, "norm_gain": norm_gain}


highest = lax.Precision.HIGHEST

def block_terms(carried, pieces):
    feat_block, b_block, c_block, step_block, decay_block = pieces
    cumulative = jnp.cumsum(decay_block, axis=1)
    row_index = lax.broadcasted_iota(jnp.int32, (SPAN, SPAN), 0)
    col_index = lax.broadcasted_iota(jnp.int32, (SPAN, SPAN), 1)
    causal = (row_index >= col_index)[None]
    spread = jnp.where(causal, cumulative[:, :, None] - cumulative[:, None, :], 0.0)
    decay_table = jnp.where(causal, jnp.exp(spread), 0.0)
    affinity = jnp.dot(c_block.T, b_block, preferred_element_type=jnp.float32)
    scores = (decay_table * affinity[None]).astype(jnp.bfloat16)
    weighted = (feat_block.astype(jnp.float32) * step_block[:, :, None]).astype(jnp.bfloat16)
    within = jnp.einsum('htu,hup->htp', scores.astype(jnp.float32), weighted.astype(jnp.float32), precision=highest)
    to_end = jnp.exp(cumulative[:, -1:] - cumulative)
    contrib = (weighted.astype(jnp.float32) * to_end[:, :, None]).astype(jnp.bfloat16)
    block_state = jnp.einsum('hup,nu->hpn', contrib.astype(jnp.float32), b_block.astype(jnp.float32), precision=highest)
    entering = carried.astype(jnp.bfloat16)
    carried_in = jnp.einsum('nt,hpn->htp', c_block.astype(jnp.float32), entering.astype(jnp.float32), precision=highest) * jnp.exp(cumulative)[:, :, None]
    carried = jnp.exp(cumulative[:, -1])[:, None, None] * carried + block_state
    return (carried, within + carried_in)

def ssd_sequence(features, state_proj, step_size, log_decay, skip_gain):
    spans = SEQUENCE_LENGTH // SPAN
    feat_blocks = features.reshape(spans, SPAN, HEADS, HEAD_DIM).transpose(0, 2, 1, 3)
    b_blocks = state_proj[0].reshape(STATE, spans, SPAN).transpose(1, 0, 2)
    c_blocks = state_proj[1].reshape(STATE, spans, SPAN).transpose(1, 0, 2)
    step_blocks = step_size.reshape(HEADS, spans, SPAN).transpose(1, 0, 2)
    decay_blocks = log_decay.reshape(HEADS, spans, SPAN).transpose(1, 0, 2)
    initial = jnp.zeros((HEADS, HEAD_DIM, STATE), jnp.float32)
    _, blocks = lax.scan(block_terms, initial, (feat_blocks, b_blocks, c_blocks, step_blocks, decay_blocks))
    mixed = blocks.transpose(0, 2, 1, 3).reshape(SEQUENCE_LENGTH, DI)
    skip_wide = jnp.repeat(skip_gain, HEAD_DIM)
    return mixed + features.astype(jnp.float32) * skip_wide[None, :]

def reference(features, gate_in, state_proj, step_size, log_decay, skip_gain, norm_gain):
    mixed = jnp.stack([ssd_sequence(features[seq_index], state_proj[:, seq_index], step_size[seq_index], log_decay[seq_index], skip_gain) for seq_index in range(SEQUENCE_COUNT)])
    gated = mixed * jax.nn.silu(gate_in.astype(jnp.float32))
    inv_rms = lax.rsqrt(lax.optimization_barrier(jnp.mean(gated * gated, axis=-1, keepdims=True)) + 1e-05)
    return (gated * inv_rms * norm_gain).astype(jnp.bfloat16)
```

```python
import functools

import jax
import jax.numpy as jnp
from jax import lax
from jax.experimental import pallas as pl
from jax.experimental.pallas import tpu as pltpu
from jax.sharding import PartitionSpec as P

SPAN = 128
CHUNK = 256
F32 = jnp.float32
BF16 = jnp.bfloat16
VMEM_LIMIT = 40 * 1024 * 1024


def mm(a, b):
    return jnp.dot(a, b, preferred_element_type=F32)


def mm_t(a, b):
    return lax.dot_general(a, b, (((0,), (0,)), ((), ())), preferred_element_type=F32)


def split2(v):
    high = v.astype(BF16)
    low = (v - high.astype(F32)).astype(BF16)
    return jnp.concatenate([high, low], axis=0)


def exact_dot(a, b):
    return jnp.dot(a, b, precision=lax.Precision.HIGHEST, preferred_element_type=F32)


def iotas(shape):
    return (
        lax.broadcasted_iota(jnp.int32, shape, 0),
        lax.broadcasted_iota(jnp.int32, shape, 1),
    )


def widen(column, spread32):
    return jnp.sum(spread32 * column, axis=0, keepdims=True)


def to_end_kernel(x_ref, step_ref, decay_ref, spread_ref, contrib_ref, total_ref):
    block = pl.program_id(1)
    heads, length = decay_ref.shape[1:]
    channels = x_ref.shape[2]
    decay = decay_ref[0]
    start = pl.multiple_of(block * SPAN, SPAN)
    here = decay_ref[0, :, pl.ds(start, SPAN)]
    step = step_ref[0, :, pl.ds(start, SPAN)]
    row, col = iotas((SPAN, SPAN))
    after = jnp.where(row > col, 1.0, 0.0).astype(F32)
    _, position = iotas((heads, length))
    later = jnp.sum(jnp.where(position >= start + SPAN, decay, 0.0), axis=1, keepdims=True)
    scale = split2(step * jnp.exp(exact_dot(here, after) + later))
    for lo in range(0, channels, CHUNK):
        sl = slice(lo, lo + CHUNK)
        wide = mm_t(scale, spread_ref[:, sl])
        contrib_ref[0, :, sl] = (x_ref[0, :, sl].astype(F32) * wide).astype(BF16)

    @pl.when(block == 0)
    def _():
        total = jnp.exp(jnp.sum(decay, axis=1, keepdims=True))
        total_ref[0] = widen(total, spread_ref[:heads, :].astype(F32))


def to_end(features, step_size, log_decay, spread):
    seqs, length, channels = features.shape
    heads = step_size.shape[1]
    blocks = length // SPAN
    whole = pl.BlockSpec((1, heads, length), lambda s, k: (s, 0, 0))
    tile = pl.BlockSpec((1, SPAN, channels), lambda s, k: (s, k, 0))
    return pl.pallas_call(
        to_end_kernel,
        grid=(seqs, blocks),
        in_specs=[tile, whole, whole, pl.BlockSpec(spread.shape, lambda s, k: (0, 0))],
        out_specs=[tile, pl.BlockSpec((1, 1, channels), lambda s, k: (s, 0, 0))],
        out_shape=[
            jax.ShapeDtypeStruct(features.shape, BF16),
            jax.ShapeDtypeStruct((seqs, 1, channels), F32),
        ],
        compiler_params=pltpu.CompilerParams(vmem_limit_bytes=VMEM_LIMIT),
        cost_estimate=pl.CostEstimate(
            flops=2 * seqs * length * channels * 64,
            bytes_accessed=4 * seqs * length * channels,
            transcendentals=0,
        ),
        name="contrib_to_end",
    )(features, step_size, log_decay, spread)


def state_kernel(b_ref, contrib_ref, state_ref):
    state_ref[...] = mm(b_ref[...], contrib_ref[0]).astype(BF16)


def end_state(b, contrib, seq):
    states, length = b.shape
    channels = contrib.shape[2]
    width = min(512, channels)
    return pl.pallas_call(
        state_kernel,
        grid=(channels // width,),
        in_specs=[
            pl.BlockSpec((states, length), lambda j: (0, 0)),
            pl.BlockSpec((1, length, width), lambda j: (seq, 0, j)),
        ],
        out_specs=pl.BlockSpec((states, width), lambda j: (0, j)),
        out_shape=jax.ShapeDtypeStruct((states, channels), BF16),
        compiler_params=pltpu.CompilerParams(vmem_limit_bytes=VMEM_LIMIT),
        cost_estimate=pl.CostEstimate(
            flops=2 * length * channels * states,
            bytes_accessed=2 * length * channels,
            transcendentals=0,
        ),
        name="own_end_state",
    )(b, contrib)


def local_kernel(
    x_ref, gate_ref, b_ref, c_ref, step_ref, decay_ref, spread_ref, skip_ref,
    own_ref, factor_ref, state,
):
    block = pl.program_id(0)
    heads, length = decay_ref.shape[1:]
    channels = x_ref.shape[2]

    @pl.when(block == 0)
    def _():
        state[...] = jnp.zeros_like(state)

    start = pl.multiple_of(block * SPAN, SPAN)
    decay = decay_ref[0]
    here = decay_ref[0, :, pl.ds(start, SPAN)]
    step = step_ref[0, :, pl.ds(start, SPAN)]
    row, col = iotas((SPAN, SPAN))
    _, lane = iotas((heads, SPAN))
    _, position = iotas((heads, length))
    until = jnp.where(row <= col, 1.0, 0.0).astype(F32)
    summed = exact_dot(here, until)
    middle = jnp.sum(jnp.where(lane < SPAN // 2, here, 0.0), axis=1, keepdims=True)
    last = jnp.sum(here, axis=1, keepdims=True)
    before = jnp.sum(jnp.where(position < start, decay, 0.0), axis=1, keepdims=True)
    rise = split2(jnp.exp(summed - middle))
    fall = split2(step * jnp.exp(middle - summed))
    spread32 = spread_ref[:heads, :].astype(F32)
    enter_row = widen(jnp.exp(middle), spread32)
    leave_row = widen(jnp.exp(last - middle), spread32)
    first_row = widen(jnp.exp(middle + before), spread32)

    b = b_ref[...]
    c_t = c_ref[...].T
    affinity = mm(c_t, b)
    masked = jnp.where(row >= col, affinity, 0.0).astype(BF16)
    left = jnp.concatenate([masked, c_t], axis=1)
    for lo in range(0, channels, CHUNK):
        sl = slice(lo, lo + CHUNK)
        spread = spread_ref[:, sl]
        x = x_ref[0, :, sl].astype(F32)
        weighted = (x * mm_t(fall, spread)).astype(BF16)
        entering = enter_row[:, sl] * state[:, sl]
        mixed = mm(left, jnp.concatenate([weighted, entering.astype(BF16)], axis=0))
        state[:, sl] = leave_row[:, sl] * (entering + mm(b, weighted))
        wide = mm_t(rise, spread)
        half = 0.5 * gate_ref[0, :, sl].astype(F32)
        gate = half * jnp.tanh(half) + half
        own_ref[:, sl] = ((wide * mixed + skip_ref[:, sl] * x) * gate).astype(BF16)
        factor_ref[:, sl] = (wide * first_row[:, sl] * gate).astype(BF16)


def local_terms(features, gate_in, b, c, step_size, log_decay, spread, skip_row, seq):
    _, length, channels = features.shape
    heads = step_size.shape[1]
    states = b.shape[0]
    whole = pl.BlockSpec((1, heads, length), lambda k: (seq, 0, 0))
    tile = pl.BlockSpec((1, SPAN, channels), lambda k: (seq, k, 0))
    span = pl.BlockSpec((states, SPAN), lambda k: (0, k))
    out = pl.BlockSpec((SPAN, channels), lambda k: (k, 0))
    return pl.pallas_call(
        local_kernel,
        grid=(length // SPAN,),
        in_specs=[
            tile, tile, span, span, whole, whole,
            pl.BlockSpec(spread.shape, lambda k: (0, 0)),
            pl.BlockSpec(skip_row.shape, lambda k: (0, 0)),
        ],
        out_specs=[out, out],
        out_shape=[jax.ShapeDtypeStruct((length, channels), BF16)] * 2,
        scratch_shapes=[pltpu.VMEM((states, channels), F32)],
        compiler_params=pltpu.CompilerParams(vmem_limit_bytes=VMEM_LIMIT),
        cost_estimate=pl.CostEstimate(
            flops=2 * length * channels * 512,
            bytes_accessed=8 * length * channels,
            transcendentals=length * channels,
        ),
        name="local_terms",
    )(features, gate_in, b, c, step_size, log_decay, spread, skip_row)


def joined_kernel(own_ref, factor_ref, c_ref, incoming_ref, gated_ref, square_ref):
    channels = own_ref.shape[1]
    c_t = c_ref[...].T
    squares = jnp.zeros((SPAN, 128), F32)
    for lo in range(0, channels, CHUNK):
        sl = slice(lo, lo + CHUNK)
        carried = mm(c_t, incoming_ref[:, sl])
        gated = own_ref[:, sl].astype(F32) + factor_ref[:, sl].astype(F32) * carried
        gated_ref[:, sl] = gated.astype(BF16)
        power = gated * gated
        for at in range(0, CHUNK, 128):
            squares = squares + power[:, at:at + 128]
    square_ref[0] = jnp.sum(squares.T, axis=0, keepdims=True)


def joined(own, factor, c, incoming):
    length, channels = own.shape
    states = c.shape[0]
    blocks = length // SPAN
    tile = pl.BlockSpec((SPAN, channels), lambda k: (k, 0))
    return pl.pallas_call(
        joined_kernel,
        grid=(blocks,),
        in_specs=[
            tile, tile,
            pl.BlockSpec((states, SPAN), lambda k: (0, k)),
            pl.BlockSpec((states, channels), lambda k: (0, 0)),
        ],
        out_specs=[tile, pl.BlockSpec((1, 1, SPAN), lambda k: (k, 0, 0))],
        out_shape=[
            jax.ShapeDtypeStruct((length, channels), BF16),
            jax.ShapeDtypeStruct((blocks, 1, SPAN), F32),
        ],
        compiler_params=pltpu.CompilerParams(vmem_limit_bytes=VMEM_LIMIT),
        cost_estimate=pl.CostEstimate(
            flops=2 * length * channels * states,
            bytes_accessed=6 * length * channels,
            transcendentals=0,
        ),
        name="joined",
    )(own, factor, c, incoming)


def norm_kernel(all_channels, *refs):
    gated_refs, square_ref, gain_ref, out_ref = refs[:-3], refs[-3], refs[-2], refs[-1]
    channels = out_ref.shape[2]
    seq = pl.program_id(0)
    total = jnp.sum(square_ref[:, 0, 0], axis=0)
    inverse = lax.rsqrt(total / all_channels + 1e-05)
    column = jnp.broadcast_to(inverse, (128, SPAN)).T
    for number, gated_ref in enumerate(gated_refs):

        @pl.when(seq == number)
        def _():
            for lo in range(0, channels, 128):
                sl = slice(lo, lo + 128)
                out_ref[0, :, sl] = (
                    gated_ref[:, sl].astype(F32) * column * gain_ref[:, sl]
                ).astype(BF16)


def normed(gated, squares, gain_row, all_channels):
    length, channels = gated[0].shape
    seqs = len(gated)
    shards = squares.shape[0]

    def tile_of(number):
        last = length // SPAN - 1
        return pl.BlockSpec(
            (SPAN, channels),
            lambda s, k: (jnp.where(s == number, k, jnp.where(s < number, 0, last)), 0),
        )

    return pl.pallas_call(
        functools.partial(norm_kernel, all_channels),
        grid=(seqs, length // SPAN),
        in_specs=[tile_of(number) for number in range(seqs)] + [
            pl.BlockSpec((shards, 1, 1, 1, SPAN), lambda s, k: (0, s, k, 0, 0)),
            pl.BlockSpec(gain_row.shape, lambda s, k: (0, 0)),
        ],
        out_specs=pl.BlockSpec((1, SPAN, channels), lambda s, k: (s, k, 0)),
        out_shape=jax.ShapeDtypeStruct((seqs, length, channels), BF16),
        compiler_params=pltpu.CompilerParams(vmem_limit_bytes=VMEM_LIMIT),
        cost_estimate=pl.CostEstimate(
            flops=2 * seqs * length * channels,
            bytes_accessed=4 * seqs * length * channels,
            transcendentals=0,
        ),
        name="normed",
    )(*gated, squares, gain_row)


def from_all(shard, axis):
    devices = lax.axis_size(axis)
    return [shard] + [
        lax.ppermute(shard, axis, [(i, (i + by) % devices) for i in range(devices)])
        for by in range(1, devices)
    ]


def body(features, gate_in, state_proj, step_size, log_decay, skip_gain, norm_gain):
    seqs, length, channels = features.shape
    heads = step_size.shape[1]
    head_dim = channels // heads
    spread = jnp.repeat(jnp.eye(heads, dtype=BF16), head_dim, axis=1)
    spread = jnp.concatenate([spread, spread], axis=0)
    skip_row = jnp.repeat(skip_gain, head_dim)[None, :]
    gain_row = norm_gain[None, :]

    b = [jnp.concatenate(p, axis=0) for p in zip(*[
        [piece[s] for s in range(seqs)] for piece in from_all(state_proj[0], "head")
    ])]
    c = [jnp.concatenate(p, axis=0) for p in zip(*[
        [piece[s] for s in range(seqs)] for piece in from_all(state_proj[1], "head")
    ])]
    contrib, total = to_end(features, step_size, log_decay, spread)
    own_state = [end_state(b[s], contrib, s) for s in range(seqs)]
    locals_ = [
        local_terms(features, gate_in, b[s], c[s], step_size, log_decay, spread, skip_row, s)
        for s in range(seqs)
    ]
    sent = list(own_state)
    incoming = [None] * seqs
    devices = lax.axis_size("ctx")
    for turn in range(devices - 1):
        for s in range(seqs):
            received = lax.ppermute(sent[s], "ctx", [(turn, turn + 1)])
            incoming[s] = received if incoming[s] is None else incoming[s] + received
            sent[s] = (
                own_state[s].astype(F32) + total[s] * incoming[s].astype(F32)
            ).astype(BF16)
    pairs = [joined(*locals_[s], c[s], incoming[s]) for s in range(seqs)]
    squares = [jnp.stack(from_all(pairs[s][1], "head")) for s in range(seqs)]
    squares = jnp.stack(squares, axis=1)
    return normed(
        [pairs[s][0] for s in range(seqs)], squares, gain_row,
        channels * lax.axis_size("head"),
    )


def solution(mesh):
    in_specs = (
        P("groups", "ctx", "head"),
        P("groups", "ctx", "head"),
        P(None, "groups", "head", "ctx"),
        P("groups", "head", "ctx"),
        P("groups", "head", "ctx"),
        P("head"),
        P("head"),
    )
    out_specs = P("groups", "ctx", "head")
    return jax.shard_map(body, mesh=mesh, in_specs=in_specs, out_specs=out_specs, check_vma=False)
```

```python
import functools

import jax
import jax.numpy as jnp
import numpy as np
from jax import lax
from jax.experimental import pallas as pl
from jax.experimental.pallas import tpu as pltpu
from jax.sharding import PartitionSpec as P

SPAN = 128
HALF = 256
F32 = jnp.float32
BF16 = jnp.bfloat16
VMEM_LIMIT = 20 * 1024 * 1024
PARAMS = pltpu.CompilerParams(vmem_limit_bytes=VMEM_LIMIT)
ENTER, LEAVE, FIRST, REST, TOTAL = range(5)


def mm(a, b):
    return jnp.dot(a, b, preferred_element_type=F32)


def exact_dot(a, b):
    return jnp.dot(a, b, precision=lax.Precision.HIGHEST, preferred_element_type=F32)


def iotas(shape):
    return (
        lax.broadcasted_iota(jnp.int32, shape, 0),
        lax.broadcasted_iota(jnp.int32, shape, 1),
    )


def two_parts(v):
    high = v.astype(BF16).astype(F32)
    return [high, v - high]


def upright(parts):
    return jnp.concatenate(parts, axis=0).T.astype(BF16)


def tables_kernel(step_ref, decay_ref, spread_ref, scale_ref, both_ref, rows_ref):
    seqs, heads, length = decay_ref.shape
    blocks = length // SPAN
    at, lane = iotas((length, SPAN))
    kind, block = lane // blocks, lane % blocks
    first, mid, end = block * SPAN, block * SPAN + SPAN // 2, block * SPAN + SPAN
    chosen = (
        ((kind == ENTER) & (at >= first) & (at < mid))
        | ((kind == LEAVE) & (at >= mid) & (at < end))
        | ((kind == FIRST) & (at < mid))
        | ((kind == REST) & (at >= first))
        | (kind == TOTAL)
    )
    chosen = jnp.where(chosen, 1.0, 0.0).astype(F32)
    row, col = iotas((SPAN, SPAN))
    until = jnp.where(row <= col, 1.0, 0.0).astype(F32)
    for s in range(seqs):
        exponent = exact_dot(decay_ref[s], chosen)
        per_block = upright(two_parts(jnp.exp(exponent)))
        rows_ref[s] = mm(per_block, spread_ref[...])[: rows_ref.shape[1]]
        for k in range(blocks):
            sl = slice(k * SPAN, (k + 1) * SPAN)
            step = step_ref[s, :, sl]
            summed = exact_dot(decay_ref[s, :, sl], until)
            middle = exponent[:, ENTER * blocks + k:ENTER * blocks + k + 1]
            rest = exponent[:, REST * blocks + k:REST * blocks + k + 1]
            scale = step * jnp.exp(rest - summed)
            rise = jnp.exp(summed - middle)
            fall = step * jnp.exp(middle - summed)
            scale_ref[s, sl, :] = upright(two_parts(scale))
            both_ref[s, sl, :] = upright(two_parts(rise) + two_parts(fall))


def tables(step_size, log_decay, spread):
    seqs, heads, length = log_decay.shape
    channels = spread.shape[1]
    return pl.pallas_call(
        tables_kernel,
        out_shape=[
            jax.ShapeDtypeStruct((seqs, length, 2 * heads), BF16),
            jax.ShapeDtypeStruct((seqs, length, 4 * heads), BF16),
            jax.ShapeDtypeStruct((seqs, 32, channels), F32),
        ],
        compiler_params=PARAMS,
        name="tables",
    )(step_size, log_decay, spread)


def contrib_kernel(x_ref, scale_ref, spread_ref, contrib_ref):
    length, width = x_ref.shape[1:]
    for k in range(length // SPAN):
        rows = slice(k * SPAN, (k + 1) * SPAN)
        scale = scale_ref[0, rows, :]
        for lo in range(0, width, HALF):
            sl = slice(lo, lo + HALF)
            wide = mm(scale, spread_ref[:, sl]).astype(BF16)
            contrib_ref[0, rows, sl] = x_ref[0, rows, sl] * wide


def contributions(features, scale, spread):
    seqs, length, channels = features.shape
    width = min(512, channels)
    tile = pl.BlockSpec((1, length, width), lambda s, j: (s, 0, j))
    return pl.pallas_call(
        contrib_kernel,
        grid=(seqs, channels // width),
        in_specs=[
            tile,
            pl.BlockSpec((1,) + scale.shape[1:], lambda s, j: (s, 0, 0)),
            pl.BlockSpec((spread.shape[0], width), lambda s, j: (0, j)),
        ],
        out_specs=tile,
        out_shape=jax.ShapeDtypeStruct(features.shape, BF16),
        compiler_params=PARAMS,
        cost_estimate=pl.CostEstimate(
            flops=2 * seqs * length * channels * 64,
            bytes_accessed=4 * seqs * length * channels,
            transcendentals=0,
        ),
        name="contributions",
    )(features, scale, spread)


def state_kernel(b_ref, contrib_ref, state_ref):
    state_ref[...] = mm(b_ref[...], contrib_ref[0]).astype(BF16)


def end_state(b, contrib, seq):
    states, length = b.shape
    channels = contrib.shape[2]
    width = min(512, channels)
    return pl.pallas_call(
        state_kernel,
        grid=(channels // width,),
        in_specs=[
            pl.BlockSpec((states, length), lambda j: (0, 0)),
            pl.BlockSpec((1, length, width), lambda j: (seq, 0, j)),
        ],
        out_specs=pl.BlockSpec((states, width), lambda j: (0, j)),
        out_shape=jax.ShapeDtypeStruct((states, channels), BF16),
        compiler_params=PARAMS,
        cost_estimate=pl.CostEstimate(
            flops=2 * length * channels * states,
            bytes_accessed=2 * length * channels,
            transcendentals=0,
        ),
        name="own_end_state",
    )(b, contrib)


def local_kernel(
    x_ref, gate_ref, b_ref, c_ref, both_ref, rise_ref, fall_ref, rows_ref, skip_ref,
    own_ref, factor_ref, left,
):
    length, width = x_ref.shape[1:]
    blocks = length // SPAN

    @pl.when(pl.program_id(0) == 0)
    def _():
        row, col = iotas((SPAN, SPAN))
        for k in range(blocks):
            sl = slice(k * SPAN, (k + 1) * SPAN)
            c_t = c_ref[:, sl].T
            affinity = mm(c_t, b_ref[:, sl])
            left[k, :, :SPAN] = jnp.where(row >= col, affinity, 0.0).astype(BF16)
            left[k, :, SPAN:] = c_t

    halves = [slice(lo, lo + HALF) for lo in range(0, width, HALF)]
    states = [None] * len(halves)
    for k in range(blocks):
        rows = slice(k * SPAN, (k + 1) * SPAN)
        both = both_ref[0, rows, :]

        def row_of(kind, sl):
            at = kind * blocks + k
            return rows_ref[0, at:at + 1, sl]

        for number, sl in enumerate(halves):
            x = x_ref[0, rows, sl]
            weighted = x * mm(both, fall_ref[:, sl]).astype(BF16)
            if k == 0:
                mixed = mm(left[k, :, :SPAN], weighted)
            else:
                entering = row_of(ENTER, sl) * states[number]
                mixed = mm(
                    left[k], jnp.concatenate([weighted, entering.astype(BF16)], axis=0)
                )
            if k < blocks - 1:
                added = mm(b_ref[:, rows], weighted)
                if k > 0:
                    added = added + entering
                states[number] = row_of(LEAVE, sl) * added
            half = 0.5 * gate_ref[0, rows, sl].astype(F32)
            gate = (half * jnp.tanh(half) + half).astype(BF16)
            lift = mm(both, rise_ref[:, sl]).astype(BF16) * gate
            skip = skip_ref[:, sl] * x * gate
            own_ref[rows, sl] = lift * mixed.astype(BF16) + skip
            factor_ref[rows, sl] = lift * row_of(FIRST, sl).astype(BF16)


def local_terms(features, gate_in, b, c, both, rise, fall, rows, skip_row, seq):
    _, length, channels = features.shape
    states = b.shape[0]
    width = min(512, channels)
    tile = pl.BlockSpec((1, length, width), lambda j: (seq, 0, j))
    whole = pl.BlockSpec((states, length), lambda j: (0, 0))
    column = lambda a: pl.BlockSpec((a.shape[0], width), lambda j: (0, j))
    out = pl.BlockSpec((length, width), lambda j: (0, j))
    return pl.pallas_call(
        local_kernel,
        grid=(channels // width,),
        in_specs=[
            tile, tile, whole, whole,
            pl.BlockSpec((1,) + both.shape[1:], lambda j: (seq, 0, 0)),
            column(rise), column(fall),
            pl.BlockSpec((1, rows.shape[1], width), lambda j: (seq, 0, j)),
            column(skip_row),
        ],
        out_specs=[out, out],
        out_shape=[jax.ShapeDtypeStruct((length, channels), BF16)] * 2,
        scratch_shapes=[pltpu.VMEM((length // SPAN, SPAN, SPAN + states), BF16)],
        compiler_params=PARAMS,
        cost_estimate=pl.CostEstimate(
            flops=2 * length * channels * 512,
            bytes_accessed=8 * length * channels,
            transcendentals=length * channels,
        ),
        name="local_terms",
    )(features, gate_in, b, c, both, rise, fall, rows, skip_row)


def joined_kernel(own_ref, factor_ref, c_ref, incoming_ref, gated_ref, square_ref):
    length, channels = own_ref.shape
    c_t = c_ref[...].T
    ones = jnp.ones((HALF, 128), BF16)
    squares = jnp.zeros((length, 128), F32)
    for lo in range(0, channels, HALF):
        sl = slice(lo, lo + HALF)
        carried = mm(c_t, incoming_ref[:, sl]).astype(BF16)
        gated = own_ref[:, sl] + factor_ref[:, sl] * carried
        gated_ref[:, sl] = gated
        squares = squares + mm(gated * gated, ones)
    for at in range(0, length, SPAN):
        square_ref[at // SPAN] = squares[at:at + SPAN].T[:1]


def joined(own, factor, c, incoming):
    length, channels = own.shape
    states = c.shape[0]
    blocks = length // SPAN
    tall = 2 * SPAN if blocks % 2 == 0 else SPAN
    tile = pl.BlockSpec((tall, channels), lambda k: (k, 0))
    return pl.pallas_call(
        joined_kernel,
        grid=(length // tall,),
        in_specs=[
            tile, tile,
            pl.BlockSpec((states, tall), lambda k: (0, k)),
            pl.BlockSpec((states, channels), lambda k: (0, 0)),
        ],
        out_specs=[tile, pl.BlockSpec((tall // SPAN, 1, SPAN), lambda k: (k, 0, 0))],
        out_shape=[
            jax.ShapeDtypeStruct((length, channels), BF16),
            jax.ShapeDtypeStruct((blocks, 1, SPAN), F32),
        ],
        compiler_params=PARAMS,
        cost_estimate=pl.CostEstimate(
            flops=2 * length * channels * states,
            bytes_accessed=6 * length * channels,
            transcendentals=0,
        ),
        name="joined",
    )(own, factor, c, incoming)


def norm_kernel(all_channels, gated_ref, square_ref, gain_ref, *refs):
    out_ref = refs[-1]
    tall, channels = gated_ref.shape
    for k in range(tall // SPAN):
        rows = slice(k * SPAN, (k + 1) * SPAN)
        total = jnp.sum(square_ref[:, k, 0], axis=0, keepdims=True)
        inverse = lax.rsqrt(total / all_channels + 1e-05)
        column = jnp.broadcast_to(inverse, (128, SPAN)).T
        for lo in range(0, channels, 128):
            sl = slice(lo, lo + 128)
            out_ref[0, rows, sl] = (
                gated_ref[rows, sl].astype(F32) * column * gain_ref[:, sl]
            ).astype(BF16)


def normed(gated, squares, gain_row, all_channels, seq, seqs, before):
    length, channels = gated.shape
    shards, blocks = squares.shape[:2]
    tall = 2 * SPAN if blocks % 2 == 0 else SPAN
    operands = [gated, squares, gain_row]
    in_specs = [
        pl.BlockSpec((tall, channels), lambda k: (k, 0)),
        pl.BlockSpec((shards, tall // SPAN, 1, SPAN), lambda k: (0, k, 0, 0)),
        pl.BlockSpec(gain_row.shape, lambda k: (0, 0)),
    ]
    if before is not None:
        operands.append(before)
        in_specs.append(pl.BlockSpec(memory_space=pl.ANY))
    return pl.pallas_call(
        functools.partial(norm_kernel, all_channels),
        grid=(length // tall,),
        in_specs=in_specs,
        out_specs=pl.BlockSpec((1, tall, channels), lambda k: (seq, k, 0)),
        out_shape=jax.ShapeDtypeStruct((seqs, length, channels), BF16),
        input_output_aliases={} if before is None else {3: 0},
        compiler_params=PARAMS,
        cost_estimate=pl.CostEstimate(
            flops=2 * length * channels,
            bytes_accessed=4 * length * channels,
            transcendentals=0,
        ),
        name="normed",
    )(*operands)


def from_all(shard, axis):
    devices = lax.axis_size(axis)
    return [shard] + [
        lax.ppermute(shard, axis, [(i, (i + by) % devices) for i in range(devices)])
        for by in range(1, devices)
    ]


def body(features, gate_in, state_proj, step_size, log_decay, skip_gain, norm_gain):
    seqs, length, channels = features.shape
    heads = step_size.shape[1]
    head_dim = channels // heads
    features = pltpu.with_memory_space_constraint(features, pltpu.HBM)
    gate_in = pltpu.with_memory_space_constraint(gate_in, pltpu.HBM)
    one = np.repeat(np.eye(heads, dtype=np.float32), head_dim, axis=1)
    pair = np.concatenate([one, one], axis=0)
    none = np.zeros_like(pair)
    spread = jnp.asarray(pair, BF16)
    rise = jnp.asarray(np.concatenate([pair, none], axis=0), BF16)
    fall = jnp.asarray(np.concatenate([none, pair], axis=0), BF16)
    skip_row = jnp.repeat(skip_gain.astype(BF16), head_dim)[None, :]
    gain_row = norm_gain[None, :]

    b = [jnp.concatenate(p, axis=0) for p in zip(*[
        [piece[s] for s in range(seqs)] for piece in from_all(state_proj[0], "head")
    ])]
    c = [jnp.concatenate(p, axis=0) for p in zip(*[
        [piece[s] for s in range(seqs)] for piece in from_all(state_proj[1], "head")
    ])]
    scale, both, rows = tables(step_size, log_decay, spread)
    total_at = TOTAL * (length // SPAN)
    total = [rows[s, total_at:total_at + 1] for s in range(seqs)]
    contrib = contributions(features, scale, spread)
    own_state = [end_state(b[s], contrib, s) for s in range(seqs)]
    locals_ = [
        local_terms(features, gate_in, b[s], c[s], both, rise, fall, rows, skip_row, s)
        for s in range(seqs)
    ]
    sent = list(own_state)
    incoming = [None] * seqs
    devices = lax.axis_size("ctx")
    for turn in range(devices - 1):
        for s in range(seqs):
            received = lax.ppermute(sent[s], "ctx", [(turn, turn + 1)])
            incoming[s] = received if incoming[s] is None else incoming[s] + received
            sent[s] = (
                own_state[s].astype(F32) + total[s] * incoming[s].astype(F32)
            ).astype(BF16)
    pairs = [joined(*locals_[s], c[s], incoming[s]) for s in range(seqs)]
    out = None
    for s in range(seqs):
        squares = jnp.stack(from_all(pairs[s][1], "head"))
        out = normed(
            pairs[s][0], squares, gain_row, channels * lax.axis_size("head"), s, seqs, out
        )
    return out


def solution(mesh):
    in_specs = (
        P("groups", "ctx", "head"),
        P("groups", "ctx", "head"),
        P(None, "groups", "head", "ctx"),
        P("groups", "head", "ctx"),
        P("groups", "head", "ctx"),
        P("head"),
        P("head"),
    )
    out_specs = P("groups", "ctx", "head")
    return jax.shard_map(body, mesh=mesh, in_specs=in_specs, out_specs=out_specs, check_vma=False)
```

```python
import functools

import jax
import jax.numpy as jnp
import numpy as np
from jax import lax
from jax.experimental import pallas as pl
from jax.experimental.pallas import tpu as pltpu
from jax.sharding import PartitionSpec as P

SPAN = 128
HALF = 256
F32 = jnp.float32
BF16 = jnp.bfloat16
VMEM_LIMIT = 20 * 1024 * 1024
PARAMS = pltpu.CompilerParams(vmem_limit_bytes=VMEM_LIMIT)
ENTER, LEAVE, FIRST, REST, TOTAL = range(5)
ROWS = 32
WHOLE = pl.BlockSpec(memory_space=pltpu.VMEM)


def in_vmem(array):
    return pltpu.with_memory_space_constraint(array, pltpu.VMEM)


def in_hbm(array):
    return pltpu.with_memory_space_constraint(array, pltpu.HBM)


def mm(a, b):
    return jnp.dot(a, b, preferred_element_type=F32)


def exact_dot(a, b):
    return jnp.dot(a, b, precision=lax.Precision.HIGHEST, preferred_element_type=F32)


def iotas(shape):
    return (
        lax.broadcasted_iota(jnp.int32, shape, 0),
        lax.broadcasted_iota(jnp.int32, shape, 1),
    )


def two_parts(v):
    high = v.astype(BF16).astype(F32)
    return [high, v - high]


def upright(parts):
    return jnp.concatenate(parts, axis=0).T.astype(BF16)


def fill_tables(step_ref, decay_ref, skip_ref, spread_ref, scale_ref, both_ref, rows_ref):
    seqs, heads, length = decay_ref.shape
    blocks = length // SPAN
    at, lane = iotas((length, SPAN))
    kind, block = lane // blocks, lane % blocks
    first, mid, end = block * SPAN, block * SPAN + SPAN // 2, block * SPAN + SPAN
    chosen = (
        ((kind == ENTER) & (at >= first) & (at < mid))
        | ((kind == LEAVE) & (at >= mid) & (at < end))
        | ((kind == FIRST) & (at < mid))
        | ((kind == REST) & (at >= first))
        | (kind == TOTAL)
    )
    chosen = jnp.where(chosen, 1.0, 0.0).astype(F32)
    row, col = iotas((SPAN, SPAN))
    until = jnp.where(row <= col, 1.0, 0.0).astype(F32)
    spread = spread_ref[:heads, :]
    skip = jnp.broadcast_to(skip_ref[...], (8, heads))
    skip_row = sum(mm(part.astype(BF16), spread) for part in two_parts(skip))
    for s in range(seqs):
        exponent = exact_dot(decay_ref[s], chosen)
        per_block = upright(two_parts(jnp.exp(exponent)))
        rows_ref[s] = mm(per_block, spread_ref[...])[:ROWS]
        rows_ref[s, ROWS - 1:ROWS] = skip_row[:1]
        for k in range(blocks):
            sl = slice(k * SPAN, (k + 1) * SPAN)
            step = step_ref[s, :, sl]
            summed = exact_dot(decay_ref[s, :, sl], until)
            middle = exponent[:, ENTER * blocks + k:ENTER * blocks + k + 1]
            rest = exponent[:, REST * blocks + k:REST * blocks + k + 1]
            scale = step * jnp.exp(rest - summed)
            rise = jnp.exp(summed - middle)
            fall = step * jnp.exp(middle - summed)
            scale_ref[s, sl, :] = upright(two_parts(scale))
            both_ref[s, sl, :] = upright(two_parts(rise) + two_parts(fall))


def front_kernel(
    x_ref, step_ref, decay_ref, skip_ref, spread_ref, contrib_ref, both_ref, rows_ref, scale_ref
):
    seq, part = pl.program_id(0), pl.program_id(1)
    length, width = x_ref.shape[1:]

    @pl.when((seq == 0) & (part == 0))
    def _():
        fill_tables(step_ref, decay_ref, skip_ref, spread_ref, scale_ref, both_ref, rows_ref)

    scale = scale_ref[seq]
    for lo in range(0, width, HALF):
        at = pl.ds(pl.multiple_of(part * width + lo, HALF), HALF)
        wide = mm(scale, spread_ref[:, at]).astype(BF16)
        contrib_ref[seq, :, at] = x_ref[0, :, lo:lo + HALF] * wide


def front(features, step_size, log_decay, skip, spread):
    seqs, length, channels = features.shape
    heads = step_size.shape[1]
    width = min(512, channels)
    return pl.pallas_call(
        front_kernel,
        grid=(seqs, channels // width),
        in_specs=[
            pl.BlockSpec((1, length, width), lambda s, j: (s, 0, j)),
            WHOLE, WHOLE, WHOLE, WHOLE,
        ],
        out_specs=[WHOLE, WHOLE, WHOLE],
        out_shape=[
            pltpu.VMEM(features.shape, BF16),
            pltpu.VMEM((seqs, length, 4 * heads), BF16),
            pltpu.VMEM((seqs, ROWS, channels), F32),
        ],
        scratch_shapes=[pltpu.VMEM((seqs, length, 2 * heads), BF16)],
        compiler_params=PARAMS,
        cost_estimate=pl.CostEstimate(
            flops=2 * seqs * length * channels * 64,
            bytes_accessed=4 * seqs * length * channels,
            transcendentals=0,
        ),
        name="front",
    )(features, step_size, log_decay, skip, spread)


def state_kernel(seq, b_ref, contrib_ref, state_ref):
    channels = state_ref.shape[1]
    for lo in range(0, channels, HALF):
        sl = slice(lo, lo + HALF)
        state_ref[:, sl] = mm(b_ref[...], contrib_ref[seq, :, sl]).astype(BF16)


def end_state(b, contrib, seq):
    states, length = b.shape
    channels = contrib.shape[2]
    return pl.pallas_call(
        functools.partial(state_kernel, seq),
        in_specs=[WHOLE, WHOLE],
        out_specs=WHOLE,
        out_shape=pltpu.VMEM((states, channels), BF16),
        compiler_params=PARAMS,
        cost_estimate=pl.CostEstimate(
            flops=2 * length * channels * states,
            bytes_accessed=2 * length * channels,
            transcendentals=0,
        ),
        name="own_end_state",
    )(b, in_vmem(contrib))


def local_kernel(
    x_ref, gate_ref, b_ref, c_ref, both_ref, rise_ref, fall_ref, rows_ref,
    own_ref, factor_ref, left,
):
    length, width = x_ref.shape[1:]
    blocks = length // SPAN

    @pl.when(pl.program_id(0) == 0)
    def _():
        row, col = iotas((SPAN, SPAN))
        for k in range(blocks):
            sl = slice(k * SPAN, (k + 1) * SPAN)
            c_t = c_ref[:, sl].T
            affinity = mm(c_t, b_ref[:, sl])
            left[k, :SPAN, :SPAN] = jnp.where(row >= col, affinity, 0.0).astype(BF16)
            left[k, :SPAN, SPAN:] = c_t
            left[k, SPAN:, :SPAN] = b_ref[:, sl]
            left[k, SPAN:, SPAN:] = jnp.zeros_like(c_t)

    base = pl.program_id(0) * width
    halves = [slice(lo, lo + HALF) for lo in range(0, width, HALF)]
    places = [pl.ds(pl.multiple_of(base + lo, HALF), HALF) for lo in range(0, width, HALF)]
    both = both_ref[0]
    weighted, lift, skipped = [], [], []
    for sl in halves:
        x = x_ref[0, :, sl]
        weighted.append(x * mm(both, fall_ref[:, sl]).astype(BF16))
        half = 0.5 * gate_ref[0, :, sl].astype(F32)
        gate = (half * jnp.tanh(half) + half).astype(BF16)
        lift.append(mm(both, rise_ref[:, sl]).astype(BF16) * gate)
        skipped.append(rows_ref[0, ROWS - 1:ROWS, sl].astype(BF16) * x * gate)
    states = [None] * len(halves)
    for k in range(blocks):
        rows = slice(k * SPAN, (k + 1) * SPAN)

        def row_of(kind, sl):
            at = kind * blocks + k
            return rows_ref[0, at:at + 1, sl]

        for number, sl in enumerate(halves):
            here = weighted[number][rows]
            if k == 0:
                product = mm(left[k, :, :SPAN], here)
            else:
                entering = row_of(ENTER, sl) * states[number]
                right = jnp.concatenate([here, entering.astype(BF16)], axis=0)
                product = mm(left[k] if k < blocks - 1 else left[k, :SPAN], right)
            if k < blocks - 1:
                added = product[SPAN:]
                if k > 0:
                    added = added + entering
                states[number] = row_of(LEAVE, sl) * added
            rise = lift[number][rows]
            own_ref[rows, places[number]] = (
                rise * product[:SPAN].astype(BF16) + skipped[number][rows]
            )
            factor_ref[rows, places[number]] = rise * row_of(FIRST, sl).astype(BF16)


def local_terms(features, gate_in, b, c, both, rise, fall, rows, seq):
    _, length, channels = features.shape
    states = b.shape[0]
    width = min(512, channels)
    tile = pl.BlockSpec((1, length, width), lambda j: (seq, 0, j))
    column = pl.BlockSpec((rise.shape[0], width), lambda j: (0, j))
    return pl.pallas_call(
        local_kernel,
        grid=(channels // width,),
        in_specs=[
            tile, tile, WHOLE, WHOLE,
            pl.BlockSpec((1,) + both.shape[1:], lambda j: (seq, 0, 0)),
            column, column,
            pl.BlockSpec((1, ROWS, width), lambda j: (seq, 0, j)),
        ],
        out_specs=[WHOLE, WHOLE],
        out_shape=[pltpu.VMEM((length, channels), BF16)] * 2,
        scratch_shapes=[pltpu.VMEM((length // SPAN, SPAN + states, SPAN + states), BF16)],
        compiler_params=PARAMS,
        cost_estimate=pl.CostEstimate(
            flops=2 * length * channels * 512,
            bytes_accessed=8 * length * channels,
            transcendentals=length * channels,
        ),
        name="local_terms",
    )(features, gate_in, b, c, both, rise, fall, rows)


def joined_kernel(own_ref, factor_ref, c_ref, incoming_ref, gated_ref, square_ref):
    length, channels = own_ref.shape
    c_t = c_ref[...].T
    ones = jnp.ones((HALF, 128), BF16)
    squares = jnp.zeros((length, 128), F32)
    for lo in range(0, channels, HALF):
        sl = slice(lo, lo + HALF)
        carried = mm(c_t, incoming_ref[:, sl]).astype(BF16)
        gated = own_ref[:, sl] + factor_ref[:, sl] * carried
        gated_ref[:, sl] = gated
        squares = squares + mm(gated * gated, ones)
    for at in range(0, length, SPAN):
        square_ref[at // SPAN] = squares[at:at + SPAN].T[:1]


def joined(own, factor, c, incoming):
    length, channels = own.shape
    states = c.shape[0]
    blocks = length // SPAN
    return pl.pallas_call(
        joined_kernel,
        in_specs=[WHOLE] * 4,
        out_specs=[WHOLE] * 2,
        out_shape=[
            pltpu.VMEM((length, channels), BF16),
            pltpu.VMEM((blocks, 1, SPAN), F32),
        ],
        compiler_params=PARAMS,
        cost_estimate=pl.CostEstimate(
            flops=2 * length * channels * states,
            bytes_accessed=6 * length * channels,
            transcendentals=0,
        ),
        name="joined",
    )(in_vmem(own), in_vmem(factor), c, incoming)


def norm_kernel(all_channels, gated_ref, square_ref, gain_ref, *refs):
    out_ref = refs[-1]
    tall, channels = out_ref.shape[1:]
    base = pl.program_id(0) * tall
    for k in range(tall // SPAN):
        rows = slice(k * SPAN, (k + 1) * SPAN)
        place = pl.ds(pl.multiple_of(base + k * SPAN, SPAN), SPAN)
        total = jnp.sum(square_ref[:, k, 0], axis=0, keepdims=True)
        inverse = lax.rsqrt(total / all_channels + 1e-05)
        column = jnp.broadcast_to(inverse, (128, SPAN)).T
        for lo in range(0, channels, 128):
            sl = slice(lo, lo + 128)
            out_ref[0, rows, sl] = (
                gated_ref[place, sl].astype(F32) * column * gain_ref[:, sl]
            ).astype(BF16)


def normed(gated, squares, gain_row, all_channels, seq, seqs, before):
    length, channels = gated.shape
    shards, blocks = squares.shape[:2]
    tall = 2 * SPAN if blocks % 2 == 0 else SPAN
    operands = [in_vmem(gated), squares, gain_row]
    in_specs = [
        WHOLE,
        pl.BlockSpec((shards, tall // SPAN, 1, SPAN), lambda k: (0, k, 0, 0)),
        pl.BlockSpec(gain_row.shape, lambda k: (0, 0)),
    ]
    if before is not None:
        operands.append(before)
        in_specs.append(pl.BlockSpec(memory_space=pl.ANY))
    return pl.pallas_call(
        functools.partial(norm_kernel, all_channels),
        grid=(length // tall,),
        in_specs=in_specs,
        out_specs=pl.BlockSpec((1, tall, channels), lambda k: (seq, k, 0)),
        out_shape=jax.ShapeDtypeStruct((seqs, length, channels), BF16),
        input_output_aliases={} if before is None else {3: 0},
        compiler_params=PARAMS,
        cost_estimate=pl.CostEstimate(
            flops=2 * length * channels,
            bytes_accessed=4 * length * channels,
            transcendentals=0,
        ),
        name="normed",
    )(*operands)


def from_all(shard, axis):
    devices = lax.axis_size(axis)
    return [shard] + [
        lax.ppermute(shard, axis, [(i, (i + by) % devices) for i in range(devices)])
        for by in range(1, devices)
    ]


def body(features, gate_in, state_proj, step_size, log_decay, skip_gain, norm_gain):
    seqs, length, channels = features.shape
    heads = step_size.shape[1]
    head_dim = channels // heads
    one = np.repeat(np.eye(heads, dtype=np.float32), head_dim, axis=1)
    pair = np.concatenate([one, one], axis=0)
    none = np.zeros_like(pair)
    spread = jnp.asarray(pair, BF16)
    rise = jnp.asarray(np.concatenate([pair, none], axis=0), BF16)
    fall = jnp.asarray(np.concatenate([none, pair], axis=0), BF16)
    gain_row = norm_gain[None, :]

    def whole(pieces):
        return [jnp.concatenate([piece[s] for piece in pieces], axis=0) for s in range(seqs)]

    b_own, c_own = lax.optimization_barrier((state_proj[0], state_proj[1]))
    b = whole(from_all(b_own, "head"))
    contrib, both, rows = front(
        in_hbm(features), in_hbm(step_size), in_hbm(log_decay), skip_gain[None, :], in_hbm(spread)
    )
    c_own, contrib = lax.optimization_barrier((c_own, contrib))
    c = whole(from_all(c_own, "head"))
    own_state = [end_state(b[s], contrib, s) for s in range(seqs)]
    total_at = TOTAL * (length // SPAN)
    total = [rows[s, total_at:total_at + 1] for s in range(seqs)]
    devices = lax.axis_size("ctx")
    incoming = [None] * seqs
    sent = list(own_state)
    terms = [None] * seqs

    def pass_on(turn, s):
        return lax.ppermute(sent[s], "ctx", [(turn, turn + 1)])

    def take(received, s):
        incoming[s] = received if incoming[s] is None else incoming[s] + received
        sent[s] = (
            own_state[s].astype(F32) + total[s] * incoming[s].astype(F32)
        ).astype(BF16)

    for turn in range(devices - 1):
        received = [pass_on(turn, s) for s in range(seqs)]
        for s in range(seqs):
            if turn == 1:
                b[s], _ = lax.optimization_barrier((b[s], tuple(sent)))
                terms[s] = local_terms(
                    in_hbm(features), in_hbm(gate_in), b[s], c[s], both, rise, fall, rows, s
                )
                received[s], terms[s] = lax.optimization_barrier((received[s], terms[s]))
            take(received[s], s)
    out = None
    parts = [joined(*terms[s], c[s], incoming[s]) for s in range(seqs)]
    for s in range(seqs):
        squares = jnp.stack(from_all(parts[s][1], "head"))
        out = normed(
            parts[s][0], squares, gain_row, channels * lax.axis_size("head"), s, seqs, out
        )
    return out


def solution(mesh):
    in_specs = (
        P("groups", "ctx", "head"),
        P("groups", "ctx", "head"),
        P(None, "groups", "head", "ctx"),
        P("groups", "head", "ctx"),
        P("groups", "head", "ctx"),
        P("head"),
        P("head"),
    )
    out_specs = P("groups", "ctx", "head")
    return jax.shard_map(body, mesh=mesh, in_specs=in_specs, out_specs=out_specs, check_vma=False)
```

```python
import functools

import jax
import jax.numpy as jnp
import numpy as np
from jax import lax
from jax.experimental import pallas as pl
from jax.experimental.pallas import tpu as pltpu
from jax.sharding import PartitionSpec as P

SPAN = 128
HALF = 256
F32 = jnp.float32
BF16 = jnp.bfloat16
VMEM_LIMIT = 20 * 1024 * 1024
PARAMS = pltpu.CompilerParams(vmem_limit_bytes=VMEM_LIMIT)
ENTER, LEAVE, FIRST, TOTAL = range(4)
ROWS = 32
WHOLE = pl.BlockSpec(memory_space=pltpu.VMEM)
ANYWHERE = pl.BlockSpec(memory_space=pl.ANY)


def in_vmem(array):
    return pltpu.with_memory_space_constraint(array, pltpu.VMEM)


def in_hbm(array):
    return pltpu.with_memory_space_constraint(array, pltpu.HBM)


def mm(a, b):
    return jnp.dot(a, b, preferred_element_type=F32)


def exact_dot(a, b):
    return jnp.dot(a, b, precision=lax.Precision.HIGHEST, preferred_element_type=F32)


def iotas(shape):
    return (
        lax.broadcasted_iota(jnp.int32, shape, 0),
        lax.broadcasted_iota(jnp.int32, shape, 1),
    )


def two_parts(v):
    high = v.astype(BF16).astype(F32)
    return [high, v - high]


def upright(parts):
    return jnp.concatenate(parts, axis=0).T.astype(BF16)


def fill_tables(step_ref, decay_ref, skip_ref, spread, both_ref, rows_ref):
    seqs, heads, length = decay_ref.shape
    blocks = length // SPAN
    at, lane = iotas((length, SPAN))
    kind, block = lane // blocks, lane % blocks
    first, mid, end = block * SPAN, block * SPAN + SPAN // 2, block * SPAN + SPAN
    chosen = (
        ((kind == ENTER) & (at >= first) & (at < mid))
        | ((kind == LEAVE) & (at >= mid) & (at < end))
        | ((kind == FIRST) & (at < mid))
        | (kind == TOTAL)
    )
    chosen = jnp.where(chosen, 1.0, 0.0).astype(F32)
    row, col = iotas((SPAN, SPAN))
    until = jnp.where(row <= col, 1.0, 0.0).astype(F32)
    skip = jnp.broadcast_to(skip_ref[...], (8, heads))
    skip_row = sum(mm(part.astype(BF16), spread[:heads]) for part in two_parts(skip))
    for s in range(seqs):
        exponent = exact_dot(decay_ref[s], chosen)
        per_block = upright(two_parts(jnp.exp(exponent)))
        rows_ref[s] = mm(per_block, spread)[:ROWS]
        rows_ref[s, ROWS - 1:ROWS] = skip_row[:1]
        for k in range(blocks):
            sl = slice(k * SPAN, (k + 1) * SPAN)
            summed = exact_dot(decay_ref[s, :, sl], until)
            middle = exponent[:, ENTER * blocks + k:ENTER * blocks + k + 1]
            rise = jnp.exp(summed - middle)
            fall = step_ref[s, :, sl] * jnp.exp(middle - summed)
            both_ref[s, sl, :] = upright(two_parts(rise) + two_parts(fall))


def front_kernel(
    x_hbm, step_ref, decay_ref, skip_ref, bands_hbm,
    x_ref, weighted_ref, both_ref, rows_ref, bands, sems,
):
    seqs, length, channels = x_ref.shape
    blocks = length // SPAN
    heads = decay_ref.shape[1]
    band_copy = pltpu.make_async_copy(bands_hbm, bands, sems.at[seqs * blocks])
    band_copy.start()
    copies = []
    for s in range(seqs):
        for k in range(blocks):
            place = (s, pl.ds(k * SPAN, SPAN))
            copies.append(
                pltpu.make_async_copy(x_hbm.at[place], x_ref.at[place], sems.at[s * blocks + k])
            )
            copies[-1].start()
    band_copy.wait()
    fill_tables(
        step_ref, decay_ref, skip_ref, bands[2 * heads:4 * heads], both_ref, rows_ref
    )
    for s in range(seqs):
        for k in range(blocks):
            rows = slice(k * SPAN, (k + 1) * SPAN)
            copies[s * blocks + k].wait()
            both = both_ref[s, rows]
            for lo in range(0, channels, HALF):
                sl = slice(lo, lo + HALF)
                wide = mm(both, bands[:4 * heads, sl]).astype(BF16)
                weighted_ref[s, rows, sl] = x_ref[s, rows, sl] * wide


def front(features, step_size, log_decay, skip, bands):
    seqs, length, channels = features.shape
    heads = step_size.shape[1]
    return pl.pallas_call(
        front_kernel,
        in_specs=[ANYWHERE, WHOLE, WHOLE, WHOLE, ANYWHERE],
        out_specs=[WHOLE] * 4,
        out_shape=[
            pltpu.VMEM(features.shape, BF16),
            pltpu.VMEM(features.shape, BF16),
            pltpu.VMEM((seqs, length, 4 * heads), BF16),
            pltpu.VMEM((seqs, ROWS, channels), F32),
        ],
        scratch_shapes=[
            pltpu.VMEM(bands.shape, BF16),
            pltpu.SemaphoreType.DMA((seqs * (length // SPAN) + 1,)),
        ],
        compiler_params=PARAMS,
        cost_estimate=pl.CostEstimate(
            flops=2 * seqs * length * channels * 64,
            bytes_accessed=4 * seqs * length * channels,
            transcendentals=0,
        ),
        name="front",
    )(features, step_size, log_decay, skip, bands)


def state_kernel(seq, b_ref, weighted_ref, rows_ref, entering_ref, state_ref):
    length = weighted_ref.shape[1]
    channels = state_ref.shape[1]
    blocks = length // SPAN
    for lo in range(0, channels, HALF):
        sl = slice(lo, lo + HALF)
        state = None
        for k in range(blocks):
            rows = slice(k * SPAN, (k + 1) * SPAN)
            added = mm(b_ref[:, rows], weighted_ref[seq, rows, sl])
            if k > 0:
                at = ENTER * blocks + k
                entering = rows_ref[seq, at:at + 1, sl] * state
                entering_ref[k - 1, :, sl] = entering.astype(BF16)
                added = added + entering
            at = LEAVE * blocks + k
            state = rows_ref[seq, at:at + 1, sl] * added
        state_ref[:, sl] = state.astype(BF16)


def end_state(b, weighted, rows, seq):
    states, length = b.shape
    channels = weighted.shape[2]
    return pl.pallas_call(
        functools.partial(state_kernel, seq),
        in_specs=[WHOLE] * 3,
        out_specs=[WHOLE] * 2,
        out_shape=[
            pltpu.VMEM((length // SPAN - 1, states, channels), BF16),
            pltpu.VMEM((states, channels), BF16),
        ],
        compiler_params=PARAMS,
        cost_estimate=pl.CostEstimate(
            flops=2 * length * channels * states,
            bytes_accessed=2 * length * channels,
            transcendentals=0,
        ),
        name="own_states",
    )(b, in_vmem(weighted), in_vmem(rows))


def local_kernel(
    seq, gate_hbm, x_ref, weighted_ref, entering_ref, b_ref, c_ref, both_ref, bands_ref, rows_ref,
    own_ref, factor_ref, gates, sems,
):
    length, channels = own_ref.shape
    blocks = length // SPAN
    heads4 = both_ref.shape[2]
    copies = []
    for k in range(blocks):
        rows = pl.ds(k * SPAN, SPAN)
        copies.append(
            pltpu.make_async_copy(gate_hbm.at[seq, rows], gates.at[rows], sems.at[k])
        )
        copies[-1].start()
    row, col = iotas((SPAN, SPAN))
    for k in range(blocks):
        rows = slice(k * SPAN, (k + 1) * SPAN)
        c_t = c_ref[:, rows].T
        affinity = mm(c_t, b_ref[:, rows])
        left = jnp.where(row >= col, affinity, 0.0).astype(BF16)
        if k > 0:
            left = jnp.concatenate([left, c_t], axis=1)
        both = both_ref[seq, rows]
        copies[k].wait()
        at = FIRST * blocks + k
        for lo in range(0, channels, HALF):
            sl = slice(lo, lo + HALF)
            right = weighted_ref[seq, rows, sl]
            if k > 0:
                right = jnp.concatenate([right, entering_ref[k - 1, :, sl]], axis=0)
            mixed = mm(left, right).astype(BF16)
            half = 0.5 * gates[rows, sl].astype(F32)
            gate = (half * jnp.tanh(half) + half).astype(BF16)
            rise = mm(both, bands_ref[heads4 // 2:heads4 // 2 + heads4, sl]).astype(BF16) * gate
            skip = rows_ref[seq, ROWS - 1:ROWS, sl].astype(BF16) * x_ref[seq, rows, sl]
            own_ref[rows, sl] = rise * mixed + skip * gate
            factor_ref[rows, sl] = rise * rows_ref[seq, at:at + 1, sl].astype(BF16)


def local_terms(gate_in, x, weighted, entering, b, c, both, bands, rows, seq):
    _, length, channels = gate_in.shape
    return pl.pallas_call(
        functools.partial(local_kernel, seq),
        in_specs=[ANYWHERE] + [WHOLE] * 8,
        out_specs=[WHOLE, WHOLE],
        out_shape=[pltpu.VMEM((length, channels), BF16)] * 2,
        scratch_shapes=[
            pltpu.VMEM((length, channels), BF16),
            pltpu.SemaphoreType.DMA((length // SPAN,)),
        ],
        compiler_params=PARAMS,
        cost_estimate=pl.CostEstimate(
            flops=2 * length * channels * 512,
            bytes_accessed=8 * length * channels,
            transcendentals=length * channels,
        ),
        name="local_terms",
    )(
        gate_in, in_vmem(x), in_vmem(weighted), in_vmem(entering), b, c, in_vmem(both), bands,
        in_vmem(rows),
    )


def joined_kernel(own_ref, factor_ref, c_ref, incoming_ref, gated_ref, square_ref):
    length, channels = own_ref.shape
    for at in range(0, length, SPAN):
        rows = slice(at, at + SPAN)
        c_t = c_ref[:, rows].T
        squares = jnp.zeros((SPAN, 128), F32)
        for lo in range(0, channels, HALF):
            sl = slice(lo, lo + HALF)
            carried = mm(c_t, incoming_ref[:, sl]).astype(BF16)
            gated = own_ref[rows, sl] + factor_ref[rows, sl] * carried
            gated_ref[rows, sl] = gated
            power = gated * gated
            pair = sum(power[:, left:left + 128] for left in range(0, HALF, 128))
            squares = squares + pair.astype(F32)
        square_ref[at // SPAN] = jnp.sum(squares.T, axis=0, keepdims=True)


def joined(own, factor, c, incoming):
    length, channels = own.shape
    states = c.shape[0]
    blocks = length // SPAN
    return pl.pallas_call(
        joined_kernel,
        in_specs=[WHOLE] * 4,
        out_specs=[WHOLE] * 2,
        out_shape=[
            pltpu.VMEM((length, channels), BF16),
            pltpu.VMEM((blocks, 1, SPAN), F32),
        ],
        compiler_params=PARAMS,
        cost_estimate=pl.CostEstimate(
            flops=2 * length * channels * states,
            bytes_accessed=6 * length * channels,
            transcendentals=0,
        ),
        name="joined",
    )(in_vmem(own), in_vmem(factor), c, incoming)


def norm_kernel(all_channels, seq, gated_ref, square_ref, gain_ref, *refs):
    out_hbm, staged, sems = refs[-3:]
    length, channels = gated_ref.shape
    copies = []
    for k in range(length // SPAN):
        rows = slice(k * SPAN, (k + 1) * SPAN)
        total = jnp.sum(square_ref[:, k, 0], axis=0, keepdims=True)
        inverse = lax.rsqrt(total / all_channels + 1e-05)
        column = jnp.broadcast_to(inverse, (128, SPAN)).T
        for lo in range(0, channels, 128):
            sl = slice(lo, lo + 128)
            staged[rows, sl] = (
                gated_ref[rows, sl].astype(F32) * column * gain_ref[:, sl]
            ).astype(BF16)
        place = pl.ds(k * SPAN, SPAN)
        copies.append(
            pltpu.make_async_copy(staged.at[place], out_hbm.at[seq, place], sems.at[k])
        )
        copies[-1].start()
    for copy in copies:
        copy.wait()


def normed(gated, squares, gain_row, all_channels, seq, seqs, before):
    length, channels = gated.shape
    operands = [in_vmem(gated), squares, gain_row]
    in_specs = [WHOLE] * 3
    if before is not None:
        operands.append(before)
        in_specs.append(ANYWHERE)
    return pl.pallas_call(
        functools.partial(norm_kernel, all_channels, seq),
        in_specs=in_specs,
        out_specs=ANYWHERE,
        out_shape=jax.ShapeDtypeStruct((seqs, length, channels), BF16),
        input_output_aliases={} if before is None else {3: 0},
        scratch_shapes=[
            pltpu.VMEM((length, channels), BF16),
            pltpu.SemaphoreType.DMA((length // SPAN,)),
        ],
        compiler_params=PARAMS,
        cost_estimate=pl.CostEstimate(
            flops=2 * length * channels,
            bytes_accessed=4 * length * channels,
            transcendentals=0,
        ),
        name="normed",
    )(*operands)


def from_all(shard, axis):
    devices = lax.axis_size(axis)
    return [shard] + [
        lax.ppermute(shard, axis, [(i, (i + by) % devices) for i in range(devices)])
        for by in range(1, devices)
    ]


def at_once(shard, axis):
    devices = lax.axis_size(axis)
    return lax.all_to_all(jnp.broadcast_to(shard, (devices,) + shard.shape), axis, 0, 0)


def body(features, gate_in, state_proj, step_size, log_decay, skip_gain, norm_gain):
    seqs, length, channels = features.shape
    heads = step_size.shape[1]
    pair = np.repeat(np.concatenate([np.eye(heads)] * 2), channels // heads, axis=1)
    bands = jnp.asarray(np.concatenate([0 * pair, pair, 0 * pair]), BF16)
    gain_row = norm_gain[None, :]

    def whole(pieces):
        return [jnp.concatenate([piece[s] for piece in pieces], axis=0) for s in range(seqs)]

    b_own, c_own = lax.optimization_barrier((state_proj[0], state_proj[1]))
    b = whole(from_all(b_own, "head"))
    x, weighted, both, rows = front(
        in_hbm(features), in_hbm(step_size), in_hbm(log_decay), in_hbm(skip_gain[None, :]),
        in_hbm(bands),
    )
    c_own, weighted = lax.optimization_barrier((c_own, weighted))
    c = from_all(c_own, "head")
    entering, sent = zip(*[end_state(b[s], weighted, rows, s) for s in range(seqs)])
    own_state, sent = list(sent), list(sent)
    total_at = TOTAL * (length // SPAN)
    total = [rows[s, total_at:total_at + 1] for s in range(seqs)]
    devices = lax.axis_size("ctx")
    incoming = [None] * seqs
    terms = [None] * seqs

    def pass_on(turn, s):
        return lax.ppermute(sent[s], "ctx", [(turn, turn + 1)])

    def take(received, s):
        incoming[s] = received if incoming[s] is None else incoming[s] + received
        sent[s] = (
            own_state[s].astype(F32) + total[s] * incoming[s].astype(F32)
        ).astype(BF16)
        if s > 0:
            sent[s], _ = lax.optimization_barrier((sent[s], sent[s - 1]))

    for turn in range(devices - 1):
        received = [pass_on(turn, s) for s in range(seqs)]
        if turn == 1:
            c, _ = lax.optimization_barrier((c, tuple(sent)))
            c = whole(c)
        for s in range(seqs):
            if turn == 1:
                if s > 0:
                    c[s], _ = lax.optimization_barrier((c[s], sent[s - 1]))
                terms[s] = local_terms(
                    in_hbm(gate_in), x, weighted, entering[s], b[s], c[s], both, bands, rows, s
                )
                received[s], terms[s] = lax.optimization_barrier((received[s], terms[s]))
            take(received[s], s)
    out = None
    parts = [joined(*terms[s], c[s], incoming[s]) for s in range(seqs)]
    for s in range(seqs):
        squares = at_once(parts[s][1], "head")
        out = normed(
            parts[s][0], squares, gain_row, channels * lax.axis_size("head"), s, seqs, out
        )
    return out


def solution(mesh):
    in_specs = (
        P("groups", "ctx", "head"),
        P("groups", "ctx", "head"),
        P(None, "groups", "head", "ctx"),
        P("groups", "head", "ctx"),
        P("groups", "head", "ctx"),
        P("head"),
        P("head"),
    )
    out_specs = P("groups", "ctx", "head")
    return jax.shard_map(body, mesh=mesh, in_specs=in_specs, out_specs=out_specs, check_vma=False)
```

```python
import functools

import jax
import jax.numpy as jnp
import numpy as np
from jax import lax
from jax.experimental import pallas as pl
from jax.experimental.pallas import tpu as pltpu
from jax.sharding import PartitionSpec as P

SPAN = 128
HALF = 256
F32 = jnp.float32
BF16 = jnp.bfloat16
VMEM_LIMIT = 12 * 1024 * 1024
PARAMS = pltpu.CompilerParams(vmem_limit_bytes=VMEM_LIMIT)
ENTER, LEAVE, FIRST, TOTAL = range(4)
ROWS = 32
WHOLE = pl.BlockSpec(memory_space=pltpu.VMEM)
ANYWHERE = pl.BlockSpec(memory_space=pl.ANY)


def in_vmem(array):
    return pltpu.with_memory_space_constraint(array, pltpu.VMEM)


def in_hbm(array):
    return pltpu.with_memory_space_constraint(array, pltpu.HBM)


def mm(a, b):
    return jnp.dot(a, b, preferred_element_type=F32)


def exact_dot(a, b):
    return jnp.dot(a, b, precision=lax.Precision.HIGHEST, preferred_element_type=F32)


def iotas(shape):
    return (
        lax.broadcasted_iota(jnp.int32, shape, 0),
        lax.broadcasted_iota(jnp.int32, shape, 1),
    )


def two_parts(v):
    high = v.astype(BF16).astype(F32)
    return [high, v - high]


def upright(parts):
    return jnp.concatenate(parts, axis=0).T.astype(BF16)


def fill_tables(step_ref, decay_ref, skip_ref, spread, both_ref, rows_ref):
    seqs, heads, length = decay_ref.shape
    blocks = length // SPAN
    at, lane = iotas((length, SPAN))
    kind, block = lane // blocks, lane % blocks
    first, mid, end = block * SPAN, block * SPAN + SPAN // 2, block * SPAN + SPAN
    chosen = (
        ((kind == ENTER) & (at >= first) & (at < mid))
        | ((kind == LEAVE) & (at >= mid) & (at < end))
        | ((kind == FIRST) & (at < mid))
        | (kind == TOTAL)
    )
    chosen = jnp.where(chosen, 1.0, 0.0).astype(F32)
    row, col = iotas((SPAN, SPAN))
    until = jnp.where(row <= col, 1.0, 0.0).astype(F32)
    skip = jnp.broadcast_to(skip_ref[...], (8, heads))
    skip_row = sum(mm(part.astype(BF16), spread[:heads]) for part in two_parts(skip))
    for s in range(seqs):
        exponent = exact_dot(decay_ref[s], chosen)
        per_block = upright(two_parts(jnp.exp(exponent)))
        rows_ref[s] = mm(per_block, spread)[:ROWS]
        rows_ref[s, ROWS - 1:ROWS] = skip_row[:1]
        for k in range(blocks):
            sl = slice(k * SPAN, (k + 1) * SPAN)
            summed = exact_dot(decay_ref[s, :, sl], until)
            middle = exponent[:, ENTER * blocks + k:ENTER * blocks + k + 1]
            rise = jnp.exp(summed - middle)
            fall = step_ref[s, :, sl] * jnp.exp(middle - summed)
            both_ref[s, sl, :] = upright(two_parts(rise) + two_parts(fall))


def front_kernel(
    x_ref, step_ref, decay_ref, skip_ref, bands_ref, weighted_ref, both_ref, rows_ref
):
    seqs, length, channels = x_ref.shape
    heads = decay_ref.shape[1]
    fill_tables(
        step_ref, decay_ref, skip_ref, bands_ref[2 * heads:4 * heads], both_ref, rows_ref
    )
    for s in range(seqs):
        for k in range(length // SPAN):
            rows = slice(k * SPAN, (k + 1) * SPAN)
            both = both_ref[s, rows]
            for lo in range(0, channels, HALF):
                sl = slice(lo, lo + HALF)
                wide = mm(both, bands_ref[:4 * heads, sl]).astype(BF16)
                weighted_ref[s, rows, sl] = x_ref[s, rows, sl] * wide


def front(features, step_size, log_decay, skip, bands):
    seqs, length, channels = features.shape
    heads = step_size.shape[1]
    return pl.pallas_call(
        front_kernel,
        in_specs=[WHOLE] * 5,
        out_specs=[WHOLE] * 3,
        out_shape=[
            pltpu.VMEM(features.shape, BF16),
            pltpu.VMEM((seqs, length, 4 * heads), BF16),
            pltpu.VMEM((seqs, ROWS, channels), F32),
        ],
        compiler_params=PARAMS,
        cost_estimate=pl.CostEstimate(
            flops=2 * seqs * length * channels * 64,
            bytes_accessed=4 * seqs * length * channels,
            transcendentals=0,
        ),
        name="front",
    )(in_vmem(features), step_size, log_decay, skip, bands)


def state_kernel(b_ref, weighted_ref, rows_ref, entering_ref, state_ref):
    seqs, length, channels = weighted_ref.shape
    blocks = length // SPAN
    for s in range(seqs):
        for lo in range(0, channels, HALF):
            sl = slice(lo, lo + HALF)
            state = None
            for k in range(blocks):
                rows = slice(k * SPAN, (k + 1) * SPAN)
                added = mm(b_ref[s, :, rows], weighted_ref[s, rows, sl])
                if k > 0:
                    at = ENTER * blocks + k
                    entering = rows_ref[s, at:at + 1, sl] * state
                    entering_ref[s, k - 1, :, sl] = entering.astype(BF16)
                    added = added + entering
                at = LEAVE * blocks + k
                state = rows_ref[s, at:at + 1, sl] * added
            state_ref[s, :, sl] = state.astype(BF16)


def own_states(b, weighted, rows):
    seqs, states, length = b.shape
    channels = weighted.shape[2]
    return pl.pallas_call(
        state_kernel,
        in_specs=[WHOLE] * 3,
        out_specs=[WHOLE] * 2,
        out_shape=[
            pltpu.VMEM((seqs, length // SPAN - 1, states, channels), BF16),
            pltpu.VMEM((seqs, states, channels), BF16),
        ],
        compiler_params=PARAMS,
        cost_estimate=pl.CostEstimate(
            flops=2 * seqs * length * channels * states,
            bytes_accessed=2 * seqs * length * channels,
            transcendentals=0,
        ),
        name="own_states",
    )(b, in_vmem(weighted), in_vmem(rows))


def local_kernel(
    gate_ref, x_ref, weighted_ref, entering_ref, b_ref, c_ref, both_ref, bands_ref, rows_ref,
    own_ref, factor_ref,
):
    seqs, length, channels = own_ref.shape
    blocks = length // SPAN
    heads4 = both_ref.shape[2]
    row, col = iotas((SPAN, SPAN))
    for s in range(seqs):
        for k in range(blocks):
            rows = slice(k * SPAN, (k + 1) * SPAN)
            c_t = c_ref[s, :, rows].T
            affinity = mm(c_t, b_ref[s, :, rows])
            left = jnp.where(row >= col, affinity, 0.0).astype(BF16)
            if k > 0:
                left = jnp.concatenate([left, c_t], axis=1)
            both = both_ref[s, rows]
            at = FIRST * blocks + k
            for lo in range(0, channels, HALF):
                sl = slice(lo, lo + HALF)
                right = weighted_ref[s, rows, sl]
                if k > 0:
                    right = jnp.concatenate([right, entering_ref[s, k - 1, :, sl]], axis=0)
                mixed = mm(left, right).astype(BF16)
                half = 0.5 * gate_ref[s, rows, sl].astype(F32)
                gate = (half * jnp.tanh(half) + half).astype(BF16)
                wide = mm(both, bands_ref[heads4 // 2:heads4 // 2 + heads4, sl])
                rise = wide.astype(BF16) * gate
                skip = rows_ref[s, ROWS - 1:ROWS, sl].astype(BF16) * x_ref[s, rows, sl]
                own_ref[s, rows, sl] = rise * mixed + skip * gate
                factor_ref[s, rows, sl] = rise * rows_ref[s, at:at + 1, sl].astype(BF16)


def local_terms(gate_in, x, weighted, entering, b, c, both, bands, rows):
    seqs, length, channels = gate_in.shape
    return pl.pallas_call(
        local_kernel,
        in_specs=[WHOLE] * 9,
        out_specs=[WHOLE, WHOLE],
        out_shape=[pltpu.VMEM(gate_in.shape, BF16)] * 2,
        compiler_params=PARAMS,
        cost_estimate=pl.CostEstimate(
            flops=2 * seqs * length * channels * 512,
            bytes_accessed=8 * seqs * length * channels,
            transcendentals=seqs * length * channels,
        ),
        name="local_terms",
    )(
        in_vmem(gate_in), in_vmem(x), in_vmem(weighted), in_vmem(entering), b, c, in_vmem(both),
        bands, in_vmem(rows),
    )


def joined_kernel(own_ref, factor_ref, c_ref, *refs):
    gated_ref, square_ref = refs[-2:]
    seqs, length, channels = own_ref.shape
    blocks = length // SPAN
    for s in range(seqs):
        for k in range(blocks):
            rows = slice(k * SPAN, (k + 1) * SPAN)
            c_t = c_ref[s, :, rows].T
            squares = jnp.zeros((SPAN, 128), F32)
            for lo in range(0, channels, HALF):
                sl = slice(lo, lo + HALF)
                carried = mm(c_t, refs[s][:, sl]).astype(BF16)
                gated = own_ref[s, rows, sl] + factor_ref[s, rows, sl] * carried
                gated_ref[s, rows, sl] = gated
                power = gated * gated
                pair = sum(power[:, left:left + 128] for left in range(0, HALF, 128))
                squares = squares + pair.astype(F32)
            square_ref[s * blocks + k] = jnp.sum(squares.T, axis=0, keepdims=True)


def joined(own, factor, c, incoming):
    seqs, length, channels = own.shape
    states = c.shape[1]
    return pl.pallas_call(
        joined_kernel,
        in_specs=[WHOLE] * (3 + seqs),
        out_specs=[WHOLE] * 2,
        out_shape=[
            pltpu.VMEM(own.shape, BF16),
            pltpu.VMEM((seqs * (length // SPAN), 1, SPAN), F32),
        ],
        input_output_aliases={0: 0},
        compiler_params=PARAMS,
        cost_estimate=pl.CostEstimate(
            flops=2 * seqs * length * channels * states,
            bytes_accessed=6 * seqs * length * channels,
            transcendentals=0,
        ),
        name="joined",
    )(in_vmem(own), in_vmem(factor), c, *incoming)


def norm_kernel(all_channels, gated_ref, square_ref, gain_ref, out_hbm, staged, sems):
    seqs, length, channels = gated_ref.shape
    blocks = length // SPAN
    copies = []
    for s in range(seqs):
        for k in range(blocks):
            at = s * blocks + k
            rows = slice(k * SPAN, (k + 1) * SPAN)
            total = jnp.sum(square_ref[:, at, 0], axis=0, keepdims=True)
            inverse = lax.rsqrt(total / all_channels + 1e-05)
            column = jnp.broadcast_to(inverse, (128, SPAN)).T
            for lo in range(0, channels, 128):
                sl = slice(lo, lo + 128)
                staged[s, rows, sl] = (
                    gated_ref[s, rows, sl].astype(F32) * column * gain_ref[:, sl]
                ).astype(BF16)
            place = (s, pl.ds(k * SPAN, SPAN))
            copies.append(
                pltpu.make_async_copy(staged.at[place], out_hbm.at[place], sems.at[at])
            )
            copies[-1].start()
    for copy in copies:
        copy.wait()


def normed(gated, squares, gain_row, all_channels):
    seqs, length, channels = gated.shape
    return pl.pallas_call(
        functools.partial(norm_kernel, all_channels),
        in_specs=[WHOLE] * 3,
        out_specs=ANYWHERE,
        out_shape=jax.ShapeDtypeStruct(gated.shape, BF16),
        scratch_shapes=[
            pltpu.VMEM(gated.shape, BF16),
            pltpu.SemaphoreType.DMA((seqs * (length // SPAN),)),
        ],
        compiler_params=PARAMS,
        cost_estimate=pl.CostEstimate(
            flops=2 * seqs * length * channels,
            bytes_accessed=4 * seqs * length * channels,
            transcendentals=0,
        ),
        name="normed",
    )(in_vmem(gated), squares, gain_row)


def from_all(shard, axis):
    devices = lax.axis_size(axis)
    return [shard] + [
        lax.ppermute(shard, axis, [(i, (i + by) % devices) for i in range(devices)])
        for by in range(1, devices)
    ]


def as_parts(row):
    high = row.astype(BF16)
    low = (row - high.astype(F32)).astype(BF16)
    return jnp.concatenate([high, low, jnp.zeros((14, row.shape[1]), BF16)], axis=0)


def body(features, gate_in, state_proj, step_size, log_decay, skip_gain, norm_gain):
    seqs, length, channels = features.shape
    heads = step_size.shape[1]
    pair = np.repeat(np.concatenate([np.eye(heads)] * 2), channels // heads, axis=1)
    bands = jnp.asarray(np.concatenate([0 * pair, pair, 0 * pair]), BF16)
    b_own, c_own = lax.optimization_barrier((state_proj[0], state_proj[1]))
    c = from_all(c_own, "head")
    b = jnp.concatenate(from_all(b_own, "head"), axis=1)
    states = b.shape[1]
    weighted, both, rows = front(
        features, in_hbm(step_size), in_hbm(log_decay), in_hbm(skip_gain[None, :]), in_hbm(bands)
    )
    entering, ends = own_states(b, weighted, rows)

    place = lax.axis_index("ctx")
    even = place % 2 == 0
    devices = lax.axis_size("ctx")
    swap = [(i, i ^ 1) for i in range(devices)]
    total_at = TOTAL * (length // SPAN)
    decay = [rows[s, total_at:total_at + 1] for s in range(seqs)]
    other = lax.ppermute(
        jnp.concatenate([
            jnp.where(even, ends[1], ends[0]),
            as_parts(jnp.where(even, decay[1], decay[0])),
        ]),
        "ctx", swap,
    )
    end_other = other[:states].astype(F32)
    decay_other = other[states:states + 1].astype(F32) + other[states + 1:states + 2].astype(F32)
    end_first = ends[0].astype(F32)
    past = jnp.where(
        even,
        end_other + decay_other * end_first,
        ends[1].astype(F32) + decay[1] * end_other,
    )
    decay_past = decay_other * jnp.where(even, decay[0], decay[1])
    entered = None
    for hop in range(0, devices - 2, 2):
        sent = past if entered is None else past + decay_past * entered.astype(F32)
        got = lax.ppermute(sent.astype(BF16), "ctx", [(hop, hop + 2), (hop + 1, hop + 3)])
        if entered is None:
            c, _ = lax.optimization_barrier((c, sent))
            c = jnp.concatenate(c, axis=1)
            terms = local_terms(
                gate_in, features, weighted, entering, b, c, both, in_hbm(bands), rows
            )
            got, terms = lax.optimization_barrier((got, terms))
        entered = got if entered is None else entered + got
    entered32 = entered.astype(F32)
    shared = lax.ppermute(
        jnp.where(even, end_first + decay[0] * entered32, entered32).astype(BF16), "ctx", swap
    )
    incoming = [
        jnp.where(even, entered, shared),
        jnp.where(even, shared, (end_other + decay_other * entered32).astype(BF16)),
    ]
    gated, squares = joined(*terms, c, incoming)
    squares = jnp.stack(from_all(squares, "head"))
    return normed(gated, squares, norm_gain[None, :], channels * lax.axis_size("head"))


def solution(mesh):
    in_specs = (
        P("groups", "ctx", "head"),
        P("groups", "ctx", "head"),
        P(None, "groups", "head", "ctx"),
        P("groups", "head", "ctx"),
        P("groups", "head", "ctx"),
        P("head"),
        P("head"),
    )
    out_specs = P("groups", "ctx", "head")
    return jax.shard_map(body, mesh=mesh, in_specs=in_specs, out_specs=out_specs, check_vma=False)
```

```python
import functools

import jax
import jax.numpy as jnp
import numpy as np
from jax import lax
from jax.experimental import pallas as pl
from jax.experimental.pallas import tpu as pltpu
from jax.sharding import PartitionSpec as P

SPAN = 128
HALF = 256
F32 = jnp.float32
BF16 = jnp.bfloat16
VMEM_LIMIT = 12 * 1024 * 1024
PARAMS = pltpu.CompilerParams(vmem_limit_bytes=VMEM_LIMIT)
ENTER, LEAVE, FIRST, TOTAL = range(4)
ROWS = 32
WHOLE = pl.BlockSpec(memory_space=pltpu.VMEM)
ANYWHERE = pl.BlockSpec(memory_space=pl.ANY)


def in_vmem(array):
    return pltpu.with_memory_space_constraint(array, pltpu.VMEM)


def in_hbm(array):
    return pltpu.with_memory_space_constraint(array, pltpu.HBM)


def mm(a, b):
    return jnp.dot(a, b, preferred_element_type=F32)


def mm_nt(a, b):
    return lax.dot_general(a, b, (((1,), (1,)), ((), ())), preferred_element_type=F32)


def iotas(shape):
    return (
        lax.broadcasted_iota(jnp.int32, shape, 0),
        lax.broadcasted_iota(jnp.int32, shape, 1),
    )


def three_parts(v):
    high = v.astype(BF16)
    rest = v - high.astype(F32)
    mid = rest.astype(BF16)
    return [high, mid, (rest - mid.astype(F32)).astype(BF16)]


def fill_tables(step_ref, decay_ref, skip_ref, sums_ref, rise_band, both_ref, rows_ref):
    seqs, heads, length = decay_ref.shape
    blocks = length // SPAN
    _, lane = iotas((SPAN, 4 * heads))
    rising = lane < 2 * heads
    is_high = (lane < heads) | ((lane >= 2 * heads) & (lane < 3 * heads))
    until = sums_ref[:SPAN]
    same = sums_ref[SPAN:]

    def parts_of(v):
        high = v.astype(BF16).astype(F32)
        return jnp.where(is_high[:v.shape[0]], high, v - high).astype(BF16)

    skip = jnp.concatenate([skip_ref[...]] * 4, axis=1)
    for s in range(seqs):
        decays = three_parts(jnp.concatenate([decay_ref[s]] * 4, axis=0))
        steps = three_parts(jnp.concatenate([step_ref[s]] * 4, axis=0))
        enter, leave, first = [], [], []
        before = jnp.zeros((1, 4 * heads), F32)
        for k in range(blocks):
            sl = slice(k * SPAN, (k + 1) * SPAN)
            summed = mm_nt(until, jnp.concatenate([p[:, sl] for p in decays], axis=1))
            step = mm_nt(same, jnp.concatenate([p[:, sl] for p in steps], axis=1))
            middle = summed[SPAN // 2 - 1:SPAN // 2]
            last = summed[SPAN - 1:]
            above = summed - middle
            factor = jnp.exp(jnp.where(rising, above, -above))
            both_ref[s, sl, :] = parts_of(jnp.where(rising, factor, step * factor))
            enter.append(jnp.exp(middle))
            leave.append(jnp.exp(last - middle))
            first.append(jnp.exp(middle + before))
            before = before + last
        table = enter + leave + first + [jnp.exp(before)]
        table = table + [jnp.zeros_like(before)] * (ROWS - 1 - len(table)) + [skip]
        rows_ref[s] = mm(parts_of(jnp.concatenate(table, axis=0)), rise_band)


def front_kernel(
    x_hbm, step_hbm, decay_hbm, skip_ref, sums_ref, bands_hbm,
    x_ref, weighted_ref, both_ref, rows_ref, step, decay, bands, sems,
):
    seqs, length, channels = x_ref.shape
    heads = decay.shape[1]
    blocks = length // SPAN
    small = [
        pltpu.make_async_copy(source, target, sems.at[seqs * blocks + i])
        for i, (source, target) in enumerate(
            [(decay_hbm, decay), (step_hbm, step), (bands_hbm, bands)]
        )
    ]
    for copy in small:
        copy.start()
    copies = []
    for s in range(seqs):
        for k in range(blocks):
            place = (s, pl.ds(k * SPAN, SPAN))
            copies.append(
                pltpu.make_async_copy(x_hbm.at[place], x_ref.at[place], sems.at[s * blocks + k])
            )
            copies[-1].start(priority=k % 2)
    for copy in small:
        copy.wait()
    fill_tables(
        step, decay, skip_ref, sums_ref, bands[2 * heads:], both_ref, rows_ref
    )
    for s in range(seqs):
        for k in range(blocks):
            rows = slice(k * SPAN, (k + 1) * SPAN)
            copies[s * blocks + k].wait()
            both = both_ref[s, rows]
            for lo in range(0, channels, HALF):
                sl = slice(lo, lo + HALF)
                wide = mm(both, bands[:4 * heads, sl]).astype(BF16)
                weighted_ref[s, rows, sl] = x_ref[s, rows, sl] * wide


def front(features, step_size, log_decay, skip, sums, bands):
    seqs, length, channels = features.shape
    heads = step_size.shape[1]
    return pl.pallas_call(
        front_kernel,
        in_specs=[ANYWHERE, ANYWHERE, ANYWHERE, WHOLE, WHOLE, ANYWHERE],
        out_specs=[WHOLE] * 4,
        out_shape=[
            pltpu.VMEM(features.shape, BF16),
            pltpu.VMEM(features.shape, BF16),
            pltpu.VMEM((seqs, length, 4 * heads), BF16),
            pltpu.VMEM((seqs, ROWS, channels), F32),
        ],
        scratch_shapes=[
            pltpu.VMEM(step_size.shape, F32),
            pltpu.VMEM(log_decay.shape, F32),
            pltpu.VMEM(bands.shape, BF16),
            pltpu.SemaphoreType.DMA((seqs * (length // SPAN) + 3,)),
        ],
        compiler_params=PARAMS,
        cost_estimate=pl.CostEstimate(
            flops=2 * seqs * length * channels * 64,
            bytes_accessed=4 * seqs * length * channels,
            transcendentals=0,
        ),
        name="front",
    )(
        in_hbm(features), in_hbm(step_size), in_hbm(log_decay), in_hbm(skip), in_hbm(sums),
        in_hbm(bands),
    )


def state_kernel(b_ref, weighted_ref, rows_ref, entering_ref, state_ref):
    seqs, length, channels = weighted_ref.shape
    blocks = length // SPAN
    for s in range(seqs):
        for lo in range(0, channels, HALF):
            sl = slice(lo, lo + HALF)
            state = None
            for k in range(blocks):
                rows = slice(k * SPAN, (k + 1) * SPAN)
                added = mm(b_ref[s, :, rows], weighted_ref[s, rows, sl])
                if k > 0:
                    at = ENTER * blocks + k
                    entering = rows_ref[s, at:at + 1, sl] * state
                    entering_ref[s, k - 1, :, sl] = entering.astype(BF16)
                    added = added + entering
                at = LEAVE * blocks + k
                state = rows_ref[s, at:at + 1, sl] * added
            state_ref[s, :, sl] = state.astype(BF16)


def own_states(b, weighted, rows):
    seqs, states, length = b.shape
    channels = weighted.shape[2]
    return pl.pallas_call(
        state_kernel,
        in_specs=[WHOLE] * 3,
        out_specs=[WHOLE] * 2,
        out_shape=[
            pltpu.VMEM((seqs, length // SPAN - 1, states, channels), BF16),
            pltpu.VMEM((seqs, states, channels), BF16),
        ],
        compiler_params=PARAMS,
        cost_estimate=pl.CostEstimate(
            flops=2 * seqs * length * channels * states,
            bytes_accessed=2 * seqs * length * channels,
            transcendentals=0,
        ),
        name="own_states",
    )(b, in_vmem(weighted), in_vmem(rows))


def gate_kernel(gate_ref, x_ref, both_ref, band_ref, rows_ref, lift_ref, skipped_ref):
    seqs, length, channels = lift_ref.shape
    for s in range(seqs):
        for k in range(length // SPAN):
            rows = slice(k * SPAN, (k + 1) * SPAN)
            both = both_ref[s, rows]
            for lo in range(0, channels, HALF):
                sl = slice(lo, lo + HALF)
                half = 0.5 * gate_ref[s, rows, sl].astype(F32)
                gate = (half * jnp.tanh(half) + half).astype(BF16)
                lift_ref[s, rows, sl] = mm(both, band_ref[:, sl]).astype(BF16) * gate
                skip = rows_ref[s, ROWS - 1:ROWS, sl].astype(BF16) * x_ref[s, rows, sl]
                skipped_ref[s, rows, sl] = skip * gate


def gates(gate_in, x, both, band, rows):
    seqs, length, channels = gate_in.shape
    return pl.pallas_call(
        gate_kernel,
        in_specs=[WHOLE] * 5,
        out_specs=[WHOLE, WHOLE],
        out_shape=[pltpu.VMEM(gate_in.shape, BF16)] * 2,
        compiler_params=PARAMS,
        cost_estimate=pl.CostEstimate(
            flops=2 * seqs * length * channels * 256,
            bytes_accessed=8 * seqs * length * channels,
            transcendentals=seqs * length * channels,
        ),
        name="gates",
    )(in_vmem(gate_in), in_vmem(x), in_vmem(both), band, in_vmem(rows))


def final_kernel(
    weighted_ref, entering_ref, lift_ref, skipped_ref, b_ref, c_ref, rows_ref, *refs
):
    gated_ref, square_ref = refs[-2:]
    seqs, length, channels = lift_ref.shape
    blocks = length // SPAN
    row, col = iotas((SPAN, SPAN))
    for s in range(seqs):
        for k in range(blocks):
            rows = slice(k * SPAN, (k + 1) * SPAN)
            c_t = c_ref[s, :, rows].T
            affinity = mm(c_t, b_ref[s, :, rows])
            masked = jnp.where(row >= col, affinity, 0.0).astype(BF16)
            left = jnp.concatenate([masked, c_t], axis=1)
            squares = jnp.zeros((SPAN, 128), F32)
            at = FIRST * blocks + k
            for lo in range(0, channels, HALF):
                sl = slice(lo, lo + HALF)
                entering = rows_ref[s, at:at + 1, sl].astype(BF16) * refs[s][:, sl]
                if k > 0:
                    entering = entering + entering_ref[s, k - 1, :, sl]
                right = jnp.concatenate([weighted_ref[s, rows, sl], entering], axis=0)
                mixed = mm(left, right).astype(BF16)
                gated = lift_ref[s, rows, sl] * mixed + skipped_ref[s, rows, sl]
                gated_ref[s, rows, sl] = gated
                power = gated * gated
                pair = sum(power[:, left_:left_ + 128] for left_ in range(0, HALF, 128))
                squares = squares + pair.astype(F32)
            square_ref[s * blocks + k] = jnp.sum(squares.T, axis=0, keepdims=True)


def final(weighted, entering, lift, skipped, b, c, rows, incoming):
    seqs, length, channels = lift.shape
    states = c.shape[1]
    return pl.pallas_call(
        final_kernel,
        in_specs=[WHOLE] * (7 + seqs),
        out_specs=[WHOLE] * 2,
        out_shape=[
            pltpu.VMEM(lift.shape, BF16),
            pltpu.VMEM((seqs * (length // SPAN), 1, SPAN), F32),
        ],
        compiler_params=PARAMS,
        cost_estimate=pl.CostEstimate(
            flops=4 * seqs * length * channels * states,
            bytes_accessed=6 * seqs * length * channels,
            transcendentals=0,
        ),
        name="final",
    )(
        in_vmem(weighted), in_vmem(entering), in_vmem(lift), in_vmem(skipped), b, c,
        in_vmem(rows), *incoming,
    )


def norm_kernel(all_channels, gated_ref, square_ref, gain_ref, out_hbm, staged, sems):
    seqs, length, channels = gated_ref.shape
    blocks = length // SPAN
    copies = []
    for s in range(seqs):
        for k in range(blocks):
            at = s * blocks + k
            rows = slice(k * SPAN, (k + 1) * SPAN)
            total = jnp.sum(square_ref[:, at, 0], axis=0, keepdims=True)
            inverse = lax.rsqrt(total / all_channels + 1e-05)
            column = jnp.broadcast_to(inverse, (128, SPAN)).T
            for lo in range(0, channels, 128):
                sl = slice(lo, lo + 128)
                staged[s, rows, sl] = (
                    gated_ref[s, rows, sl].astype(F32) * column * gain_ref[:, sl]
                ).astype(BF16)
            place = (s, pl.ds(k * SPAN, SPAN))
            copies.append(
                pltpu.make_async_copy(staged.at[place], out_hbm.at[place], sems.at[at])
            )
            copies[-1].start(priority=k % 2)
    for copy in copies:
        copy.wait()


def normed(gated, squares, gain_row, all_channels):
    seqs, length, channels = gated.shape
    return pl.pallas_call(
        functools.partial(norm_kernel, all_channels),
        in_specs=[WHOLE] * 3,
        out_specs=ANYWHERE,
        out_shape=jax.ShapeDtypeStruct(gated.shape, BF16),
        scratch_shapes=[
            pltpu.VMEM(gated.shape, BF16),
            pltpu.SemaphoreType.DMA((seqs * (length // SPAN),)),
        ],
        compiler_params=PARAMS,
        cost_estimate=pl.CostEstimate(
            flops=2 * seqs * length * channels,
            bytes_accessed=4 * seqs * length * channels,
            transcendentals=0,
        ),
        name="normed",
    )(in_vmem(gated), squares, gain_row)


def from_all(shard, axis):
    devices = lax.axis_size(axis)
    return [shard] + [
        lax.ppermute(shard, axis, [(i, (i + by) % devices) for i in range(devices)])
        for by in range(1, devices)
    ]


def as_parts(row):
    high = row.astype(BF16)
    low = (row - high.astype(F32)).astype(BF16)
    return jnp.concatenate([high, low, jnp.zeros((14, row.shape[1]), BF16)], axis=0)


def body(features, gate_in, state_proj, step_size, log_decay, skip_gain, norm_gain):
    seqs, length, channels = features.shape
    heads = step_size.shape[1]
    pair = np.repeat(np.concatenate([np.eye(heads)] * 2), channels // heads, axis=1)
    bands = jnp.asarray(np.concatenate([0 * pair, pair, 0 * pair]), BF16)
    rise_band = jnp.asarray(np.concatenate([pair, 0 * pair]), BF16)
    until = np.tril(np.ones((SPAN, SPAN)))
    sums = jnp.asarray(np.concatenate([np.tile(until, 3), np.tile(np.eye(SPAN), 3)]), BF16)
    b_own, c_own = lax.optimization_barrier((state_proj[0], state_proj[1]))
    b = jnp.concatenate(from_all(b_own, "head"), axis=1)
    states = b.shape[1]
    x, weighted, both, rows = front(
        features, step_size, log_decay, skip_gain[None, :], sums, bands
    )
    entering, ends = own_states(b, weighted, rows)

    place = lax.axis_index("ctx")
    even = place % 2 == 0
    devices = lax.axis_size("ctx")
    swap = [(i, i ^ 1) for i in range(devices)]
    total_at = TOTAL * (length // SPAN)
    decay = [rows[s, total_at:total_at + 1] for s in range(seqs)]
    other = lax.ppermute(
        jnp.concatenate([
            jnp.where(even, ends[1], ends[0]),
            as_parts(jnp.where(even, decay[1], decay[0])),
        ]),
        "ctx", swap,
    )
    end_other = other[:states].astype(F32)
    decay_other = other[states:states + 1].astype(F32) + other[states + 1:states + 2].astype(F32)
    end_first = ends[0].astype(F32)
    past = jnp.where(
        even,
        end_other + decay_other * end_first,
        ends[1].astype(F32) + decay[1] * end_other,
    )
    decay_past = decay_other * jnp.where(even, decay[0], decay[1])
    entered = None
    for hop in range(0, devices - 2, 2):
        sent = past if entered is None else past + decay_past * entered.astype(F32)
        got = lax.ppermute(sent.astype(BF16), "ctx", [(hop, hop + 2), (hop + 1, hop + 3)])
        if entered is None:
            c_own, x, _ = lax.optimization_barrier((c_own, x, sent))
            c = from_all(c_own, "head")
            terms = gates(gate_in, x, both, rise_band, rows)
            got, terms, c = lax.optimization_barrier((got, terms, c))
            c = jnp.concatenate(c, axis=1)
        entered = got if entered is None else entered + got
    entered32 = entered.astype(F32)
    shared = lax.ppermute(
        jnp.where(even, end_first + decay[0] * entered32, entered32).astype(BF16), "ctx", swap
    )
    incoming = [
        jnp.where(even, entered, shared),
        jnp.where(even, shared, (end_other + decay_other * entered32).astype(BF16)),
    ]
    gated, squares = final(weighted, entering, *terms, b, c, rows, incoming)
    squares = lax.all_gather(squares, "head")
    return normed(gated, squares, norm_gain[None, :], channels * lax.axis_size("head"))


def solution(mesh):
    in_specs = (
        P("groups", "ctx", "head"),
        P("groups", "ctx", "head"),
        P(None, "groups", "head", "ctx"),
        P("groups", "head", "ctx"),
        P("groups", "head", "ctx"),
        P("head"),
        P("head"),
    )
    out_specs = P("groups", "ctx", "head")
    return jax.shard_map(body, mesh=mesh, in_specs=in_specs, out_specs=out_specs, check_vma=False)
```

```python
import functools

import jax
import jax.numpy as jnp
import numpy as np
from jax import lax
from jax.experimental import pallas as pl
from jax.experimental.pallas import tpu as pltpu
from jax.sharding import PartitionSpec as P

SPAN = 128
HALF = 256
F32 = jnp.float32
BF16 = jnp.bfloat16
MIB = 1024 * 1024
PARAMS = pltpu.CompilerParams(vmem_limit_bytes=4 * MIB)
STAGING_PARAMS = pltpu.CompilerParams(vmem_limit_bytes=10 * MIB)
ENTER, LEAVE, FIRST, TOTAL = range(4)
ROWS = 32
WHOLE = pl.BlockSpec(memory_space=pltpu.VMEM)
ANYWHERE = pl.BlockSpec(memory_space=pl.ANY)


def in_vmem(array):
    return pltpu.with_memory_space_constraint(array, pltpu.VMEM)


def in_hbm(array):
    return pltpu.with_memory_space_constraint(array, pltpu.HBM)


def mm(a, b):
    return jnp.dot(a, b, preferred_element_type=F32)


def mm_nt(a, b):
    return lax.dot_general(a, b, (((1,), (1,)), ((), ())), preferred_element_type=F32)


def iotas(shape):
    return (
        lax.broadcasted_iota(jnp.int32, shape, 0),
        lax.broadcasted_iota(jnp.int32, shape, 1),
    )


def three_parts(v):
    high = v.astype(BF16)
    rest = v - high.astype(F32)
    mid = rest.astype(BF16)
    return [high, mid, (rest - mid.astype(F32)).astype(BF16)]


def fill_tables(step_ref, decay_ref, skip_ref, sums_ref, rise_band, both_ref, rows_ref):
    seqs, heads, length = decay_ref.shape
    blocks = length // SPAN
    _, lane = iotas((SPAN, 4 * heads))
    rising = lane < 2 * heads
    is_high = (lane < heads) | ((lane >= 2 * heads) & (lane < 3 * heads))
    until = sums_ref[:SPAN]
    same = sums_ref[SPAN:]

    def parts_of(v):
        high = v.astype(BF16).astype(F32)
        return jnp.where(is_high[:v.shape[0]], high, v - high).astype(BF16)

    skip = jnp.concatenate([skip_ref[...]] * 4, axis=1)
    for s in range(seqs):
        decays = three_parts(jnp.concatenate([decay_ref[s]] * 4, axis=0))
        steps = three_parts(jnp.concatenate([step_ref[s]] * 4, axis=0))
        enter, leave, first = [], [], []
        before = jnp.zeros((1, 4 * heads), F32)
        for k in range(blocks):
            sl = slice(k * SPAN, (k + 1) * SPAN)
            summed = mm_nt(until, jnp.concatenate([p[:, sl] for p in decays], axis=1))
            step = mm_nt(same, jnp.concatenate([p[:, sl] for p in steps], axis=1))
            middle = summed[SPAN // 2 - 1:SPAN // 2]
            last = summed[SPAN - 1:]
            above = summed - middle
            factor = jnp.exp(jnp.where(rising, above, -above))
            both_ref[s, sl, :] = parts_of(jnp.where(rising, factor, step * factor))
            enter.append(jnp.exp(middle))
            leave.append(jnp.exp(last - middle))
            first.append(jnp.exp(middle + before))
            before = before + last
        table = enter + leave + first + [jnp.exp(before)]
        table = table + [jnp.zeros_like(before)] * (ROWS - 1 - len(table)) + [skip]
        rows_ref[s] = mm(parts_of(jnp.concatenate(table, axis=0)), rise_band)


def tables_kernel(
    step_ref, decay_ref, skip_ref, sums_ref, band_ref, both_ref, rows_ref
):
    fill_tables(step_ref, decay_ref, skip_ref, sums_ref, band_ref[...], both_ref, rows_ref)


def tables(step_size, log_decay, skip, sums, band):
    seqs, heads, length = log_decay.shape
    return pl.pallas_call(
        tables_kernel,
        in_specs=[WHOLE] * 5,
        out_specs=[WHOLE] * 2,
        out_shape=[
            pltpu.VMEM((seqs, length, 4 * heads), BF16),
            pltpu.VMEM((seqs, ROWS, band.shape[1]), F32),
        ],
        compiler_params=PARAMS,
        cost_estimate=pl.CostEstimate(
            flops=10 ** 9, bytes_accessed=10 ** 7, transcendentals=0
        ),
        name="tables",
    )(in_hbm(step_size), in_hbm(log_decay), in_hbm(skip), in_hbm(sums), in_hbm(band))


def weight_kernel(x_ref, both_ref, band_ref, weighted_ref):
    seqs, length, channels = x_ref.shape
    for s in range(seqs):
        for k in range(length // SPAN):
            rows = slice(k * SPAN, (k + 1) * SPAN)
            both = both_ref[s, rows]
            for lo in range(0, channels, HALF):
                sl = slice(lo, lo + HALF)
                wide = mm(both, band_ref[:, sl]).astype(BF16)
                weighted_ref[s, rows, sl] = x_ref[s, rows, sl] * wide


def weigh(x, both, band):
    seqs, length, channels = x.shape
    return pl.pallas_call(
        weight_kernel,
        in_specs=[WHOLE] * 3,
        out_specs=WHOLE,
        out_shape=pltpu.VMEM(x.shape, BF16),
        compiler_params=PARAMS,
        cost_estimate=pl.CostEstimate(
            flops=2 * seqs * length * channels * 256,
            bytes_accessed=4 * seqs * length * channels,
            transcendentals=0,
        ),
        name="weigh",
    )(in_vmem(x), in_vmem(both), band)


def state_kernel(b_ref, weighted_ref, rows_ref, entering_ref, state_ref):
    seqs, length, channels = weighted_ref.shape
    blocks = length // SPAN
    for s in range(seqs):
        for lo in range(0, channels, HALF):
            sl = slice(lo, lo + HALF)
            state = None
            for k in range(blocks):
                rows = slice(k * SPAN, (k + 1) * SPAN)
                added = mm(b_ref[s, :, rows], weighted_ref[s, rows, sl])
                if k > 0:
                    at = ENTER * blocks + k
                    entering = rows_ref[s, at:at + 1, sl] * state
                    entering_ref[s, k - 1, :, sl] = entering.astype(BF16)
                    added = added + entering
                at = LEAVE * blocks + k
                state = rows_ref[s, at:at + 1, sl] * added
            state_ref[s, :, sl] = state.astype(BF16)


def own_states(b, weighted, rows):
    seqs, states, length = b.shape
    channels = weighted.shape[2]
    return pl.pallas_call(
        state_kernel,
        in_specs=[WHOLE] * 3,
        out_specs=[WHOLE] * 2,
        out_shape=[
            pltpu.VMEM((seqs, length // SPAN - 1, states, channels), BF16),
            pltpu.VMEM((seqs, states, channels), BF16),
        ],
        compiler_params=PARAMS,
        cost_estimate=pl.CostEstimate(
            flops=2 * seqs * length * channels * states,
            bytes_accessed=2 * seqs * length * channels,
            transcendentals=0,
        ),
        name="own_states",
    )(b, in_vmem(weighted), in_vmem(rows))


def gate_kernel(gate_ref, x_ref, both_ref, band_ref, rows_ref, lift_ref, skipped_ref):
    seqs, length, channels = lift_ref.shape
    for s in range(seqs):
        for k in range(length // SPAN):
            rows = slice(k * SPAN, (k + 1) * SPAN)
            both = both_ref[s, rows]
            for lo in range(0, channels, HALF):
                sl = slice(lo, lo + HALF)
                half = 0.5 * gate_ref[s, rows, sl].astype(F32)
                gate = (half * jnp.tanh(half) + half).astype(BF16)
                lift_ref[s, rows, sl] = mm(both, band_ref[:, sl]).astype(BF16) * gate
                skip = rows_ref[s, ROWS - 1:ROWS, sl].astype(BF16) * x_ref[s, rows, sl]
                skipped_ref[s, rows, sl] = skip * gate


def gates(gate_in, x, both, band, rows):
    seqs, length, channels = gate_in.shape
    return pl.pallas_call(
        gate_kernel,
        in_specs=[WHOLE] * 5,
        out_specs=[WHOLE, WHOLE],
        out_shape=[pltpu.VMEM(gate_in.shape, BF16)] * 2,
        compiler_params=PARAMS,
        cost_estimate=pl.CostEstimate(
            flops=2 * seqs * length * channels * 256,
            bytes_accessed=8 * seqs * length * channels,
            transcendentals=seqs * length * channels,
        ),
        name="gates",
    )(in_vmem(gate_in), in_vmem(x), in_vmem(both), band, in_vmem(rows))


def left_kernel(b_ref, c_ref, left_ref):
    seqs, states, length = b_ref.shape
    row, col = iotas((SPAN, SPAN))
    for s in range(seqs):
        for k in range(length // SPAN):
            rows = slice(k * SPAN, (k + 1) * SPAN)
            c_t = c_ref[s, :, rows].T
            affinity = mm(c_t, b_ref[s, :, rows])
            left_ref[s, rows, :SPAN] = jnp.where(row >= col, affinity, 0.0).astype(BF16)
            left_ref[s, rows, SPAN:] = c_t


def left_of(b, c):
    seqs, states, length = b.shape
    return pl.pallas_call(
        left_kernel,
        in_specs=[WHOLE] * 2,
        out_specs=WHOLE,
        out_shape=pltpu.VMEM((seqs, length, SPAN + states), BF16),
        compiler_params=PARAMS,
        cost_estimate=pl.CostEstimate(
            flops=2 * seqs * length * SPAN * states,
            bytes_accessed=8 * seqs * length * SPAN,
            transcendentals=0,
        ),
        name="left",
    )(b, c)


def final_kernel(
    weighted_ref, near_ref, far_ref, lift_ref, skipped_ref, left_ref, rows_ref, *refs
):
    gated_ref, square_ref = refs[-2:]
    seqs, length, channels = lift_ref.shape
    blocks = length // SPAN
    for s in range(seqs):
        for k in range(blocks):
            rows = slice(k * SPAN, (k + 1) * SPAN)
            left = left_ref[s, rows]
            squares = jnp.zeros((SPAN, 128), F32)
            at = FIRST * blocks + k
            for lo in range(0, channels, HALF):
                sl = slice(lo, lo + HALF)
                entering = rows_ref[s, at:at + 1, sl].astype(BF16) * refs[s][:, sl]
                if k > 0:
                    entering = entering + jnp.concatenate(
                        [near_ref[s, k - 1, :, sl], far_ref[s, k - 1, :, sl]], axis=0
                    )
                right = jnp.concatenate([weighted_ref[s, rows, sl], entering], axis=0)
                mixed = mm(left, right).astype(BF16)
                gated = lift_ref[s, rows, sl] * mixed + skipped_ref[s, rows, sl]
                gated_ref[s, rows, sl] = gated
                power = gated * gated
                pair = sum(power[:, left_:left_ + 128] for left_ in range(0, HALF, 128))
                squares = squares + pair.astype(F32)
            at = s * blocks + k
            square_ref[at:at + 1] = jnp.sum(squares.T, axis=0, keepdims=True)
    unused = square_ref.shape[0] - seqs * blocks
    if unused:
        square_ref[seqs * blocks:] = jnp.zeros((unused, SPAN), F32)


def final(weighted, near, far, lift, skipped, left, rows, incoming):
    seqs, length, channels = lift.shape
    positions = -(-seqs * length // SPAN // 8) * 8
    return pl.pallas_call(
        final_kernel,
        in_specs=[WHOLE] * (7 + seqs),
        out_specs=[WHOLE] * 2,
        out_shape=[
            pltpu.VMEM(lift.shape, BF16),
            pltpu.VMEM((positions, SPAN), F32),
        ],
        compiler_params=PARAMS,
        cost_estimate=pl.CostEstimate(
            flops=4 * seqs * length * channels * SPAN,
            bytes_accessed=6 * seqs * length * channels,
            transcendentals=0,
        ),
        name="final",
    )(
        in_vmem(weighted), in_vmem(near), in_vmem(far), in_vmem(lift), in_vmem(skipped),
        in_vmem(left), in_vmem(rows), *incoming,
    )


def norm_kernel(all_channels, gated_ref, square_ref, gain_ref, out_hbm, staged, sems):
    seqs, length, channels = gated_ref.shape
    blocks = length // SPAN
    copies = []
    for s in range(seqs):
        for k in range(blocks):
            at = s * blocks + k
            rows = slice(k * SPAN, (k + 1) * SPAN)
            total = jnp.sum(square_ref[:, at], axis=0, keepdims=True)
            inverse = lax.rsqrt(total / all_channels + 1e-05)
            column = jnp.broadcast_to(inverse, (128, SPAN)).T
            for lo in range(0, channels, 128):
                sl = slice(lo, lo + 128)
                staged[s, rows, sl] = (
                    gated_ref[s, rows, sl].astype(F32) * column * gain_ref[:, sl]
                ).astype(BF16)
            place = (s, pl.ds(k * SPAN, SPAN))
            copies.append(
                pltpu.make_async_copy(staged.at[place], out_hbm.at[place], sems.at[at])
            )
            copies[-1].start(priority=k % 2)
    for copy in copies:
        copy.wait()


def normed(gated, squares, gain_row, all_channels):
    seqs, length, channels = gated.shape
    return pl.pallas_call(
        functools.partial(norm_kernel, all_channels),
        in_specs=[WHOLE] * 3,
        out_specs=ANYWHERE,
        out_shape=jax.ShapeDtypeStruct(gated.shape, BF16),
        scratch_shapes=[
            pltpu.VMEM(gated.shape, BF16),
            pltpu.SemaphoreType.DMA((seqs * (length // SPAN),)),
        ],
        compiler_params=STAGING_PARAMS,
        cost_estimate=pl.CostEstimate(
            flops=2 * seqs * length * channels,
            bytes_accessed=4 * seqs * length * channels,
            transcendentals=0,
        ),
        name="normed",
    )(in_vmem(gated), squares, gain_row)


def from_all(shard, axis):
    devices = lax.axis_size(axis)
    return [shard] + [
        lax.ppermute(shard, axis, [(i, (i + by) % devices) for i in range(devices)])
        for by in range(1, devices)
    ]


def as_parts(row):
    high = row.astype(BF16)
    low = (row - high.astype(F32)).astype(BF16)
    return jnp.concatenate([high, low, jnp.zeros((14, row.shape[1]), BF16)], axis=0)


def body(features, gate_in, state_proj, step_size, log_decay, skip_gain, norm_gain):
    seqs, length, channels = features.shape
    heads = step_size.shape[1]
    pair = np.repeat(np.concatenate([np.eye(heads)] * 2), channels // heads, axis=1)
    rise_band = jnp.asarray(np.concatenate([pair, 0 * pair]), BF16)
    fall_band = jnp.asarray(np.concatenate([0 * pair, pair]), BF16)
    until = np.tril(np.ones((SPAN, SPAN)))
    sums = jnp.asarray(np.concatenate([np.tile(until, 3), np.tile(np.eye(SPAN), 3)]), BF16)
    b_own, c_own = lax.optimization_barrier((state_proj[0], state_proj[1]))
    b_far = from_all(b_own, "head")[1:]
    both, rows = tables(step_size, log_decay, skip_gain[None, :], sums, rise_band)
    weighted = weigh(features, both, fall_band)

    place = lax.axis_index("ctx")
    even = place % 2 == 0
    devices = lax.axis_size("ctx")
    swap = [(i, i ^ 1) for i in range(devices)]
    total_at = TOTAL * (length // SPAN)
    decay = [rows[s, total_at:total_at + 1] for s in range(seqs)]

    def past_chip(ends, other, decay_other):
        return jnp.where(
            even,
            other + decay_other * ends[0].astype(F32),
            ends[1].astype(F32) + decay[1] * other,
        )

    def across(past, entered, hop):
        sent = past if entered is None else past + decay_past * entered.astype(F32)
        sent = sent.astype(BF16)
        return sent, lax.ppermute(sent, "ctx", [(hop, hop + 2), (hop + 1, hop + 3)])

    near, near_ends = own_states(b_own, weighted, rows)
    own_rows = b_own.shape[1]
    other = lax.ppermute(
        jnp.concatenate([
            jnp.where(even, near_ends[1], near_ends[0]),
            as_parts(jnp.where(even, decay[1], decay[0])),
        ]),
        "ctx", swap,
    )
    near_other = other[:own_rows].astype(F32)
    decay_other = (
        other[own_rows:own_rows + 1].astype(F32) + other[own_rows + 1:own_rows + 2].astype(F32)
    )
    decay_past = decay_other * jnp.where(even, decay[0], decay[1])
    near_past = past_chip(near_ends, near_other, decay_other)
    near_sent, near_got = across(near_past, None, 0)
    b_far, _ = lax.optimization_barrier((b_far, near_sent))
    b_far = jnp.concatenate(b_far, axis=1)
    far, far_ends = own_states(b_far, weighted, rows)
    far_other = lax.ppermute(jnp.where(even, far_ends[1], far_ends[0]), "ctx", swap).astype(F32)
    far_past = past_chip(far_ends, far_other, decay_other)
    far_sent, far_got = across(far_past, None, 0)
    c_own, features, _ = lax.optimization_barrier((c_own, features, far_sent))
    c = from_all(c_own, "head")
    terms = gates(gate_in, features, both, rise_band, rows)
    c, terms = lax.optimization_barrier((c, terms))
    left = left_of(jnp.concatenate([b_own, b_far], axis=1), jnp.concatenate(c, axis=1))
    near_got, far_got, left = lax.optimization_barrier((near_got, far_got, left))
    for hop in range(2, devices - 2, 2):
        near_got = near_got + across(near_past, near_got, hop)[1]
        far_got = far_got + across(far_past, far_got, hop)[1]
    entered = jnp.concatenate([near_got, far_got])
    entered32 = entered.astype(F32)
    ends = [jnp.concatenate([near_ends[s], far_ends[s]]).astype(F32) for s in range(seqs)]
    shared = lax.ppermute(
        jnp.where(even, ends[0] + decay[0] * entered32, entered32).astype(BF16), "ctx", swap
    )
    end_other = jnp.concatenate([near_other, far_other])
    incoming = [
        jnp.where(even, entered, shared),
        jnp.where(even, shared, (end_other + decay_other * entered32).astype(BF16)),
    ]
    gated, squares = final(weighted, near, far, *terms, left, rows, incoming)
    squares = jnp.stack(from_all(squares, "head"))
    return normed(gated, squares, norm_gain[None, :], channels * lax.axis_size("head"))


def solution(mesh):
    in_specs = (
        P("groups", "ctx", "head"),
        P("groups", "ctx", "head"),
        P(None, "groups", "head", "ctx"),
        P("groups", "head", "ctx"),
        P("groups", "head", "ctx"),
        P("head"),
        P("head"),
    )
    out_specs = P("groups", "ctx", "head")
    return jax.shard_map(body, mesh=mesh, in_specs=in_specs, out_specs=out_specs, check_vma=False)
```

```python
import functools

import jax
import jax.numpy as jnp
import numpy as np
from jax import lax
from jax.experimental import pallas as pl
from jax.experimental.pallas import tpu as pltpu
from jax.sharding import PartitionSpec as P

SPAN = 128
HALF = 256
F32 = jnp.float32
BF16 = jnp.bfloat16
MIB = 1024 * 1024
PARAMS = pltpu.CompilerParams(vmem_limit_bytes=4 * MIB)
COST = pl.CostEstimate(flops=1000, bytes_accessed=1000, transcendentals=0)
STAGING_PARAMS = pltpu.CompilerParams(vmem_limit_bytes=10 * MIB)
ENTER, LEAVE, FIRST, TOTAL = range(4)
ROWS = 32
WHOLE = pl.BlockSpec(memory_space=pltpu.VMEM)
ANYWHERE = pl.BlockSpec(memory_space=pl.ANY)


def in_vmem(array):
    return pltpu.with_memory_space_constraint(array, pltpu.VMEM)


def in_hbm(array):
    return pltpu.with_memory_space_constraint(array, pltpu.HBM)


def mm(a, b):
    return jnp.dot(a, b, preferred_element_type=F32)


def mm_nt(a, b):
    return lax.dot_general(a, b, (((1,), (1,)), ((), ())), preferred_element_type=F32)


def iotas(shape):
    return (
        lax.broadcasted_iota(jnp.int32, shape, 0),
        lax.broadcasted_iota(jnp.int32, shape, 1),
    )


def two_parts(v):
    high = v.astype(BF16)
    return [high, (v - high.astype(F32)).astype(BF16)]


def fill_tables(step_ref, decay_ref, skip_ref, sums_ref, rise_band, both_ref, rows_ref):
    seqs, heads, length = decay_ref.shape
    blocks = length // SPAN
    _, lane = iotas((SPAN, 4 * heads))
    rising = lane < 2 * heads
    is_high = (lane < heads) | ((lane >= 2 * heads) & (lane < 3 * heads))
    until = sums_ref[:SPAN]
    same = sums_ref[SPAN:]

    def parts_of(v):
        high = v.astype(BF16).astype(F32)
        return jnp.where(is_high[:v.shape[0]], high, v - high).astype(BF16)

    skip = jnp.concatenate([skip_ref[...]] * 4, axis=1)
    for s in range(seqs):
        decays = two_parts(jnp.concatenate([decay_ref[s]] * 4, axis=0))
        steps = two_parts(jnp.concatenate([step_ref[s]] * 4, axis=0))
        enter, leave, first = [], [], []
        before = jnp.zeros((1, 4 * heads), F32)
        for k in range(blocks):
            sl = slice(k * SPAN, (k + 1) * SPAN)
            summed = mm_nt(until, jnp.concatenate([p[:, sl] for p in decays], axis=1))
            step = mm_nt(same, jnp.concatenate([p[:, sl] for p in steps], axis=1))
            middle = summed[SPAN // 2 - 1:SPAN // 2]
            last = summed[SPAN - 1:]
            above = summed - middle
            factor = jnp.exp(jnp.where(rising, above, -above))
            both_ref[s, sl, :] = parts_of(jnp.where(rising, factor, step * factor))
            enter.append(jnp.exp(middle))
            leave.append(jnp.exp(last - middle))
            first.append(jnp.exp(middle + before))
            before = before + last
        table = enter + leave + first + [jnp.exp(before)]
        table = table + [jnp.zeros_like(before)] * (ROWS - 1 - len(table)) + [skip]
        rows_ref[s] = mm(parts_of(jnp.concatenate(table, axis=0)), rise_band)


def front_kernel(
    x_hbm, step_hbm, decay_hbm, skip_hbm, sums_hbm, bands_hbm,
    x_ref, weighted_ref, both_ref, rows_ref, bands, step, decay, skip, sums, sems,
):
    seqs, length, channels = x_ref.shape
    heads = decay.shape[1]
    pairs = [(decay_hbm, decay), (step_hbm, step), (sums_hbm, sums), (skip_hbm, skip)]
    pairs += [(x_hbm.at[s], x_ref.at[s]) for s in range(seqs)] + [(bands_hbm, bands)]
    copies = [
        pltpu.make_async_copy(source, target, sems.at[i])
        for i, (source, target) in enumerate(pairs)
    ]
    for copy in copies:
        copy.start()
    for copy in copies[:4] + copies[-1:]:
        copy.wait()
    fill_tables(step, decay, skip, sums, bands[2 * heads:], both_ref, rows_ref)
    for s in range(seqs):
        copies[4 + s].wait()
        for k in range(length // SPAN):
            rows = slice(k * SPAN, (k + 1) * SPAN)
            both = both_ref[s, rows]
            for lo in range(0, channels, HALF):
                sl = slice(lo, lo + HALF)
                wide = mm(both, bands[:4 * heads, sl]).astype(BF16)
                weighted_ref[s, rows, sl] = x_ref[s, rows, sl] * wide


def front(features, step_size, log_decay, skip, sums, bands):
    seqs, length, channels = features.shape
    heads = step_size.shape[1]
    operands = [features, step_size, log_decay, skip, sums, bands]
    return pl.pallas_call(
        front_kernel,
        in_specs=[ANYWHERE] * 6,
        out_specs=[WHOLE] * 5,
        out_shape=[
            pltpu.VMEM(features.shape, BF16),
            pltpu.VMEM(features.shape, BF16),
            pltpu.VMEM((seqs, length, 4 * heads), BF16),
            pltpu.VMEM((seqs, ROWS, channels), F32),
            pltpu.VMEM(bands.shape, BF16),
        ],
        scratch_shapes=[
            pltpu.VMEM(step_size.shape, F32),
            pltpu.VMEM(log_decay.shape, F32),
            pltpu.VMEM(skip.shape, F32),
            pltpu.VMEM(sums.shape, BF16),
            pltpu.SemaphoreType.DMA((seqs + 5,)),
        ],
        compiler_params=PARAMS,
        cost_estimate=COST,
        name="front",
    )(*[in_hbm(operand) for operand in operands])


def state_kernel(b_ref, weighted_ref, rows_ref, entering_ref, state_ref):
    seqs, length, channels = weighted_ref.shape
    blocks = length // SPAN
    for s in range(seqs):
        for lo in range(0, channels, HALF):
            sl = slice(lo, lo + HALF)
            state = None
            for k in range(blocks):
                rows = slice(k * SPAN, (k + 1) * SPAN)
                added = mm(b_ref[s, :, rows], weighted_ref[s, rows, sl])
                if k > 0:
                    at = ENTER * blocks + k
                    entering = rows_ref[s, at:at + 1, sl] * state
                    entering_ref[s, k - 1, :, sl] = entering.astype(BF16)
                    added = added + entering
                at = LEAVE * blocks + k
                state = rows_ref[s, at:at + 1, sl] * added
            state_ref[s, :, sl] = state.astype(BF16)


def own_states(b, weighted, rows):
    seqs, states, length = b.shape
    channels = weighted.shape[2]
    return pl.pallas_call(
        state_kernel,
        in_specs=[WHOLE] * 3,
        out_specs=[WHOLE] * 2,
        out_shape=[
            pltpu.VMEM((seqs, length // SPAN - 1, states, channels), BF16),
            pltpu.VMEM((seqs, states, channels), BF16),
        ],
        compiler_params=PARAMS,
        cost_estimate=COST,
        name="own_states",
    )(b, in_vmem(weighted), in_vmem(rows))


def gate_kernel(seq, gate_ref, x_ref, both_ref, bands_ref, rows_ref, lift_ref, skipped_ref):
    length, channels = lift_ref.shape
    heads4 = both_ref.shape[2]
    band = slice(heads4 // 2, heads4 // 2 + heads4)
    for k in range(length // SPAN):
        rows = slice(k * SPAN, (k + 1) * SPAN)
        both = both_ref[seq, rows]
        for lo in range(0, channels, HALF):
            sl = slice(lo, lo + HALF)
            half = 0.5 * gate_ref[seq, rows, sl].astype(F32)
            gate = (half * jnp.tanh(half) + half).astype(BF16)
            lift_ref[rows, sl] = mm(both, bands_ref[band, sl]).astype(BF16) * gate
            skip = rows_ref[seq, ROWS - 1:ROWS, sl].astype(BF16) * x_ref[seq, rows, sl]
            skipped_ref[rows, sl] = skip * gate


def gates(gate_in, x, both, bands, rows, seq):
    _, length, channels = gate_in.shape
    return pl.pallas_call(
        functools.partial(gate_kernel, seq),
        in_specs=[WHOLE] * 5,
        out_specs=[WHOLE, WHOLE],
        out_shape=[pltpu.VMEM((length, channels), BF16)] * 2,
        compiler_params=PARAMS,
        cost_estimate=COST,
        name="gates",
    )(in_vmem(gate_in), in_vmem(x), in_vmem(both), in_vmem(bands), in_vmem(rows))


def local_kernel(
    seq, weighted_ref, near_ref, far_ref, lift_ref, skipped_ref, b_ref, c_ref, rows_ref,
    own_ref, factor_ref, c_t_ref,
):
    length, channels = own_ref.shape
    blocks = length // SPAN
    row, col = iotas((SPAN, SPAN))
    for k in range(blocks):
        rows = slice(k * SPAN, (k + 1) * SPAN)
        c_t = c_ref[seq, :, rows].T
        c_t_ref[rows] = c_t
        affinity = mm(c_t, b_ref[seq, :, rows])
        left = jnp.where(row >= col, affinity, 0.0).astype(BF16)
        if k > 0:
            left = jnp.concatenate([left, c_t], axis=1)
        at = FIRST * blocks + k
        for lo in range(0, channels, HALF):
            sl = slice(lo, lo + HALF)
            right = weighted_ref[seq, rows, sl]
            if k > 0:
                right = jnp.concatenate(
                    [right, near_ref[seq, k - 1, :, sl], far_ref[seq, k - 1, :, sl]], axis=0
                )
            lift = lift_ref[rows, sl]
            own_ref[rows, sl] = lift * mm(left, right).astype(BF16) + skipped_ref[rows, sl]
            factor_ref[rows, sl] = lift * rows_ref[seq, at:at + 1, sl].astype(BF16)


def local_terms(weighted, near, far, lift, skipped, b, c, rows, seq):
    length, channels = lift.shape
    states = b.shape[1]
    return pl.pallas_call(
        functools.partial(local_kernel, seq),
        in_specs=[WHOLE] * 8,
        out_specs=[WHOLE] * 3,
        out_shape=[
            pltpu.VMEM(lift.shape, BF16),
            pltpu.VMEM(lift.shape, BF16),
            pltpu.VMEM((length, states), BF16),
        ],
        compiler_params=PARAMS,
        cost_estimate=COST,
        name="local_terms",
    )(
        in_vmem(weighted), in_vmem(near), in_vmem(far), in_vmem(lift), in_vmem(skipped), b, c,
        in_vmem(rows),
    )


def joined_kernel(seqs, *refs):
    gated_ref, square_ref = refs[-2:]
    length, channels = refs[0].shape
    blocks = length // SPAN
    for s in range(seqs):
        own_ref, factor_ref, c_t_ref, incoming_ref = refs[4 * s:4 * s + 4]
        for k in range(blocks):
            rows = slice(k * SPAN, (k + 1) * SPAN)
            c_t = c_t_ref[rows]
            squares = jnp.zeros((SPAN, 128), F32)
            for lo in range(0, channels, HALF):
                sl = slice(lo, lo + HALF)
                carried = mm(c_t, incoming_ref[:, sl]).astype(BF16)
                gated = own_ref[rows, sl] + factor_ref[rows, sl] * carried
                gated_ref[s, rows, sl] = gated
                power = gated * gated
                pair = sum(power[:, left:left + 128] for left in range(0, HALF, 128))
                squares = squares + pair.astype(F32)
            at = s * blocks + k
            square_ref[at:at + 1] = jnp.sum(squares.T, axis=0, keepdims=True)
    unused = square_ref.shape[0] - seqs * blocks
    if unused:
        square_ref[seqs * blocks:] = jnp.zeros((unused, SPAN), F32)


def joined(terms, incoming):
    seqs = len(terms)
    length, channels = terms[0][0].shape
    states = terms[0][2].shape[1]
    operands = []
    for s in range(seqs):
        operands += [in_vmem(term) for term in terms[s]] + [incoming[s]]
    return pl.pallas_call(
        functools.partial(joined_kernel, seqs),
        in_specs=[WHOLE] * len(operands),
        out_specs=[WHOLE] * 2,
        out_shape=[
            pltpu.VMEM((seqs, length, channels), BF16),
            pltpu.VMEM((-(-seqs * length // SPAN // 8) * 8, SPAN), F32),
        ],
        compiler_params=PARAMS,
        cost_estimate=COST,
        name="joined",
    )(*operands)


def norm_kernel(all_channels, gated_ref, square_ref, gain_ref, out_hbm, staged, sems):
    seqs, length, channels = gated_ref.shape
    blocks = length // SPAN
    copies = []
    for s in range(seqs):
        for k in range(blocks):
            at = s * blocks + k
            rows = slice(k * SPAN, (k + 1) * SPAN)
            total = jnp.sum(square_ref[:, at], axis=0, keepdims=True)
            inverse = lax.rsqrt(total / all_channels + 1e-05)
            column = jnp.broadcast_to(inverse, (128, SPAN)).T
            for lo in range(0, channels, 128):
                sl = slice(lo, lo + 128)
                staged[s, rows, sl] = (
                    gated_ref[s, rows, sl].astype(F32) * column * gain_ref[:, sl]
                ).astype(BF16)
            place = (s, pl.ds(k * SPAN, SPAN))
            copies.append(
                pltpu.make_async_copy(staged.at[place], out_hbm.at[place], sems.at[at])
            )
            copies[-1].start(priority=k % 2)
    for copy in copies:
        copy.wait()


def normed(gated, squares, gain_row, all_channels):
    seqs, length, channels = gated.shape
    return pl.pallas_call(
        functools.partial(norm_kernel, all_channels),
        in_specs=[WHOLE] * 3,
        out_specs=ANYWHERE,
        out_shape=jax.ShapeDtypeStruct(gated.shape, BF16),
        scratch_shapes=[
            pltpu.VMEM(gated.shape, BF16),
            pltpu.SemaphoreType.DMA((seqs * (length // SPAN),)),
        ],
        compiler_params=STAGING_PARAMS,
        cost_estimate=COST,
        name="normed",
    )(in_vmem(gated), squares, gain_row)


def from_all(shard, axis):
    devices = lax.axis_size(axis)
    paired = devices & (devices - 1) == 0
    return [shard] + [
        lax.ppermute(
            shard, axis, [(i, i ^ by if paired else (i + by) % devices) for i in range(devices)]
        )
        for by in range(1, devices)
    ]


def as_parts(row):
    high = row.astype(BF16)
    low = (row - high.astype(F32)).astype(BF16)
    return jnp.concatenate([high, low, jnp.zeros((14, row.shape[1]), BF16)], axis=0)


def body(features, gate_in, state_proj, step_size, log_decay, skip_gain, norm_gain):
    seqs, length, channels = features.shape
    heads = step_size.shape[1]
    pair = np.repeat(np.concatenate([np.eye(heads)] * 2), channels // heads, axis=1)
    bands = jnp.asarray(np.concatenate([0 * pair, pair, 0 * pair]), BF16)
    until = np.tril(np.ones((SPAN, SPAN)))
    sums = jnp.asarray(np.concatenate([np.tile(until, 2), np.tile(np.eye(SPAN), 2)]), BF16)
    b_own, c_own = lax.optimization_barrier((state_proj[0], state_proj[1]))
    b_far = from_all(b_own, "head")[1:]
    x, weighted, both, rows, bands = front(
        features, step_size, log_decay, skip_gain[None, :], sums, bands
    )

    place = lax.axis_index("ctx")
    even = place % 2 == 0
    devices = lax.axis_size("ctx")
    swap = [(i, i ^ 1) for i in range(devices)]
    total_at = TOTAL * (length // SPAN)
    decay = [rows[s, total_at:total_at + 1] for s in range(seqs)]

    def past_chip(ends, other, decay_other):
        return jnp.where(
            even,
            other + decay_other * ends[0].astype(F32),
            ends[1].astype(F32) + decay[1] * other,
        )

    def across(past, entered, hop):
        sent = past if entered is None else past + decay_past * entered.astype(F32)
        sent = sent.astype(BF16)
        return sent, lax.ppermute(sent, "ctx", [(hop, hop + 2), (hop + 1, hop + 3)])

    near, near_ends = own_states(b_own, weighted, rows)
    own_rows = b_own.shape[1]
    other = lax.ppermute(
        jnp.concatenate([
            jnp.where(even, near_ends[1], near_ends[0]),
            as_parts(jnp.where(even, decay[1], decay[0])),
        ]),
        "ctx", swap,
    )
    gated_by = [None] * seqs
    gate_x, _ = lax.optimization_barrier((x, near_ends))
    gated_by[0] = gates(gate_in, gate_x, both, bands, rows, 0)
    b_far, gated_by[0] = lax.optimization_barrier((b_far, gated_by[0]))
    b_far = jnp.concatenate(b_far, axis=1)
    far, far_ends = own_states(b_far, weighted, rows)
    far_other = lax.ppermute(jnp.where(even, far_ends[1], far_ends[0]), "ctx", swap).astype(F32)
    other, _ = lax.optimization_barrier((other, far_ends))
    near_other = other[:own_rows].astype(F32)
    decay_other = (
        other[own_rows:own_rows + 1].astype(F32) + other[own_rows + 1:own_rows + 2].astype(F32)
    )
    decay_past = decay_other * jnp.where(even, decay[0], decay[1])
    near_past = past_chip(near_ends, near_other, decay_other)
    near_sent, near_got = across(near_past, None, 0)
    far_other, _ = lax.optimization_barrier((far_other, near_sent))
    far_past = past_chip(far_ends, far_other, decay_other)
    far_sent, far_got = across(far_past, None, 0)
    c_own, gate_x, _ = lax.optimization_barrier((c_own, x, far_sent))
    c = from_all(c_own, "head")
    for s in range(1, seqs):
        gated_by[s] = gates(gate_in, gate_x, both, bands, rows, s)
    c, gated_by = lax.optimization_barrier((c, gated_by))
    c = jnp.concatenate(c, axis=1)
    b = jnp.concatenate([b_own, b_far], axis=1)
    terms = [local_terms(weighted, near, far, *gated_by[s], b, c, rows, s) for s in range(seqs)]
    near_got, far_got, terms = lax.optimization_barrier((near_got, far_got, terms))
    for hop in range(2, devices - 2, 2):
        near_got = near_got + across(near_past, near_got, hop)[1]
        far_got = far_got + across(far_past, far_got, hop)[1]
    entered = jnp.concatenate([near_got, far_got])
    entered32 = entered.astype(F32)
    ends = [jnp.concatenate([near_ends[s], far_ends[s]]).astype(F32) for s in range(seqs)]
    shared = lax.ppermute(
        jnp.where(even, ends[0] + decay[0] * entered32, entered32).astype(BF16), "ctx", swap
    )
    end_other = jnp.concatenate([near_other, far_other])
    incoming = [
        jnp.where(even, entered, shared),
        jnp.where(even, shared, (end_other + decay_other * entered32).astype(BF16)),
    ]
    gated, squares = joined(terms, incoming)
    squares = jnp.stack(from_all(squares, "head"))
    return normed(gated, squares, norm_gain[None, :], channels * lax.axis_size("head"))


def solution(mesh):
    in_specs = (
        P("groups", "ctx", "head"),
        P("groups", "ctx", "head"),
        P(None, "groups", "head", "ctx"),
        P("groups", "head", "ctx"),
        P("groups", "head", "ctx"),
        P("head"),
        P("head"),
    )
    out_specs = P("groups", "ctx", "head")
    return jax.shard_map(body, mesh=mesh, in_specs=in_specs, out_specs=out_specs, check_vma=False)
```

```python
import functools

import jax
import jax.numpy as jnp
import numpy as np
from jax import lax
from jax.experimental import pallas as pl
from jax.experimental.pallas import tpu as pltpu
from jax.sharding import PartitionSpec as P

SPAN = 128
HALF = 256
F32 = jnp.float32
BF16 = jnp.bfloat16
MIB = 1024 * 1024
PARAMS = pltpu.CompilerParams(vmem_limit_bytes=4 * MIB)
COST = pl.CostEstimate(flops=1000, bytes_accessed=1000, transcendentals=0)
GATES_COST = pl.CostEstimate(flops=2 * 10**9, bytes_accessed=25 * 10**6, transcendentals=3 * 10**6)
LEFT_COST = pl.CostEstimate(flops=5 * 10**7, bytes_accessed=16 * 10**5, transcendentals=0)
STAGING_PARAMS = pltpu.CompilerParams(vmem_limit_bytes=10 * MIB)
ENTER, LEAVE, FIRST, TOTAL = range(4)
ROWS = 32
WHOLE = pl.BlockSpec(memory_space=pltpu.VMEM)
ANYWHERE = pl.BlockSpec(memory_space=pl.ANY)


def in_vmem(array):
    return pltpu.with_memory_space_constraint(array, pltpu.VMEM)


def in_hbm(array):
    return pltpu.with_memory_space_constraint(array, pltpu.HBM)


def mm(a, b):
    return jnp.dot(a, b, preferred_element_type=F32)


def mm_nt(a, b):
    return lax.dot_general(a, b, (((1,), (1,)), ((), ())), preferred_element_type=F32)


def iotas(shape):
    return (
        lax.broadcasted_iota(jnp.int32, shape, 0),
        lax.broadcasted_iota(jnp.int32, shape, 1),
    )


def two_parts(v):
    high = v.astype(BF16)
    return [high, (v - high.astype(F32)).astype(BF16)]


def fill_tables(step_ref, decay_ref, skip_ref, sums_ref, rise_band, both_ref, rows_ref):
    seqs, heads, length = decay_ref.shape
    blocks = length // SPAN
    _, lane = iotas((SPAN, 4 * heads))
    rising = lane < 2 * heads
    is_high = (lane < heads) | ((lane >= 2 * heads) & (lane < 3 * heads))
    until = sums_ref[:SPAN]
    same = sums_ref[SPAN:]

    def parts_of(v):
        high = v.astype(BF16).astype(F32)
        return jnp.where(is_high[:v.shape[0]], high, v - high).astype(BF16)

    skip = jnp.concatenate([skip_ref[...]] * 4, axis=1)
    for s in range(seqs):
        decays = two_parts(jnp.concatenate([decay_ref[s]] * 4, axis=0))
        steps = two_parts(jnp.concatenate([step_ref[s]] * 4, axis=0))
        enter, leave, first = [], [], []
        before = jnp.zeros((1, 4 * heads), F32)
        for k in range(blocks):
            sl = slice(k * SPAN, (k + 1) * SPAN)
            summed = mm_nt(until, jnp.concatenate([p[:, sl] for p in decays], axis=1))
            step = mm_nt(same, jnp.concatenate([p[:, sl] for p in steps], axis=1))
            middle = summed[SPAN // 2 - 1:SPAN // 2]
            last = summed[SPAN - 1:]
            above = summed - middle
            factor = jnp.exp(jnp.where(rising, above, -above))
            both_ref[s, sl, :] = parts_of(jnp.where(rising, factor, step * factor))
            enter.append(jnp.exp(middle))
            leave.append(jnp.exp(last - middle))
            first.append(jnp.exp(middle + before))
            before = before + last
        table = enter + leave + first + [jnp.exp(before)]
        table = table + [jnp.zeros_like(before)] * (ROWS - 1 - len(table)) + [skip]
        rows_ref[s] = mm(parts_of(jnp.concatenate(table, axis=0)), rise_band)


def front_kernel(
    x_hbm, step_hbm, decay_hbm, skip_hbm, sums_hbm, bands_hbm,
    x_ref, weighted_ref, both_ref, rows_ref, bands, step, decay, skip, sums, sems,
):
    seqs, length, channels = x_ref.shape
    heads = decay.shape[1]
    pairs = [
        (decay_hbm, decay), (step_hbm, step), (sums_hbm, sums), (skip_hbm, skip), (bands_hbm, bands)
    ]
    small = len(pairs)
    pairs += [(x_hbm.at[s], x_ref.at[s]) for s in range(seqs)]
    copies = [
        pltpu.make_async_copy(source, target, sems.at[i])
        for i, (source, target) in enumerate(pairs)
    ]
    for copy in copies:
        copy.start()
    for copy in copies[:small]:
        copy.wait()
    fill_tables(step, decay, skip, sums, bands[2 * heads:], both_ref, rows_ref)
    for s in range(seqs):
        copies[small + s].wait()
        for k in range(length // SPAN):
            rows = slice(k * SPAN, (k + 1) * SPAN)
            both = both_ref[s, rows]
            for lo in range(0, channels, HALF):
                sl = slice(lo, lo + HALF)
                wide = mm(both, bands[:4 * heads, sl]).astype(BF16)
                weighted_ref[s, rows, sl] = x_ref[s, rows, sl] * wide


def front(features, step_size, log_decay, skip, sums, bands):
    seqs, length, channels = features.shape
    heads = step_size.shape[1]
    operands = [features, step_size, log_decay, skip, sums, bands]
    return pl.pallas_call(
        front_kernel,
        in_specs=[ANYWHERE] * 6,
        out_specs=[WHOLE] * 5,
        out_shape=[
            pltpu.VMEM(features.shape, BF16),
            pltpu.VMEM(features.shape, BF16),
            pltpu.VMEM((seqs, length, 4 * heads), BF16),
            pltpu.VMEM((seqs, ROWS, channels), F32),
            pltpu.VMEM(bands.shape, BF16),
        ],
        scratch_shapes=[
            pltpu.VMEM(step_size.shape, F32),
            pltpu.VMEM(log_decay.shape, F32),
            pltpu.VMEM(skip.shape, F32),
            pltpu.VMEM(sums.shape, BF16),
            pltpu.SemaphoreType.DMA((seqs + 5,)),
        ],
        compiler_params=PARAMS,
        cost_estimate=COST,
        name="front",
    )(*[in_hbm(operand) for operand in operands])


def state_kernel(b_ref, weighted_ref, rows_ref, entering_ref, state_ref):
    seqs, length, channels = weighted_ref.shape
    blocks = length // SPAN
    for s in range(seqs):
        for lo in range(0, channels, HALF):
            sl = slice(lo, lo + HALF)
            state = None
            for k in range(blocks):
                rows = slice(k * SPAN, (k + 1) * SPAN)
                added = mm(b_ref[s, :, rows], weighted_ref[s, rows, sl])
                if k > 0:
                    at = ENTER * blocks + k
                    entering = rows_ref[s, at:at + 1, sl] * state
                    entering_ref[s, k - 1, :, sl] = entering.astype(BF16)
                    added = added + entering
                at = LEAVE * blocks + k
                state = rows_ref[s, at:at + 1, sl] * added
            state_ref[s, :, sl] = state.astype(BF16)


def own_states(b, weighted, rows):
    seqs, states, length = b.shape
    channels = weighted.shape[2]
    return pl.pallas_call(
        state_kernel,
        in_specs=[WHOLE] * 3,
        out_specs=[WHOLE] * 2,
        out_shape=[
            pltpu.VMEM((seqs, length // SPAN - 1, states, channels), BF16),
            pltpu.VMEM((seqs, states, channels), BF16),
        ],
        compiler_params=PARAMS,
        cost_estimate=COST,
        name="own_states",
    )(b, in_vmem(weighted), in_vmem(rows))


def gate_kernel(gate_ref, x_ref, both_ref, bands_ref, rows_ref, lift_ref, skipped_ref):
    seqs, length, channels = lift_ref.shape
    heads4 = both_ref.shape[2]
    band = slice(heads4 // 2, heads4 // 2 + heads4)
    for s in range(seqs):
        for k in range(length // SPAN):
            rows = slice(k * SPAN, (k + 1) * SPAN)
            both = both_ref[s, rows]
            for lo in range(0, channels, HALF):
                sl = slice(lo, lo + HALF)
                half = 0.5 * gate_ref[s, rows, sl].astype(F32)
                gate = (half * jnp.tanh(half) + half).astype(BF16)
                lift_ref[s, rows, sl] = mm(both, bands_ref[band, sl]).astype(BF16) * gate
                skip = rows_ref[s, ROWS - 1:ROWS, sl].astype(BF16) * x_ref[s, rows, sl]
                skipped_ref[s, rows, sl] = skip * gate


def gates(gate_in, x, both, bands, rows):
    return pl.pallas_call(
        gate_kernel,
        in_specs=[WHOLE] * 5,
        out_specs=[WHOLE, WHOLE],
        out_shape=[pltpu.VMEM(gate_in.shape, BF16)] * 2,
        compiler_params=PARAMS,
        cost_estimate=GATES_COST,
        name="gates",
    )(in_vmem(gate_in), in_vmem(x), in_vmem(both), in_vmem(bands), in_vmem(rows))


def left_kernel(b_ref, c_ref, left_ref):
    seqs, states, length = b_ref.shape
    row, col = iotas((SPAN, SPAN))
    for s in range(seqs):
        for k in range(length // SPAN):
            rows = slice(k * SPAN, (k + 1) * SPAN)
            c_t = c_ref[s, :, rows].T
            affinity = mm(c_t, b_ref[s, :, rows])
            left_ref[s, rows, :SPAN] = jnp.where(row >= col, affinity, 0.0).astype(BF16)
            left_ref[s, rows, SPAN:] = c_t


def left_of(b, c):
    seqs, states, length = b.shape
    return pl.pallas_call(
        left_kernel,
        in_specs=[WHOLE] * 2,
        out_specs=WHOLE,
        out_shape=pltpu.VMEM((seqs, length, SPAN + states), BF16),
        compiler_params=PARAMS,
        cost_estimate=LEFT_COST,
        name="left",
    )(b, c)


def final_kernel(
    seq_ref, weighted_ref, near_ref, far_ref, lift_ref, skipped_ref, left_ref, rows_ref,
    incoming_ref, gated_ref, square_ref,
):
    length, channels = gated_ref.shape
    blocks = length // SPAN
    s = seq_ref[0]
    for k in range(blocks):
        rows = slice(k * SPAN, (k + 1) * SPAN)
        left = left_ref[s, rows]
        squares = jnp.zeros((SPAN, 128), F32)
        at = FIRST * blocks + k
        for lo in range(0, channels, HALF):
            sl = slice(lo, lo + HALF)
            entering = rows_ref[s, at:at + 1, sl].astype(BF16) * incoming_ref[:, sl]
            if k > 0:
                entering = entering + jnp.concatenate(
                    [near_ref[s, k - 1, :, sl], far_ref[s, k - 1, :, sl]], axis=0
                )
            right = jnp.concatenate([weighted_ref[s, rows, sl], entering], axis=0)
            mixed = mm(left, right).astype(BF16)
            gated = lift_ref[s, rows, sl] * mixed + skipped_ref[s, rows, sl]
            gated_ref[rows, sl] = gated
            power = gated * gated
            pair = sum(power[:, half:half + 128] for half in range(0, HALF, 128))
            squares = squares + pair.astype(F32)
        square_ref[k:k + 1] = jnp.sum(squares.T, axis=0, keepdims=True)
    unused = square_ref.shape[0] - blocks
    if unused:
        square_ref[blocks:] = jnp.zeros((unused, SPAN), F32)


def final(seq, weighted, near, far, lift, skipped, left, rows, incoming):
    _, length, channels = lift.shape
    return pl.pallas_call(
        final_kernel,
        in_specs=[pl.BlockSpec(memory_space=pltpu.SMEM)] + [WHOLE] * 8,
        out_specs=[WHOLE] * 2,
        out_shape=[
            pltpu.VMEM((length, channels), BF16),
            pltpu.VMEM((-(-length // SPAN // 8) * 8, SPAN), F32),
        ],
        compiler_params=PARAMS,
        cost_estimate=COST,
        name="final",
    )(
        seq, in_vmem(weighted), in_vmem(near), in_vmem(far), in_vmem(lift), in_vmem(skipped),
        in_vmem(left), in_vmem(rows), incoming,
    )


def norm_kernel(all_channels, seq_ref, square_ref, gain_ref, *refs):
    gated_refs, (out_hbm, staged, sems) = refs[:-3], refs[-3:]
    length, channels = gated_refs[0].shape
    blocks = length // SPAN
    stride = square_ref.shape[0] // len(gated_refs)
    copies = []
    for number, gated_ref in enumerate(gated_refs):
        s = lax.rem(seq_ref[0] + number, len(gated_refs))
        for k in range(blocks):
            rows = slice(k * SPAN, (k + 1) * SPAN)
            at = number * stride + k
            inverse = lax.rsqrt(square_ref[at:at + 1] / all_channels + 1e-05)
            column = jnp.broadcast_to(inverse, (128, SPAN)).T
            for lo in range(0, channels, 128):
                sl = slice(lo, lo + 128)
                staged[number, rows, sl] = (
                    gated_ref[rows, sl].astype(F32) * column * gain_ref[:, sl]
                ).astype(BF16)
            place = pl.ds(k * SPAN, SPAN)
            copies.append(
                pltpu.make_async_copy(
                    staged.at[number, place], out_hbm.at[s, place], sems.at[number * blocks + k]
                )
            )
            copies[-1].start(priority=k % 2)
    for copy in copies:
        copy.wait()


def normed(first, gated, squares, gain_row, all_channels):
    seqs = len(gated)
    length, channels = gated[0].shape
    return pl.pallas_call(
        functools.partial(norm_kernel, all_channels),
        in_specs=[pl.BlockSpec(memory_space=pltpu.SMEM)] + [WHOLE] * (2 + seqs),
        out_specs=ANYWHERE,
        out_shape=jax.ShapeDtypeStruct((seqs, length, channels), BF16),
        scratch_shapes=[
            pltpu.VMEM((seqs, length, channels), BF16),
            pltpu.SemaphoreType.DMA((seqs * (length // SPAN),)),
        ],
        compiler_params=STAGING_PARAMS,
        cost_estimate=COST,
        name="normed",
    )(first, squares, gain_row, *[in_vmem(one) for one in gated])


def from_all(shard, axis):
    devices = lax.axis_size(axis)
    paired = devices & (devices - 1) == 0
    return [shard] + [
        lax.ppermute(
            shard, axis, [(i, i ^ by if paired else (i + by) % devices) for i in range(devices)]
        )
        for by in range(1, devices)
    ]


def summed_over(value, axis):
    devices = lax.axis_size(axis)
    if devices & (devices - 1):
        return lax.psum(value, axis)
    by = 1
    while by < devices:
        value = value + lax.ppermute(value, axis, [(i, i ^ by) for i in range(devices)])
        by *= 2
    return value


def as_parts(row):
    high = row.astype(BF16)
    low = (row - high.astype(F32)).astype(BF16)
    return jnp.concatenate([high, low, jnp.zeros((14, row.shape[1]), BF16)], axis=0)


def body(features, gate_in, state_proj, step_size, log_decay, skip_gain, norm_gain):
    seqs, length, channels = features.shape
    heads = step_size.shape[1]
    pair = np.repeat(np.concatenate([np.eye(heads)] * 2), channels // heads, axis=1)
    bands = jnp.asarray(np.concatenate([0 * pair, pair, 0 * pair]), BF16)
    until = np.tril(np.ones((SPAN, SPAN)))
    sums = jnp.asarray(np.concatenate([np.tile(until, 2), np.tile(np.eye(SPAN), 2)]), BF16)
    b_own, c_own = lax.optimization_barrier((state_proj[0], state_proj[1]))
    b_far = from_all(b_own, "head")[1:]
    x, weighted, both, rows, bands = front(
        features, step_size, log_decay, skip_gain[None, :], sums, bands
    )

    place = lax.axis_index("ctx")
    even = place % 2 == 0
    mine = (place % 2).astype(jnp.int32)[None]
    devices = lax.axis_size("ctx")
    swap = [(i, i ^ 1) for i in range(devices)]
    total_at = TOTAL * (length // SPAN)
    decays = [rows[s, total_at:total_at + 1] for s in range(seqs)]
    decay = jnp.where(even, decays[0], decays[1])

    def past_chip(end, other, decay_other):
        return jnp.where(even, other + decay_other * end, end + decay * other)

    def across(past, entered, hop):
        sent = past if entered is None else past + decay_past * entered.astype(F32)
        sent = sent.astype(BF16)
        return sent, lax.ppermute(sent, "ctx", [(hop, hop + 2), (hop + 1, hop + 3)])

    near, near_ends = own_states(b_own, weighted, rows)
    own_rows = b_own.shape[1]
    other = lax.ppermute(
        jnp.concatenate([
            jnp.where(even, near_ends[1], near_ends[0]),
            as_parts(jnp.where(even, decays[1], decays[0])),
        ]),
        "ctx", swap,
    )
    b_far, _ = lax.optimization_barrier((b_far, near_ends))
    b_far = jnp.concatenate(b_far, axis=1)
    far, far_ends = own_states(b_far, weighted, rows)
    far_other = lax.ppermute(jnp.where(even, far_ends[1], far_ends[0]), "ctx", swap)
    other, _ = lax.optimization_barrier((other, far_ends))
    near_other = other[:own_rows].astype(F32)
    decay_other = (
        other[own_rows:own_rows + 1].astype(F32) + other[own_rows + 1:own_rows + 2].astype(F32)
    )
    decay_past = decay_other * decay
    near_end = jnp.where(even, near_ends[0], near_ends[1]).astype(F32)
    near_past = past_chip(near_end, near_other, decay_other)
    near_sent, near_got = across(near_past, None, 0)
    far_other, _ = lax.optimization_barrier((far_other, near_sent))
    far_other = far_other.astype(F32)
    far_end = jnp.where(even, far_ends[0], far_ends[1]).astype(F32)
    far_past = past_chip(far_end, far_other, decay_other)
    far_sent, far_got = across(far_past, None, 0)
    c_own, x, _ = lax.optimization_barrier((c_own, x, far_sent))
    c = from_all(c_own, "head")
    gated_by = gates(gate_in, x, both, bands, rows)
    c, gated_by = lax.optimization_barrier((c, gated_by))
    left = left_of(jnp.concatenate([b_own, b_far], axis=1), jnp.concatenate(c, axis=1))
    near_got, far_got, left = lax.optimization_barrier((near_got, far_got, left))
    for hop in range(2, devices - 2, 2):
        near_got = near_got + across(near_past, near_got, hop)[1]
        far_got = far_got + across(far_past, far_got, hop)[1]
    entered = jnp.concatenate([near_got, far_got])
    entered32 = entered.astype(F32)
    end = jnp.concatenate([near_end, far_end])
    end_other = jnp.concatenate([near_other, far_other])
    shared = lax.ppermute(
        jnp.where(even, end + decay * entered32, entered32).astype(BF16), "ctx", swap
    )
    incoming = jnp.where(even, entered32, end_other + decay_other * entered32).astype(BF16)
    operands = (weighted, near, far, *gated_by, left, rows)
    gated, squares = final(mine, *operands, incoming)
    shared, _ = lax.optimization_barrier((shared, squares))
    gated_next, squares_next = final(1 - mine, *operands, shared)
    squares = summed_over(jnp.concatenate([squares, squares_next]), "head")
    return normed(
        mine, [gated, gated_next], squares, norm_gain[None, :],
        channels * lax.axis_size("head"),
    )


def solution(mesh):
    in_specs = (
        P("groups", "ctx", "head"),
        P("groups", "ctx", "head"),
        P(None, "groups", "head", "ctx"),
        P("groups", "head", "ctx"),
        P("groups", "head", "ctx"),
        P("head"),
        P("head"),
    )
    out_specs = P("groups", "ctx", "head")
    return jax.shard_map(body, mesh=mesh, in_specs=in_specs, out_specs=out_specs, check_vma=False)
```

```python
import functools

import jax
import jax.numpy as jnp
import numpy as np
from jax import lax
from jax.experimental import pallas as pl
from jax.experimental.pallas import tpu as pltpu
from jax.sharding import PartitionSpec as P

SPAN = 128
HALF = 256
F32 = jnp.float32
BF16 = jnp.bfloat16
MIB = 1024 * 1024
PARAMS = pltpu.CompilerParams(vmem_limit_bytes=4 * MIB)
COST = pl.CostEstimate(flops=1000, bytes_accessed=1000, transcendentals=0)
GATES_COST = pl.CostEstimate(flops=10**9, bytes_accessed=12 * 10**6, transcendentals=15 * 10**5)
LEFT_COST = pl.CostEstimate(flops=5 * 10**7, bytes_accessed=16 * 10**5, transcendentals=0)
STAGING_PARAMS = pltpu.CompilerParams(vmem_limit_bytes=10 * MIB)
ENTER, LEAVE, FIRST, TOTAL = range(4)
ROWS = 32
WHOLE = pl.BlockSpec(memory_space=pltpu.VMEM)
ANYWHERE = pl.BlockSpec(memory_space=pl.ANY)


def in_vmem(array):
    return pltpu.with_memory_space_constraint(array, pltpu.VMEM)


def in_hbm(array):
    return pltpu.with_memory_space_constraint(array, pltpu.HBM)


def mm(a, b):
    return jnp.dot(a, b, preferred_element_type=F32)


def mm_nt(a, b):
    return lax.dot_general(a, b, (((1,), (1,)), ((), ())), preferred_element_type=F32)


def iotas(shape):
    return (
        lax.broadcasted_iota(jnp.int32, shape, 0),
        lax.broadcasted_iota(jnp.int32, shape, 1),
    )


def two_parts(v):
    high = v.astype(BF16)
    return [high, (v - high.astype(F32)).astype(BF16)]


def fill_tables(step_ref, decay_ref, skip_ref, sums_ref, rise_band, both_ref, rows_ref):
    seqs, heads, length = decay_ref.shape
    blocks = length // SPAN
    _, lane = iotas((SPAN, 4 * heads))
    rising = lane < 2 * heads
    is_high = (lane < heads) | ((lane >= 2 * heads) & (lane < 3 * heads))
    until = sums_ref[:SPAN]
    same = sums_ref[SPAN:]

    def parts_of(v):
        high = v.astype(BF16).astype(F32)
        return jnp.where(is_high[:v.shape[0]], high, v - high).astype(BF16)

    skip = jnp.concatenate([skip_ref[...]] * 4, axis=1)
    for s in range(seqs):
        decays = two_parts(jnp.concatenate([decay_ref[s]] * 4, axis=0))
        steps = two_parts(jnp.concatenate([step_ref[s]] * 4, axis=0))
        enter, leave, first = [], [], []
        before = jnp.zeros((1, 4 * heads), F32)
        for k in range(blocks):
            sl = slice(k * SPAN, (k + 1) * SPAN)
            summed = mm_nt(until, jnp.concatenate([p[:, sl] for p in decays], axis=1))
            step = mm_nt(same, jnp.concatenate([p[:, sl] for p in steps], axis=1))
            middle = summed[SPAN // 2 - 1:SPAN // 2]
            last = summed[SPAN - 1:]
            above = summed - middle
            factor = jnp.exp(jnp.where(rising, above, -above))
            both_ref[s, sl, :] = parts_of(jnp.where(rising, factor, step * factor))
            enter.append(jnp.exp(middle))
            leave.append(jnp.exp(last - middle))
            first.append(jnp.exp(middle + before))
            before = before + last
        table = enter + leave + first + [jnp.exp(before)]
        table = table + [jnp.zeros_like(before)] * (ROWS - 1 - len(table)) + [skip]
        rows_ref[s] = mm(parts_of(jnp.concatenate(table, axis=0)), rise_band)


def front_kernel(
    x_hbm, step_hbm, decay_hbm, skip_hbm, sums_hbm, bands_hbm,
    x_ref, weighted_ref, both_ref, rows_ref, bands, step, decay, skip, sums, sems,
):
    seqs, length, channels = x_ref.shape
    heads = decay.shape[1]
    pairs = [
        (decay_hbm, decay), (step_hbm, step), (sums_hbm, sums), (skip_hbm, skip), (bands_hbm, bands)
    ]
    small = len(pairs)
    pairs += [(x_hbm.at[s], x_ref.at[s]) for s in range(seqs)]
    copies = [
        pltpu.make_async_copy(source, target, sems.at[i])
        for i, (source, target) in enumerate(pairs)
    ]
    for copy in copies:
        copy.start()
    for copy in copies[:small]:
        copy.wait()
    fill_tables(step, decay, skip, sums, bands[2 * heads:], both_ref, rows_ref)
    for s in range(seqs):
        copies[small + s].wait()
        for k in range(length // SPAN):
            rows = slice(k * SPAN, (k + 1) * SPAN)
            both = both_ref[s, rows]
            for lo in range(0, channels, HALF):
                sl = slice(lo, lo + HALF)
                wide = mm(both, bands[:4 * heads, sl]).astype(BF16)
                weighted_ref[s, rows, sl] = x_ref[s, rows, sl] * wide


def front(features, step_size, log_decay, skip, sums, bands):
    seqs, length, channels = features.shape
    heads = step_size.shape[1]
    operands = [features, step_size, log_decay, skip, sums, bands]
    return pl.pallas_call(
        front_kernel,
        in_specs=[ANYWHERE] * 6,
        out_specs=[WHOLE] * 5,
        out_shape=[
            pltpu.VMEM(features.shape, BF16),
            pltpu.VMEM(features.shape, BF16),
            pltpu.VMEM((seqs, length, 4 * heads), BF16),
            pltpu.VMEM((seqs, ROWS, channels), F32),
            pltpu.VMEM(bands.shape, BF16),
        ],
        scratch_shapes=[
            pltpu.VMEM(step_size.shape, F32),
            pltpu.VMEM(log_decay.shape, F32),
            pltpu.VMEM(skip.shape, F32),
            pltpu.VMEM(sums.shape, BF16),
            pltpu.SemaphoreType.DMA((seqs + 5,)),
        ],
        compiler_params=PARAMS,
        cost_estimate=COST,
        name="front",
    )(*[in_hbm(operand) for operand in operands])


def state_kernel(b_ref, weighted_ref, rows_ref, entering_ref, state_ref):
    seqs, length, channels = weighted_ref.shape
    blocks = length // SPAN
    for s in range(seqs):
        for lo in range(0, channels, HALF):
            sl = slice(lo, lo + HALF)
            state = None
            for k in range(blocks):
                rows = slice(k * SPAN, (k + 1) * SPAN)
                added = mm(b_ref[s, :, rows], weighted_ref[s, rows, sl])
                if k > 0:
                    at = ENTER * blocks + k
                    entering = rows_ref[s, at:at + 1, sl] * state
                    entering_ref[s, k - 1, :, sl] = entering.astype(BF16)
                    added = added + entering
                at = LEAVE * blocks + k
                state = rows_ref[s, at:at + 1, sl] * added
            state_ref[s, :, sl] = state.astype(BF16)


def own_states(b, weighted, rows):
    seqs, states, length = b.shape
    channels = weighted.shape[2]
    return pl.pallas_call(
        state_kernel,
        in_specs=[WHOLE] * 3,
        out_specs=[WHOLE] * 2,
        out_shape=[
            pltpu.VMEM((seqs, length // SPAN - 1, states, channels), BF16),
            pltpu.VMEM((seqs, states, channels), BF16),
        ],
        compiler_params=PARAMS,
        cost_estimate=COST,
        name="own_states",
    )(b, in_vmem(weighted), in_vmem(rows))


def gate_kernel(seq_ref, gate_ref, x_ref, both_ref, bands_ref, rows_ref, lift_ref, skipped_ref):
    length, channels = lift_ref.shape
    heads4 = both_ref.shape[2]
    band = slice(heads4 // 2, heads4 // 2 + heads4)
    seq = seq_ref[0]
    for k in range(length // SPAN):
        rows = slice(k * SPAN, (k + 1) * SPAN)
        both = both_ref[seq, rows]
        for lo in range(0, channels, HALF):
            sl = slice(lo, lo + HALF)
            half = 0.5 * gate_ref[seq, rows, sl].astype(F32)
            gate = (half * jnp.tanh(half) + half).astype(BF16)
            lift_ref[rows, sl] = mm(both, bands_ref[band, sl]).astype(BF16) * gate
            skip = rows_ref[seq, ROWS - 1:ROWS, sl].astype(BF16) * x_ref[seq, rows, sl]
            skipped_ref[rows, sl] = skip * gate


def gates(seq, gate_in, x, both, bands, rows):
    _, length, channels = gate_in.shape
    return pl.pallas_call(
        gate_kernel,
        in_specs=[pl.BlockSpec(memory_space=pltpu.SMEM)] + [WHOLE] * 5,
        out_specs=[WHOLE, WHOLE],
        out_shape=[pltpu.VMEM((length, channels), BF16)] * 2,
        compiler_params=PARAMS,
        cost_estimate=GATES_COST,
        name="gates",
    )(seq, in_vmem(gate_in), in_vmem(x), in_vmem(both), in_vmem(bands), in_vmem(rows))


def left_kernel(b_ref, c_ref, left_ref):
    seqs, states, length = b_ref.shape
    row, col = iotas((SPAN, SPAN))
    for s in range(seqs):
        for k in range(length // SPAN):
            rows = slice(k * SPAN, (k + 1) * SPAN)
            c_t = c_ref[s, :, rows].T
            affinity = mm(c_t, b_ref[s, :, rows])
            left_ref[s, rows, :SPAN] = jnp.where(row >= col, affinity, 0.0).astype(BF16)
            left_ref[s, rows, SPAN:] = c_t


def left_of(b, c):
    seqs, states, length = b.shape
    return pl.pallas_call(
        left_kernel,
        in_specs=[WHOLE] * 2,
        out_specs=WHOLE,
        out_shape=pltpu.VMEM((seqs, length, SPAN + states), BF16),
        compiler_params=PARAMS,
        cost_estimate=LEFT_COST,
        name="left",
    )(b, c)


def final_kernel(
    seq_ref, weighted_ref, near_ref, far_ref, left_ref, rows_ref, lift_ref, skipped_ref,
    incoming_ref, gated_ref, square_ref,
):
    length, channels = gated_ref.shape
    blocks = length // SPAN
    s = seq_ref[0]
    for k in range(blocks):
        rows = slice(k * SPAN, (k + 1) * SPAN)
        left = left_ref[s, rows]
        squares = jnp.zeros((SPAN, 128), F32)
        at = FIRST * blocks + k
        for lo in range(0, channels, HALF):
            sl = slice(lo, lo + HALF)
            entering = rows_ref[s, at:at + 1, sl].astype(BF16) * incoming_ref[:, sl]
            if k > 0:
                entering = entering + jnp.concatenate(
                    [near_ref[s, k - 1, :, sl], far_ref[s, k - 1, :, sl]], axis=0
                )
            right = jnp.concatenate([weighted_ref[s, rows, sl], entering], axis=0)
            mixed = mm(left, right).astype(BF16)
            gated = lift_ref[rows, sl] * mixed + skipped_ref[rows, sl]
            gated_ref[rows, sl] = gated
            power = gated * gated
            pair = sum(power[:, half:half + 128] for half in range(0, HALF, 128))
            squares = squares + pair.astype(F32)
        square_ref[k:k + 1] = jnp.sum(squares.T, axis=0, keepdims=True)
    unused = square_ref.shape[0] - blocks
    if unused:
        square_ref[blocks:] = jnp.zeros((unused, SPAN), F32)


def final(seq, weighted, near, far, left, rows, lift, skipped, incoming):
    length, channels = lift.shape
    return pl.pallas_call(
        final_kernel,
        in_specs=[pl.BlockSpec(memory_space=pltpu.SMEM)] + [WHOLE] * 8,
        out_specs=[WHOLE] * 2,
        out_shape=[
            pltpu.VMEM((length, channels), BF16),
            pltpu.VMEM((-(-length // SPAN // 8) * 8, SPAN), F32),
        ],
        compiler_params=PARAMS,
        cost_estimate=COST,
        name="final",
    )(
        seq, in_vmem(weighted), in_vmem(near), in_vmem(far), in_vmem(left), in_vmem(rows),
        in_vmem(lift), in_vmem(skipped), incoming,
    )


def norm_kernel(all_channels, seq_ref, square_ref, gain_ref, *refs):
    gated_refs, (out_hbm, staged, sems) = refs[:-3], refs[-3:]
    length, channels = gated_refs[0].shape
    blocks = length // SPAN
    stride = square_ref.shape[0] // len(gated_refs)
    copies = []
    for number, gated_ref in enumerate(gated_refs):
        s = lax.rem(seq_ref[0] + number, len(gated_refs))
        for k in range(blocks):
            rows = slice(k * SPAN, (k + 1) * SPAN)
            at = number * stride + k
            inverse = lax.rsqrt(square_ref[at:at + 1] / all_channels + 1e-05)
            column = jnp.broadcast_to(inverse, (128, SPAN)).T
            for lo in range(0, channels, 128):
                sl = slice(lo, lo + 128)
                staged[number, rows, sl] = (
                    gated_ref[rows, sl].astype(F32) * column * gain_ref[:, sl]
                ).astype(BF16)
            place = pl.ds(k * SPAN, SPAN)
            copies.append(
                pltpu.make_async_copy(
                    staged.at[number, place], out_hbm.at[s, place], sems.at[number * blocks + k]
                )
            )
            copies[-1].start(priority=k % 2)
    for copy in copies:
        copy.wait()


def normed(first, gated, squares, gain_row, all_channels):
    seqs = len(gated)
    length, channels = gated[0].shape
    return pl.pallas_call(
        functools.partial(norm_kernel, all_channels),
        in_specs=[pl.BlockSpec(memory_space=pltpu.SMEM)] + [WHOLE] * (2 + seqs),
        out_specs=ANYWHERE,
        out_shape=jax.ShapeDtypeStruct((seqs, length, channels), BF16),
        scratch_shapes=[
            pltpu.VMEM((seqs, length, channels), BF16),
            pltpu.SemaphoreType.DMA((seqs * (length // SPAN),)),
        ],
        compiler_params=STAGING_PARAMS,
        cost_estimate=COST,
        name="normed",
    )(first, squares, gain_row, *[in_vmem(one) for one in gated])


def from_all(shard, axis):
    devices = lax.axis_size(axis)
    paired = devices & (devices - 1) == 0
    return [shard] + [
        lax.ppermute(
            shard, axis, [(i, i ^ by if paired else (i + by) % devices) for i in range(devices)]
        )
        for by in range(1, devices)
    ]


def as_parts(row):
    high = row.astype(BF16)
    low = (row - high.astype(F32)).astype(BF16)
    return jnp.concatenate([high, low, jnp.zeros((14, row.shape[1]), BF16)], axis=0)


def body(features, gate_in, state_proj, step_size, log_decay, skip_gain, norm_gain):
    seqs, length, channels = features.shape
    heads = step_size.shape[1]
    pair = np.repeat(np.concatenate([np.eye(heads)] * 2), channels // heads, axis=1)
    bands = jnp.asarray(np.concatenate([0 * pair, pair, 0 * pair]), BF16)
    until = np.tril(np.ones((SPAN, SPAN)))
    sums = jnp.asarray(np.concatenate([np.tile(until, 2), np.tile(np.eye(SPAN), 2)]), BF16)
    b_own, c_own = lax.optimization_barrier((state_proj[0], state_proj[1]))
    b_pieces = from_all(b_own, "head")
    x, weighted, both, rows, bands = front(
        features, step_size, log_decay, skip_gain[None, :], sums, bands
    )

    place = lax.axis_index("ctx")
    even = place % 2 == 0
    mine = (place % 2).astype(jnp.int32)[None]
    devices = lax.axis_size("ctx")
    swap = [(i, i ^ 1) for i in range(devices)]
    total_at = TOTAL * (length // SPAN)
    decays = [rows[s, total_at:total_at + 1] for s in range(seqs)]
    decay = jnp.where(even, decays[0], decays[1])

    def past_chip(end, other, decay_other):
        return jnp.where(even, other + decay_other * end, end + decay * other)

    def across(past, entered, hop):
        sent = past if entered is None else past + decay_past * entered.astype(F32)
        sent = sent.astype(BF16)
        return sent, lax.ppermute(sent, "ctx", [(hop, hop + 2), (hop + 1, hop + 3)])

    b_near = jnp.concatenate(b_pieces[:2], axis=1)
    near, near_ends = own_states(b_near, weighted, rows)
    near_rows = b_near.shape[1]
    other = lax.ppermute(
        jnp.concatenate([
            jnp.where(even, near_ends[1], near_ends[0]),
            as_parts(jnp.where(even, decays[1], decays[0])),
        ]),
        "ctx", swap,
    )
    near_other = other[:near_rows].astype(F32)
    decay_other = (
        other[near_rows:near_rows + 1].astype(F32) + other[near_rows + 1:near_rows + 2].astype(F32)
    )
    decay_past = decay_other * decay
    near_end = jnp.where(even, near_ends[0], near_ends[1]).astype(F32)
    near_past = past_chip(near_end, near_other, decay_other)
    near_sent, near_got = across(near_past, None, 0)
    b_far, _ = lax.optimization_barrier((b_pieces[2:], near_sent))
    b_far = jnp.concatenate(b_far, axis=1)
    far, far_ends = own_states(b_far, weighted, rows)
    far_other = lax.ppermute(jnp.where(even, far_ends[1], far_ends[0]), "ctx", swap).astype(F32)
    far_end = jnp.where(even, far_ends[0], far_ends[1]).astype(F32)
    far_past = past_chip(far_end, far_other, decay_other)
    far_sent, far_got = across(far_past, None, 0)
    c_own, _ = lax.optimization_barrier((c_own, near_ends))
    c = from_all(c_own, "head")
    x, _ = lax.optimization_barrier((x, far_sent))
    lifts = gates(mine, gate_in, x, both, bands, rows)
    x, lifts, c = lax.optimization_barrier((x, lifts, c))
    lifts_next = gates(1 - mine, gate_in, x, both, bands, rows)
    left = left_of(jnp.concatenate([b_near, b_far], axis=1), jnp.concatenate(c, axis=1))
    left, lifts_next = lax.optimization_barrier((left, lifts_next))
    near_got, far_got, left = lax.optimization_barrier((near_got, far_got, left))
    for hop in range(2, devices - 2, 2):
        near_got = near_got + across(near_past, near_got, hop)[1]
        far_got = far_got + across(far_past, far_got, hop)[1]
    entered = jnp.concatenate([near_got, far_got])
    entered32 = entered.astype(F32)
    end = jnp.concatenate([near_end, far_end])
    end_other = jnp.concatenate([near_other, far_other])
    shared = lax.ppermute(
        jnp.where(even, end + decay * entered32, entered32).astype(BF16), "ctx", swap
    )
    incoming = jnp.where(even, entered32, end_other + decay_other * entered32).astype(BF16)
    operands = (weighted, near, far, left, rows)
    gated, squares = final(mine, *operands, *lifts, incoming)
    shared, _ = lax.optimization_barrier((shared, squares))
    gated_next, squares_next = final(1 - mine, *operands, *lifts_next, shared)
    squares = sum(from_all(jnp.concatenate([squares, squares_next]), "head"))
    return normed(
        mine, [gated, gated_next], squares, norm_gain[None, :],
        channels * lax.axis_size("head"),
    )


def solution(mesh):
    in_specs = (
        P("groups", "ctx", "head"),
        P("groups", "ctx", "head"),
        P(None, "groups", "head", "ctx"),
        P("groups", "head", "ctx"),
        P("groups", "head", "ctx"),
        P("head"),
        P("head"),
    )
    out_specs = P("groups", "ctx", "head")
    return jax.shard_map(body, mesh=mesh, in_specs=in_specs, out_specs=out_specs, check_vma=False)
```

```python
import functools

import jax
import jax.numpy as jnp
import numpy as np
from jax import lax
from jax.experimental import pallas as pl
from jax.experimental.pallas import tpu as pltpu
from jax.sharding import PartitionSpec as P

SPAN = 128
HALF = 256
F32 = jnp.float32
BF16 = jnp.bfloat16
MIB = 1024 * 1024
PARAMS = pltpu.CompilerParams(vmem_limit_bytes=4 * MIB)
COST = pl.CostEstimate(flops=1000, bytes_accessed=1000, transcendentals=0)
GATES_COST = pl.CostEstimate(flops=10**9, bytes_accessed=12 * 10**6, transcendentals=15 * 10**5)
LEFT_COST = pl.CostEstimate(flops=5 * 10**7, bytes_accessed=16 * 10**5, transcendentals=0)
STAGING_PARAMS = pltpu.CompilerParams(vmem_limit_bytes=10 * MIB)
ENTER, LEAVE, FIRST, TOTAL = range(4)
ROWS = 32
WHOLE = pl.BlockSpec(memory_space=pltpu.VMEM)
ANYWHERE = pl.BlockSpec(memory_space=pl.ANY)


def in_vmem(array):
    return pltpu.with_memory_space_constraint(array, pltpu.VMEM)


def in_hbm(array):
    return pltpu.with_memory_space_constraint(array, pltpu.HBM)


def mm(a, b):
    return jnp.dot(a, b, preferred_element_type=F32)


def mm_nt(a, b):
    return lax.dot_general(a, b, (((1,), (1,)), ((), ())), preferred_element_type=F32)


def iotas(shape):
    return (
        lax.broadcasted_iota(jnp.int32, shape, 0),
        lax.broadcasted_iota(jnp.int32, shape, 1),
    )


def two_parts(v):
    high = v.astype(BF16)
    return [high, (v - high.astype(F32)).astype(BF16)]


def fill_tables(step_ref, decay_ref, skip_ref, sums_ref, rise_band, both_ref, rows_ref):
    seqs, heads, length = decay_ref.shape
    blocks = length // SPAN
    _, lane = iotas((SPAN, 4 * heads))
    rising = lane < 2 * heads
    is_high = (lane < heads) | ((lane >= 2 * heads) & (lane < 3 * heads))
    until = sums_ref[:SPAN]
    same = sums_ref[SPAN:]

    def parts_of(v):
        high = v.astype(BF16).astype(F32)
        return jnp.where(is_high[:v.shape[0]], high, v - high).astype(BF16)

    skip = jnp.concatenate([skip_ref[...]] * 4, axis=1)
    for s in range(seqs):
        decays = two_parts(jnp.concatenate([decay_ref[s]] * 4, axis=0))
        steps = two_parts(jnp.concatenate([step_ref[s]] * 4, axis=0))
        enter, leave, first = [], [], []
        before = jnp.zeros((1, 4 * heads), F32)
        for k in range(blocks):
            sl = slice(k * SPAN, (k + 1) * SPAN)
            summed = mm_nt(until, jnp.concatenate([p[:, sl] for p in decays], axis=1))
            step = mm_nt(same, jnp.concatenate([p[:, sl] for p in steps], axis=1))
            middle = summed[SPAN // 2 - 1:SPAN // 2]
            last = summed[SPAN - 1:]
            above = summed - middle
            factor = jnp.exp(jnp.where(rising, above, -above))
            both_ref[s, sl, :] = parts_of(jnp.where(rising, factor, step * factor))
            enter.append(jnp.exp(middle))
            leave.append(jnp.exp(last - middle))
            first.append(jnp.exp(middle + before))
            before = before + last
        table = enter + leave + first + [jnp.exp(before)]
        table = table + [jnp.zeros_like(before)] * (ROWS - 1 - len(table)) + [skip]
        rows_ref[s] = mm(parts_of(jnp.concatenate(table, axis=0)), rise_band)


def front_kernel(
    x_hbm, step_hbm, decay_hbm, skip_hbm, sums_hbm, bands_hbm,
    x_ref, weighted_ref, both_ref, rows_ref, bands, step, decay, skip, sums, sems,
):
    seqs, length, channels = x_ref.shape
    heads = decay.shape[1]
    pairs = [
        (decay_hbm, decay), (step_hbm, step), (sums_hbm, sums), (skip_hbm, skip), (bands_hbm, bands)
    ]
    small = len(pairs)
    pairs += [(x_hbm.at[s], x_ref.at[s]) for s in range(seqs)]
    copies = [
        pltpu.make_async_copy(source, target, sems.at[i])
        for i, (source, target) in enumerate(pairs)
    ]
    for copy in copies:
        copy.start()
    for copy in copies[:small]:
        copy.wait()
    fill_tables(step, decay, skip, sums, bands[2 * heads:], both_ref, rows_ref)
    for s in range(seqs):
        copies[small + s].wait()
        for k in range(length // SPAN):
            rows = slice(k * SPAN, (k + 1) * SPAN)
            both = both_ref[s, rows]
            for lo in range(0, channels, HALF):
                sl = slice(lo, lo + HALF)
                wide = mm(both, bands[:4 * heads, sl]).astype(BF16)
                weighted_ref[s, rows, sl] = x_ref[s, rows, sl] * wide


def front(features, step_size, log_decay, skip, sums, bands):
    seqs, length, channels = features.shape
    heads = step_size.shape[1]
    operands = [features, step_size, log_decay, skip, sums, bands]
    return pl.pallas_call(
        front_kernel,
        in_specs=[ANYWHERE] * 6,
        out_specs=[WHOLE] * 5,
        out_shape=[
            pltpu.VMEM(features.shape, BF16),
            pltpu.VMEM(features.shape, BF16),
            pltpu.VMEM((seqs, length, 4 * heads), BF16),
            pltpu.VMEM((seqs, ROWS, channels), F32),
            pltpu.VMEM(bands.shape, BF16),
        ],
        scratch_shapes=[
            pltpu.VMEM(step_size.shape, F32),
            pltpu.VMEM(log_decay.shape, F32),
            pltpu.VMEM(skip.shape, F32),
            pltpu.VMEM(sums.shape, BF16),
            pltpu.SemaphoreType.DMA((seqs + 5,)),
        ],
        compiler_params=PARAMS,
        cost_estimate=COST,
        name="front",
    )(*[in_hbm(operand) for operand in operands])


def state_kernel(b_ref, weighted_ref, rows_ref, entering_ref, state_ref):
    seqs, length, channels = weighted_ref.shape
    blocks = length // SPAN
    for s in range(seqs):
        for lo in range(0, channels, HALF):
            sl = slice(lo, lo + HALF)
            state = None
            for k in range(blocks):
                rows = slice(k * SPAN, (k + 1) * SPAN)
                added = mm(b_ref[s, :, rows], weighted_ref[s, rows, sl])
                if k > 0:
                    at = ENTER * blocks + k
                    entering = rows_ref[s, at:at + 1, sl] * state
                    entering_ref[s, k - 1, :, sl] = entering.astype(BF16)
                    added = added + entering
                at = LEAVE * blocks + k
                state = rows_ref[s, at:at + 1, sl] * added
            state_ref[s, :, sl] = state.astype(BF16)


def own_states(b, weighted, rows):
    seqs, states, length = b.shape
    channels = weighted.shape[2]
    return pl.pallas_call(
        state_kernel,
        in_specs=[WHOLE] * 3,
        out_specs=[WHOLE] * 2,
        out_shape=[
            pltpu.VMEM((seqs, length // SPAN - 1, states, channels), BF16),
            pltpu.VMEM((seqs, states, channels), BF16),
        ],
        compiler_params=PARAMS,
        cost_estimate=COST,
        name="own_states",
    )(b, in_vmem(weighted), in_vmem(rows))


def gate_kernel(seq_ref, gate_ref, x_ref, both_ref, bands_ref, rows_ref, lift_ref, skipped_ref):
    length, channels = lift_ref.shape
    heads4 = both_ref.shape[2]
    band = slice(heads4 // 2, heads4 // 2 + heads4)
    seq = seq_ref[0]
    for k in range(length // SPAN):
        rows = slice(k * SPAN, (k + 1) * SPAN)
        both = both_ref[seq, rows]
        for lo in range(0, channels, HALF):
            sl = slice(lo, lo + HALF)
            half = 0.5 * gate_ref[seq, rows, sl].astype(F32)
            gate = (half * jnp.tanh(half) + half).astype(BF16)
            lift_ref[rows, sl] = mm(both, bands_ref[band, sl]).astype(BF16) * gate
            skip = rows_ref[seq, ROWS - 1:ROWS, sl].astype(BF16) * x_ref[seq, rows, sl]
            skipped_ref[rows, sl] = skip * gate


def gates(seq, gate_in, x, both, bands, rows):
    _, length, channels = gate_in.shape
    return pl.pallas_call(
        gate_kernel,
        in_specs=[pl.BlockSpec(memory_space=pltpu.SMEM)] + [WHOLE] * 5,
        out_specs=[WHOLE, WHOLE],
        out_shape=[pltpu.VMEM((length, channels), BF16)] * 2,
        compiler_params=PARAMS,
        cost_estimate=GATES_COST,
        name="gates",
    )(seq, in_vmem(gate_in), in_vmem(x), in_vmem(both), in_vmem(bands), in_vmem(rows))


def left_kernel(b_ref, c_ref, left_ref):
    seqs, states, length = b_ref.shape
    row, col = iotas((SPAN, SPAN))
    for s in range(seqs):
        for k in range(length // SPAN):
            rows = slice(k * SPAN, (k + 1) * SPAN)
            c_t = c_ref[s, :, rows].T
            affinity = mm(c_t, b_ref[s, :, rows])
            left_ref[s, rows, :SPAN] = jnp.where(row >= col, affinity, 0.0).astype(BF16)
            left_ref[s, rows, SPAN:] = c_t


def left_of(b, c):
    seqs, states, length = b.shape
    return pl.pallas_call(
        left_kernel,
        in_specs=[WHOLE] * 2,
        out_specs=WHOLE,
        out_shape=pltpu.VMEM((seqs, length, SPAN + states), BF16),
        compiler_params=PARAMS,
        cost_estimate=LEFT_COST,
        name="left",
    )(b, c)


def final_kernel(
    seq_ref, weighted_ref, near_ref, far_ref, left_ref, rows_ref, lift_ref, skipped_ref,
    incoming_ref, gated_ref, square_ref,
):
    length, channels = gated_ref.shape
    blocks = length // SPAN
    s = seq_ref[0]
    for k in range(blocks):
        rows = slice(k * SPAN, (k + 1) * SPAN)
        left = left_ref[s, rows]
        squares = jnp.zeros((SPAN, 128), F32)
        at = FIRST * blocks + k
        for lo in range(0, channels, HALF):
            sl = slice(lo, lo + HALF)
            entering = rows_ref[s, at:at + 1, sl].astype(BF16) * incoming_ref[:, sl]
            if k > 0:
                entering = entering + jnp.concatenate(
                    [near_ref[s, k - 1, :, sl], far_ref[s, k - 1, :, sl]], axis=0
                )
            right = jnp.concatenate([weighted_ref[s, rows, sl], entering], axis=0)
            mixed = mm(left, right).astype(BF16)
            gated = lift_ref[rows, sl] * mixed + skipped_ref[rows, sl]
            gated_ref[rows, sl] = gated
            power = gated * gated
            pair = sum(power[:, half:half + 128] for half in range(0, HALF, 128))
            squares = squares + pair.astype(F32)
        square_ref[k:k + 1] = jnp.sum(squares.T, axis=0, keepdims=True)
    unused = square_ref.shape[0] - blocks
    if unused:
        square_ref[blocks:] = jnp.zeros((unused, SPAN), F32)


def final(seq, weighted, near, far, left, rows, lift, skipped, incoming):
    length, channels = lift.shape
    return pl.pallas_call(
        final_kernel,
        in_specs=[pl.BlockSpec(memory_space=pltpu.SMEM)] + [WHOLE] * 8,
        out_specs=[WHOLE] * 2,
        out_shape=[
            pltpu.VMEM((length, channels), BF16),
            pltpu.VMEM((-(-length // SPAN // 8) * 8, SPAN), F32),
        ],
        compiler_params=PARAMS,
        cost_estimate=COST,
        name="final",
    )(
        seq, in_vmem(weighted), in_vmem(near), in_vmem(far), in_vmem(left), in_vmem(rows),
        in_vmem(lift), in_vmem(skipped), incoming,
    )


def norm_kernel(all_channels, seq_ref, square_ref, gain_ref, *refs):
    gated_refs, (out_hbm, staged, sems) = refs[:-3], refs[-3:]
    length, channels = gated_refs[0].shape
    blocks = length // SPAN
    stride = square_ref.shape[0] // len(gated_refs)
    copies = []
    for number, gated_ref in enumerate(gated_refs):
        s = lax.rem(seq_ref[0] + number, len(gated_refs))
        for k in range(blocks):
            rows = slice(k * SPAN, (k + 1) * SPAN)
            at = number * stride + k
            inverse = lax.rsqrt(square_ref[at:at + 1] / all_channels + 1e-05)
            column = jnp.broadcast_to(inverse, (128, SPAN)).T
            for lo in range(0, channels, 128):
                sl = slice(lo, lo + 128)
                staged[number, rows, sl] = (
                    gated_ref[rows, sl].astype(F32) * column * gain_ref[:, sl]
                ).astype(BF16)
            place = pl.ds(k * SPAN, SPAN)
            copies.append(
                pltpu.make_async_copy(
                    staged.at[number, place], out_hbm.at[s, place], sems.at[number * blocks + k]
                )
            )
            copies[-1].start(priority=k % 2)
    for copy in copies:
        copy.wait()


def normed(first, gated, squares, gain_row, all_channels):
    seqs = len(gated)
    length, channels = gated[0].shape
    return pl.pallas_call(
        functools.partial(norm_kernel, all_channels),
        in_specs=[pl.BlockSpec(memory_space=pltpu.SMEM)] + [WHOLE] * (2 + seqs),
        out_specs=ANYWHERE,
        out_shape=jax.ShapeDtypeStruct((seqs, length, channels), BF16),
        scratch_shapes=[
            pltpu.VMEM((seqs, length, channels), BF16),
            pltpu.SemaphoreType.DMA((seqs * (length // SPAN),)),
        ],
        compiler_params=STAGING_PARAMS,
        cost_estimate=COST,
        name="normed",
    )(first, squares, gain_row, *[in_vmem(one) for one in gated])


def from_partner(shard, axis, by):
    devices = lax.axis_size(axis)
    paired = devices & (devices - 1) == 0
    return lax.ppermute(
        shard, axis, [(i, i ^ by if paired else (i + by) % devices) for i in range(devices)]
    )


def from_all(shard, axis):
    return [shard] + [from_partner(shard, axis, by) for by in range(1, lax.axis_size(axis))]


def as_parts(row):
    high = row.astype(BF16)
    low = (row - high.astype(F32)).astype(BF16)
    return jnp.concatenate([high, low, jnp.zeros((14, row.shape[1]), BF16)], axis=0)


def body(features, gate_in, state_proj, step_size, log_decay, skip_gain, norm_gain):
    seqs, length, channels = features.shape
    heads = step_size.shape[1]
    pair = np.repeat(np.concatenate([np.eye(heads)] * 2), channels // heads, axis=1)
    bands = jnp.asarray(np.concatenate([0 * pair, pair, 0 * pair]), BF16)
    until = np.tril(np.ones((SPAN, SPAN)))
    sums = jnp.asarray(np.concatenate([np.tile(until, 2), np.tile(np.eye(SPAN), 2)]), BF16)
    b_own, c_own = lax.optimization_barrier((state_proj[0], state_proj[1]))
    b_next = from_partner(b_own, "head", 1)
    x, weighted, both, rows, bands = front(
        features, step_size, log_decay, skip_gain[None, :], sums, bands
    )

    b_own, rows = lax.optimization_barrier((b_own, rows))
    b_far = [from_partner(b_own, "head", by) for by in range(2, lax.axis_size("head"))]

    place = lax.axis_index("ctx")
    even = place % 2 == 0
    mine = (place % 2).astype(jnp.int32)[None]
    devices = lax.axis_size("ctx")
    swap = [(i, i ^ 1) for i in range(devices)]
    total_at = TOTAL * (length // SPAN)
    decays = [rows[s, total_at:total_at + 1] for s in range(seqs)]
    decay = jnp.where(even, decays[0], decays[1])

    def past_chip(end, other, decay_other):
        return jnp.where(even, other + decay_other * end, end + decay * other)

    def across(past, entered, hop):
        sent = past if entered is None else past + decay_past * entered.astype(F32)
        sent = sent.astype(BF16)
        return sent, lax.ppermute(sent, "ctx", [(hop, hop + 2), (hop + 1, hop + 3)])

    b_near = jnp.concatenate([b_own, b_next], axis=1)
    near, near_ends = own_states(b_near, weighted, rows)
    near_rows = b_near.shape[1]
    other = lax.ppermute(
        jnp.concatenate([
            jnp.where(even, near_ends[1], near_ends[0]),
            as_parts(jnp.where(even, decays[1], decays[0])),
        ]),
        "ctx", swap,
    )
    near_other = other[:near_rows].astype(F32)
    decay_other = (
        other[near_rows:near_rows + 1].astype(F32) + other[near_rows + 1:near_rows + 2].astype(F32)
    )
    decay_past = decay_other * decay
    near_end = jnp.where(even, near_ends[0], near_ends[1]).astype(F32)
    near_past = past_chip(near_end, near_other, decay_other)
    near_sent, near_got = across(near_past, None, 0)
    b_far, _ = lax.optimization_barrier((b_far, near_sent))
    b_far = jnp.concatenate(b_far, axis=1)
    far, far_ends = own_states(b_far, weighted, rows)
    far_other = lax.ppermute(jnp.where(even, far_ends[1], far_ends[0]), "ctx", swap).astype(F32)
    far_end = jnp.where(even, far_ends[0], far_ends[1]).astype(F32)
    far_past = past_chip(far_end, far_other, decay_other)
    far_sent, far_got = across(far_past, None, 0)
    c_own, _ = lax.optimization_barrier((c_own, near_sent))
    c = from_all(c_own, "head")
    x, _ = lax.optimization_barrier((x, far_sent))
    lifts = gates(mine, gate_in, x, both, bands, rows)
    x, lifts, c = lax.optimization_barrier((x, lifts, c))
    lifts_next = gates(1 - mine, gate_in, x, both, bands, rows)
    left = left_of(jnp.concatenate([b_near, b_far], axis=1), jnp.concatenate(c, axis=1))
    left, lifts_next = lax.optimization_barrier((left, lifts_next))
    near_got, far_got, left = lax.optimization_barrier((near_got, far_got, left))
    for hop in range(2, devices - 2, 2):
        near_got = near_got + across(near_past, near_got, hop)[1]
        far_got = far_got + across(far_past, far_got, hop)[1]
    entered = jnp.concatenate([near_got, far_got])
    entered32 = entered.astype(F32)
    end = jnp.concatenate([near_end, far_end])
    end_other = jnp.concatenate([near_other, far_other])
    shared = lax.ppermute(
        jnp.where(even, end + decay * entered32, entered32).astype(BF16), "ctx", swap
    )
    incoming = jnp.where(even, entered32, end_other + decay_other * entered32).astype(BF16)
    operands = (weighted, near, far, left, rows)
    gated, squares = final(mine, *operands, *lifts, incoming)
    shared, _ = lax.optimization_barrier((shared, squares))
    gated_next, squares_next = final(1 - mine, *operands, *lifts_next, shared)
    squares = sum(from_all(jnp.concatenate([squares, squares_next]), "head"))
    return normed(
        mine, [gated, gated_next], squares, norm_gain[None, :],
        channels * lax.axis_size("head"),
    )


def solution(mesh):
    in_specs = (
        P("groups", "ctx", "head"),
        P("groups", "ctx", "head"),
        P(None, "groups", "head", "ctx"),
        P("groups", "head", "ctx"),
        P("groups", "head", "ctx"),
        P("head"),
        P("head"),
    )
    out_specs = P("groups", "ctx", "head")
    return jax.shard_map(body, mesh=mesh, in_specs=in_specs, out_specs=out_specs, check_vma=False)
```

```python
import functools

import jax
import jax.numpy as jnp
import numpy as np
from jax import lax
from jax.experimental import pallas as pl
from jax.experimental.pallas import tpu as pltpu
from jax.sharding import PartitionSpec as P

SPAN = 128
HALF = 256
F32 = jnp.float32
BF16 = jnp.bfloat16
MIB = 1024 * 1024
PARAMS = pltpu.CompilerParams(vmem_limit_bytes=4 * MIB)
COST = pl.CostEstimate(flops=1000, bytes_accessed=1000, transcendentals=0)
GATES_COST = pl.CostEstimate(flops=10**9, bytes_accessed=12 * 10**6, transcendentals=15 * 10**5)
LEFT_COST = pl.CostEstimate(flops=5 * 10**7, bytes_accessed=16 * 10**5, transcendentals=0)
STAGING_PARAMS = pltpu.CompilerParams(vmem_limit_bytes=10 * MIB)
ENTER, LEAVE, FIRST, TOTAL = range(4)
ROWS = 32
WHOLE = pl.BlockSpec(memory_space=pltpu.VMEM)
ANYWHERE = pl.BlockSpec(memory_space=pl.ANY)


def in_vmem(array):
    return pltpu.with_memory_space_constraint(array, pltpu.VMEM)


def in_hbm(array):
    return pltpu.with_memory_space_constraint(array, pltpu.HBM)


def mm(a, b):
    return jnp.dot(a, b, preferred_element_type=F32)


def mm_nt(a, b):
    return lax.dot_general(a, b, (((1,), (1,)), ((), ())), preferred_element_type=F32)


def iotas(shape):
    return (
        lax.broadcasted_iota(jnp.int32, shape, 0),
        lax.broadcasted_iota(jnp.int32, shape, 1),
    )


def two_parts(v):
    high = v.astype(BF16)
    return [high, (v - high.astype(F32)).astype(BF16)]


def fill_tables(step_ref, decay_ref, skip_ref, sums_ref, rise_band, both_ref, rows_ref):
    seqs, heads, length = decay_ref.shape
    blocks = length // SPAN
    _, lane = iotas((SPAN, 4 * heads))
    rising = lane < 2 * heads
    is_high = (lane < heads) | ((lane >= 2 * heads) & (lane < 3 * heads))
    until = sums_ref[:SPAN]
    same = sums_ref[SPAN:]

    def parts_of(v):
        high = v.astype(BF16).astype(F32)
        return jnp.where(is_high[:v.shape[0]], high, v - high).astype(BF16)

    skip = jnp.concatenate([skip_ref[...]] * 4, axis=1)
    for s in range(seqs):
        decays = two_parts(jnp.concatenate([decay_ref[s]] * 4, axis=0))
        steps = two_parts(jnp.concatenate([step_ref[s]] * 4, axis=0))
        enter, leave, first = [], [], []
        before = jnp.zeros((1, 4 * heads), F32)
        for k in range(blocks):
            sl = slice(k * SPAN, (k + 1) * SPAN)
            summed = mm_nt(until, jnp.concatenate([p[:, sl] for p in decays], axis=1))
            step = mm_nt(same, jnp.concatenate([p[:, sl] for p in steps], axis=1))
            middle = summed[SPAN // 2 - 1:SPAN // 2]
            last = summed[SPAN - 1:]
            above = summed - middle
            factor = jnp.exp(jnp.where(rising, above, -above))
            both_ref[s, sl, :] = parts_of(jnp.where(rising, factor, step * factor))
            enter.append(jnp.exp(middle))
            leave.append(jnp.exp(last - middle))
            first.append(jnp.exp(middle + before))
            before = before + last
        table = enter + leave + first + [jnp.exp(before)]
        table = table + [jnp.zeros_like(before)] * (ROWS - 1 - len(table)) + [skip]
        rows_ref[s] = mm(parts_of(jnp.concatenate(table, axis=0)), rise_band)


def front_kernel(
    x_hbm, step_hbm, decay_hbm, skip_hbm, sums_hbm, bands_hbm,
    weighted_ref, both_ref, rows_ref, bands, step, decay, skip, sums, sems,
):
    seqs, length, channels = weighted_ref.shape
    heads = decay.shape[1]
    pairs = [
        (decay_hbm, decay), (step_hbm, step), (sums_hbm, sums), (skip_hbm, skip), (bands_hbm, bands)
    ]
    small = len(pairs)
    pairs += [(x_hbm.at[s], weighted_ref.at[s]) for s in range(seqs)]
    copies = [
        pltpu.make_async_copy(source, target, sems.at[i])
        for i, (source, target) in enumerate(pairs)
    ]
    for copy in copies:
        copy.start()
    for copy in copies[:small]:
        copy.wait()
    fill_tables(step, decay, skip, sums, bands[2 * heads:], both_ref, rows_ref)
    for s in range(seqs):
        copies[small + s].wait()
        for k in range(length // SPAN):
            rows = slice(k * SPAN, (k + 1) * SPAN)
            both = both_ref[s, rows]
            for lo in range(0, channels, HALF):
                sl = slice(lo, lo + HALF)
                wide = mm(both, bands[:4 * heads, sl]).astype(BF16)
                weighted_ref[s, rows, sl] = weighted_ref[s, rows, sl] * wide


def front(features, step_size, log_decay, skip, sums, bands):
    seqs, length, channels = features.shape
    heads = step_size.shape[1]
    operands = [features, step_size, log_decay, skip, sums, bands]
    return pl.pallas_call(
        front_kernel,
        in_specs=[ANYWHERE] * 6,
        out_specs=[WHOLE] * 4,
        out_shape=[
            pltpu.VMEM(features.shape, BF16),
            pltpu.VMEM((seqs, length, 4 * heads), BF16),
            pltpu.VMEM((seqs, ROWS, channels), F32),
            pltpu.VMEM(bands.shape, BF16),
        ],
        scratch_shapes=[
            pltpu.VMEM(step_size.shape, F32),
            pltpu.VMEM(log_decay.shape, F32),
            pltpu.VMEM(skip.shape, F32),
            pltpu.VMEM(sums.shape, BF16),
            pltpu.SemaphoreType.DMA((seqs + 5,)),
        ],
        compiler_params=PARAMS,
        cost_estimate=COST,
        name="front",
    )(*[in_hbm(operand) for operand in operands])


def state_kernel(b_ref, weighted_ref, rows_ref, entering_ref, state_ref):
    seqs, length, channels = weighted_ref.shape
    blocks = length // SPAN
    for s in range(seqs):
        for lo in range(0, channels, HALF):
            sl = slice(lo, lo + HALF)
            state = None
            for k in range(blocks):
                rows = slice(k * SPAN, (k + 1) * SPAN)
                added = mm(b_ref[s, :, rows], weighted_ref[s, rows, sl])
                if k > 0:
                    at = ENTER * blocks + k
                    entering = rows_ref[s, at:at + 1, sl] * state
                    entering_ref[s, k - 1, :, sl] = entering.astype(BF16)
                    added = added + entering
                at = LEAVE * blocks + k
                state = rows_ref[s, at:at + 1, sl] * added
            state_ref[s, :, sl] = state.astype(BF16)


def own_states(b, weighted, rows):
    seqs, states, length = b.shape
    channels = weighted.shape[2]
    return pl.pallas_call(
        state_kernel,
        in_specs=[WHOLE] * 3,
        out_specs=[WHOLE] * 2,
        out_shape=[
            pltpu.VMEM((seqs, length // SPAN - 1, states, channels), BF16),
            pltpu.VMEM((seqs, states, channels), BF16),
        ],
        compiler_params=PARAMS,
        cost_estimate=COST,
        name="own_states",
    )(b, in_vmem(weighted), in_vmem(rows))


def gate_kernel(seq_ref, gate_ref, x_ref, both_ref, bands_ref, rows_ref, lift_ref, skipped_ref):
    length, channels = lift_ref.shape
    heads4 = both_ref.shape[2]
    band = slice(heads4 // 2, heads4 // 2 + heads4)
    seq = seq_ref[0]
    for k in range(length // SPAN):
        rows = slice(k * SPAN, (k + 1) * SPAN)
        both = both_ref[seq, rows]
        for lo in range(0, channels, HALF):
            sl = slice(lo, lo + HALF)
            half = 0.5 * gate_ref[seq, rows, sl].astype(F32)
            gate = (half * jnp.tanh(half) + half).astype(BF16)
            lift_ref[rows, sl] = mm(both, bands_ref[band, sl]).astype(BF16) * gate
            skip = rows_ref[seq, ROWS - 1:ROWS, sl].astype(BF16) * x_ref[seq, rows, sl]
            skipped_ref[rows, sl] = skip * gate


def gates(seq, gate_in, x, both, bands, rows):
    _, length, channels = gate_in.shape
    return pl.pallas_call(
        gate_kernel,
        in_specs=[pl.BlockSpec(memory_space=pltpu.SMEM)] + [WHOLE] * 5,
        out_specs=[WHOLE, WHOLE],
        out_shape=[pltpu.VMEM((length, channels), BF16)] * 2,
        compiler_params=PARAMS,
        cost_estimate=GATES_COST,
        name="gates",
    )(seq, in_vmem(gate_in), in_vmem(x), in_vmem(both), in_vmem(bands), in_vmem(rows))


def left_kernel(b_ref, c_ref, left_ref):
    seqs, states, length = b_ref.shape
    row, col = iotas((SPAN, SPAN))
    for s in range(seqs):
        for k in range(length // SPAN):
            rows = slice(k * SPAN, (k + 1) * SPAN)
            c_t = c_ref[s, :, rows].T
            affinity = mm(c_t, b_ref[s, :, rows])
            left_ref[s, rows, :SPAN] = jnp.where(row >= col, affinity, 0.0).astype(BF16)
            left_ref[s, rows, SPAN:] = c_t


def left_of(b, c):
    seqs, states, length = b.shape
    return pl.pallas_call(
        left_kernel,
        in_specs=[WHOLE] * 2,
        out_specs=WHOLE,
        out_shape=pltpu.VMEM((seqs, length, SPAN + states), BF16),
        compiler_params=PARAMS,
        cost_estimate=LEFT_COST,
        name="left",
    )(b, c)


def final_kernel(
    seq_ref, weighted_ref, near_ref, far_ref, left_ref, rows_ref, lift_ref, skipped_ref,
    incoming_ref, gated_ref, square_ref,
):
    length, channels = gated_ref.shape
    blocks = length // SPAN
    s = seq_ref[0]
    for k in range(blocks):
        rows = slice(k * SPAN, (k + 1) * SPAN)
        left = left_ref[s, rows]
        squares = jnp.zeros((SPAN, 128), F32)
        at = FIRST * blocks + k
        for lo in range(0, channels, HALF):
            sl = slice(lo, lo + HALF)
            entering = rows_ref[s, at:at + 1, sl].astype(BF16) * incoming_ref[:, sl]
            if k > 0:
                entering = entering + jnp.concatenate(
                    [near_ref[s, k - 1, :, sl], far_ref[s, k - 1, :, sl]], axis=0
                )
            right = jnp.concatenate([weighted_ref[s, rows, sl], entering], axis=0)
            mixed = mm(left, right).astype(BF16)
            gated = lift_ref[rows, sl] * mixed + skipped_ref[rows, sl]
            gated_ref[rows, sl] = gated
            power = gated * gated
            pair = sum(power[:, half:half + 128] for half in range(0, HALF, 128))
            squares = squares + pair.astype(F32)
        square_ref[k:k + 1] = jnp.sum(squares.T, axis=0, keepdims=True)
    unused = square_ref.shape[0] - blocks
    if unused:
        square_ref[blocks:] = jnp.zeros((unused, SPAN), F32)


def final(seq, weighted, near, far, left, rows, lift, skipped, incoming):
    length, channels = lift.shape
    return pl.pallas_call(
        final_kernel,
        in_specs=[pl.BlockSpec(memory_space=pltpu.SMEM)] + [WHOLE] * 8,
        out_specs=[WHOLE] * 2,
        out_shape=[
            pltpu.VMEM((length, channels), BF16),
            pltpu.VMEM((-(-length // SPAN // 8) * 8, SPAN), F32),
        ],
        compiler_params=PARAMS,
        cost_estimate=COST,
        name="final",
    )(
        seq, in_vmem(weighted), in_vmem(near), in_vmem(far), in_vmem(left), in_vmem(rows),
        in_vmem(lift), in_vmem(skipped), incoming,
    )


def norm_kernel(all_channels, seq_ref, square_ref, gain_ref, *refs):
    gated_refs, (out_hbm, staged, sems) = refs[:-3], refs[-3:]
    length, channels = gated_refs[0].shape
    blocks = length // SPAN
    stride = square_ref.shape[0] // len(gated_refs)
    copies = []
    for number, gated_ref in enumerate(gated_refs):
        s = lax.rem(seq_ref[0] + number, len(gated_refs))
        for k in range(blocks):
            rows = slice(k * SPAN, (k + 1) * SPAN)
            at = number * stride + k
            inverse = lax.rsqrt(square_ref[at:at + 1] / all_channels + 1e-05)
            column = jnp.broadcast_to(inverse, (128, SPAN)).T
            for lo in range(0, channels, 128):
                sl = slice(lo, lo + 128)
                staged[number, rows, sl] = (
                    gated_ref[rows, sl].astype(F32) * column * gain_ref[:, sl]
                ).astype(BF16)
            place = pl.ds(k * SPAN, SPAN)
            copies.append(
                pltpu.make_async_copy(
                    staged.at[number, place], out_hbm.at[s, place], sems.at[number * blocks + k]
                )
            )
            copies[-1].start(priority=k % 2)
    for copy in copies:
        copy.wait()


def normed(first, gated, squares, gain_row, all_channels):
    seqs = len(gated)
    length, channels = gated[0].shape
    return pl.pallas_call(
        functools.partial(norm_kernel, all_channels),
        in_specs=[pl.BlockSpec(memory_space=pltpu.SMEM)] + [WHOLE] * (2 + seqs),
        out_specs=ANYWHERE,
        out_shape=jax.ShapeDtypeStruct((seqs, length, channels), BF16),
        scratch_shapes=[
            pltpu.VMEM((seqs, length, channels), BF16),
            pltpu.SemaphoreType.DMA((seqs * (length // SPAN),)),
        ],
        compiler_params=STAGING_PARAMS,
        cost_estimate=COST,
        name="normed",
    )(first, squares, gain_row, *[in_vmem(one) for one in gated])


def from_partner(shard, axis, by):
    return lax.ppermute(shard, axis, [(i, i ^ by) for i in range(lax.axis_size(axis))])


def doubled(block, axis, by, behind=()):
    other = from_partner(block, axis, by)
    other, _ = lax.optimization_barrier((other, behind))
    return jnp.concatenate([block, other], axis=1)


def from_all(shard, axis):
    return [shard] + [from_partner(shard, axis, by) for by in range(1, lax.axis_size(axis))]


def as_parts(row):
    high = row.astype(BF16)
    low = (row - high.astype(F32)).astype(BF16)
    return jnp.concatenate([high, low, jnp.zeros((14, row.shape[1]), BF16)], axis=0)


def body(features, gate_in, state_proj, step_size, log_decay, skip_gain, norm_gain):
    seqs, length, channels = features.shape
    heads = step_size.shape[1]
    pair = np.repeat(np.concatenate([np.eye(heads)] * 2), channels // heads, axis=1)
    bands = jnp.asarray(np.concatenate([0 * pair, pair, 0 * pair]), BF16)
    until = np.tril(np.ones((SPAN, SPAN)))
    sums = jnp.asarray(np.concatenate([np.tile(until, 2), np.tile(np.eye(SPAN), 2)]), BF16)
    b_own, c_own = lax.optimization_barrier((state_proj[0], state_proj[1]))
    b_near = doubled(b_own, "head", 1)
    c_near = doubled(c_own, "head", 1)
    weighted, both, rows, bands = front(
        features, step_size, log_decay, skip_gain[None, :], sums, bands
    )

    place = lax.axis_index("ctx")
    even = place % 2 == 0
    mine = (place % 2).astype(jnp.int32)[None]
    devices = lax.axis_size("ctx")
    swap = [(i, i ^ 1) for i in range(devices)]
    total_at = TOTAL * (length // SPAN)
    decays = [rows[s, total_at:total_at + 1] for s in range(seqs)]
    decay = jnp.where(even, decays[0], decays[1])

    def past_chip(end, other, decay_other):
        return jnp.where(even, other + decay_other * end, end + decay * other)

    def across(past, entered, hop):
        sent = past if entered is None else past + decay_past * entered.astype(F32)
        sent = sent.astype(BF16)
        return sent, lax.ppermute(sent, "ctx", [(hop, hop + 2), (hop + 1, hop + 3)])

    near, near_ends = own_states(b_near, weighted, rows)
    near_rows = b_near.shape[1]
    other = lax.ppermute(
        jnp.concatenate([
            jnp.where(even, near_ends[1], near_ends[0]),
            as_parts(jnp.where(even, decays[1], decays[0])),
        ]),
        "ctx", swap,
    )
    near_other = other[:near_rows].astype(F32)
    decay_other = (
        other[near_rows:near_rows + 1].astype(F32) + other[near_rows + 1:near_rows + 2].astype(F32)
    )
    decay_past = decay_other * decay
    near_end = jnp.where(even, near_ends[0], near_ends[1]).astype(F32)
    near_past = past_chip(near_end, near_other, decay_other)
    near_sent, near_got = across(near_past, None, 0)
    b = b_near
    for by in (1 << i for i in range(1, (lax.axis_size("head") - 1).bit_length())):
        b = doubled(b, "head", by, near_sent)
    b_far = b[:, near_rows:]
    far, far_ends = own_states(b_far, weighted, rows)
    far_other = lax.ppermute(jnp.where(even, far_ends[1], far_ends[0]), "ctx", swap).astype(F32)
    far_end = jnp.where(even, far_ends[0], far_ends[1]).astype(F32)
    far_past = past_chip(far_end, far_other, decay_other)
    far_sent, far_got = across(far_past, None, 0)
    c, _ = lax.optimization_barrier((c_near, near_sent))
    both, _ = lax.optimization_barrier((both, far_sent))
    lifts = gates(mine, gate_in, features, both, bands, rows)
    for by in (1 << i for i in range(1, (lax.axis_size("head") - 1).bit_length())):
        c = doubled(c, "head", by, lifts)
    both, c = lax.optimization_barrier((both, c))
    lifts_next = gates(1 - mine, gate_in, features, both, bands, rows)
    left = left_of(b, c)
    left, lifts_next = lax.optimization_barrier((left, lifts_next))
    near_got, far_got, left = lax.optimization_barrier((near_got, far_got, left))
    for hop in range(2, devices - 2, 2):
        near_got = near_got + across(near_past, near_got, hop)[1]
        far_got = far_got + across(far_past, far_got, hop)[1]
    entered = jnp.concatenate([near_got, far_got])
    entered32 = entered.astype(F32)
    end = jnp.concatenate([near_end, far_end])
    end_other = jnp.concatenate([near_other, far_other])
    shared = lax.ppermute(
        jnp.where(even, end + decay * entered32, entered32).astype(BF16), "ctx", swap
    )
    incoming = jnp.where(even, entered32, end_other + decay_other * entered32).astype(BF16)
    operands = (weighted, near, far, left, rows)
    gated, squares = final(mine, *operands, *lifts, incoming)
    shared, _ = lax.optimization_barrier((shared, squares))
    gated_next, squares_next = final(1 - mine, *operands, *lifts_next, shared)
    squares = sum(from_all(jnp.concatenate([squares, squares_next]), "head"))
    return normed(
        mine, [gated, gated_next], squares, norm_gain[None, :],
        channels * lax.axis_size("head"),
    )


def solution(mesh):
    in_specs = (
        P("groups", "ctx", "head"),
        P("groups", "ctx", "head"),
        P(None, "groups", "head", "ctx"),
        P("groups", "head", "ctx"),
        P("groups", "head", "ctx"),
        P("head"),
        P("head"),
    )
    out_specs = P("groups", "ctx", "head")
    return jax.shard_map(body, mesh=mesh, in_specs=in_specs, out_specs=out_specs, check_vma=False)
```

```python
import functools

import jax
import jax.numpy as jnp
import numpy as np
from jax import lax
from jax.experimental import pallas as pl
from jax.experimental.pallas import tpu as pltpu
from jax.sharding import PartitionSpec as P

SPAN = 128
HALF = 256
F32 = jnp.float32
BF16 = jnp.bfloat16
MIB = 1024 * 1024
PARAMS = pltpu.CompilerParams(vmem_limit_bytes=4 * MIB)
COST = pl.CostEstimate(flops=1000, bytes_accessed=1000, transcendentals=0)
GATES_COST = pl.CostEstimate(flops=10**9, bytes_accessed=12 * 10**6, transcendentals=15 * 10**5)
LEFT_COST = pl.CostEstimate(flops=5 * 10**7, bytes_accessed=16 * 10**5, transcendentals=0)
STAGING_PARAMS = pltpu.CompilerParams(vmem_limit_bytes=10 * MIB)
ENTER, LEAVE, FIRST, TOTAL = range(4)
ROWS = 32
WHOLE = pl.BlockSpec(memory_space=pltpu.VMEM)
ANYWHERE = pl.BlockSpec(memory_space=pl.ANY)


def in_vmem(array):
    return pltpu.with_memory_space_constraint(array, pltpu.VMEM)


def in_hbm(array):
    return pltpu.with_memory_space_constraint(array, pltpu.HBM)


def mm(a, b):
    return jnp.dot(a, b, preferred_element_type=F32)


def mm_nt(a, b):
    return lax.dot_general(a, b, (((1,), (1,)), ((), ())), preferred_element_type=F32)


def iotas(shape):
    return (
        lax.broadcasted_iota(jnp.int32, shape, 0),
        lax.broadcasted_iota(jnp.int32, shape, 1),
    )


def two_parts(v):
    high = v.astype(BF16)
    return [high, (v - high.astype(F32)).astype(BF16)]


def fill_tables(step_ref, decay_ref, skip_ref, sums_ref, rise_band, both_ref, rows_ref):
    seqs, heads, length = decay_ref.shape
    blocks = length // SPAN
    _, lane = iotas((SPAN, 4 * heads))
    rising = lane < 2 * heads
    is_high = (lane < heads) | ((lane >= 2 * heads) & (lane < 3 * heads))
    until = sums_ref[:SPAN]
    same = sums_ref[SPAN:]

    def parts_of(v):
        high = v.astype(BF16).astype(F32)
        return jnp.where(is_high[:v.shape[0]], high, v - high).astype(BF16)

    skip = jnp.concatenate([skip_ref[...]] * 4, axis=1)
    for s in range(seqs):
        decays = two_parts(jnp.concatenate([decay_ref[s]] * 4, axis=0))
        steps = two_parts(jnp.concatenate([step_ref[s]] * 4, axis=0))
        enter, leave, first = [], [], []
        before = jnp.zeros((1, 4 * heads), F32)
        for k in range(blocks):
            sl = slice(k * SPAN, (k + 1) * SPAN)
            summed = mm_nt(until, jnp.concatenate([p[:, sl] for p in decays], axis=1))
            step = mm_nt(same, jnp.concatenate([p[:, sl] for p in steps], axis=1))
            middle = summed[SPAN // 2 - 1:SPAN // 2]
            last = summed[SPAN - 1:]
            above = summed - middle
            factor = jnp.exp(jnp.where(rising, above, -above))
            both_ref[s, sl, :] = parts_of(jnp.where(rising, factor, step * factor))
            enter.append(jnp.exp(middle))
            leave.append(jnp.exp(last - middle))
            first.append(jnp.exp(middle + before))
            before = before + last
        table = enter + leave + first + [jnp.exp(before)]
        table = table + [jnp.zeros_like(before)] * (ROWS - 1 - len(table)) + [skip]
        rows_ref[s] = mm(parts_of(jnp.concatenate(table, axis=0)), rise_band)


def front_kernel(
    x_hbm, step_hbm, decay_hbm, skip_hbm, sums_hbm, bands_hbm,
    weighted_ref, both_ref, rows_ref, bands, step, decay, skip, sums, sems,
):
    seqs, length, channels = weighted_ref.shape
    heads = decay.shape[1]
    pairs = [
        (decay_hbm, decay), (step_hbm, step), (sums_hbm, sums), (skip_hbm, skip), (bands_hbm, bands)
    ]
    small = len(pairs)
    pairs += [(x_hbm.at[s], weighted_ref.at[s]) for s in range(seqs)]
    copies = [
        pltpu.make_async_copy(source, target, sems.at[i])
        for i, (source, target) in enumerate(pairs)
    ]
    for copy in copies:
        copy.start()
    for copy in copies[:small]:
        copy.wait()
    fill_tables(step, decay, skip, sums, bands[2 * heads:], both_ref, rows_ref)
    for s in range(seqs):
        copies[small + s].wait()
        for k in range(length // SPAN):
            rows = slice(k * SPAN, (k + 1) * SPAN)
            both = both_ref[s, rows]
            for lo in range(0, channels, HALF):
                sl = slice(lo, lo + HALF)
                wide = mm(both, bands[:4 * heads, sl]).astype(BF16)
                weighted_ref[s, rows, sl] = weighted_ref[s, rows, sl] * wide


def front(features, step_size, log_decay, skip, sums, bands):
    seqs, length, channels = features.shape
    heads = step_size.shape[1]
    operands = [features, step_size, log_decay, skip, sums, bands]
    return pl.pallas_call(
        front_kernel,
        in_specs=[ANYWHERE] * 6,
        out_specs=[WHOLE] * 4,
        out_shape=[
            pltpu.VMEM(features.shape, BF16),
            pltpu.VMEM((seqs, length, 4 * heads), BF16),
            pltpu.VMEM((seqs, ROWS, channels), F32),
            pltpu.VMEM(bands.shape, BF16),
        ],
        scratch_shapes=[
            pltpu.VMEM(step_size.shape, F32),
            pltpu.VMEM(log_decay.shape, F32),
            pltpu.VMEM(skip.shape, F32),
            pltpu.VMEM(sums.shape, BF16),
            pltpu.SemaphoreType.DMA((seqs + 5,)),
        ],
        compiler_params=PARAMS,
        cost_estimate=COST,
        name="front",
    )(*[in_hbm(operand) for operand in operands])


def state_kernel(b_ref, weighted_ref, rows_ref, entering_ref, state_ref):
    seqs, length, channels = weighted_ref.shape
    blocks = length // SPAN
    for s in range(seqs):
        for lo in range(0, channels, HALF):
            sl = slice(lo, lo + HALF)
            state = None
            for k in range(blocks):
                rows = slice(k * SPAN, (k + 1) * SPAN)
                added = mm(b_ref[s, :, rows], weighted_ref[s, rows, sl])
                if k > 0:
                    at = ENTER * blocks + k
                    entering = rows_ref[s, at:at + 1, sl] * state
                    entering_ref[s, k - 1, :, sl] = entering.astype(BF16)
                    added = added + entering
                at = LEAVE * blocks + k
                state = rows_ref[s, at:at + 1, sl] * added
            state_ref[s, :, sl] = state.astype(BF16)


def own_states(b, weighted, rows):
    seqs, states, length = b.shape
    channels = weighted.shape[2]
    return pl.pallas_call(
        state_kernel,
        in_specs=[WHOLE] * 3,
        out_specs=[WHOLE] * 2,
        out_shape=[
            pltpu.VMEM((seqs, length // SPAN - 1, states, channels), BF16),
            pltpu.VMEM((seqs, states, channels), BF16),
        ],
        compiler_params=PARAMS,
        cost_estimate=COST,
        name="own_states",
    )(b, in_vmem(weighted), in_vmem(rows))


def gate_kernel(seq_ref, gate_ref, x_ref, both_ref, bands_ref, rows_ref, lift_ref, skipped_ref):
    length, channels = lift_ref.shape
    heads4 = both_ref.shape[2]
    band = slice(heads4 // 2, heads4 // 2 + heads4)
    seq = seq_ref[0]
    for k in range(length // SPAN):
        rows = slice(k * SPAN, (k + 1) * SPAN)
        both = both_ref[seq, rows]
        for lo in range(0, channels, HALF):
            sl = slice(lo, lo + HALF)
            half = 0.5 * gate_ref[seq, rows, sl].astype(F32)
            gate = (half * jnp.tanh(half) + half).astype(BF16)
            lift_ref[rows, sl] = mm(both, bands_ref[band, sl]).astype(BF16) * gate
            skip = rows_ref[seq, ROWS - 1:ROWS, sl].astype(BF16) * x_ref[seq, rows, sl]
            skipped_ref[rows, sl] = skip * gate


def gates(seq, gate_in, x, both, bands, rows):
    _, length, channels = gate_in.shape
    return pl.pallas_call(
        gate_kernel,
        in_specs=[pl.BlockSpec(memory_space=pltpu.SMEM)] + [WHOLE] * 5,
        out_specs=[WHOLE, WHOLE],
        out_shape=[pltpu.VMEM((length, channels), BF16)] * 2,
        compiler_params=PARAMS,
        cost_estimate=GATES_COST,
        name="gates",
    )(seq, in_vmem(gate_in), in_vmem(x), in_vmem(both), in_vmem(bands), in_vmem(rows))


def left_kernel(b_ref, c_ref, left_ref):
    seqs, states, length = b_ref.shape
    row, col = iotas((SPAN, SPAN))
    for s in range(seqs):
        for k in range(length // SPAN):
            rows = slice(k * SPAN, (k + 1) * SPAN)
            c_t = c_ref[s, :, rows].T
            affinity = mm(c_t, b_ref[s, :, rows])
            left_ref[s, rows, :SPAN] = jnp.where(row >= col, affinity, 0.0).astype(BF16)
            left_ref[s, rows, SPAN:] = c_t


def left_of(b, c):
    seqs, states, length = b.shape
    return pl.pallas_call(
        left_kernel,
        in_specs=[WHOLE] * 2,
        out_specs=WHOLE,
        out_shape=pltpu.VMEM((seqs, length, SPAN + states), BF16),
        compiler_params=PARAMS,
        cost_estimate=LEFT_COST,
        name="left",
    )(b, c)


def final_kernel(
    seq_ref, weighted_ref, near_ref, far_ref, left_ref, rows_ref, lift_ref, skipped_ref,
    incoming_ref, gated_ref, square_ref,
):
    length, channels = gated_ref.shape
    blocks = length // SPAN
    s = seq_ref[0]
    for k in range(blocks):
        rows = slice(k * SPAN, (k + 1) * SPAN)
        left = left_ref[s, rows]
        squares = jnp.zeros((SPAN, 128), F32)
        at = FIRST * blocks + k
        for lo in range(0, channels, HALF):
            sl = slice(lo, lo + HALF)
            entering = rows_ref[s, at:at + 1, sl].astype(BF16) * incoming_ref[:, sl]
            if k > 0:
                entering = entering + jnp.concatenate(
                    [near_ref[s, k - 1, :, sl], far_ref[s, k - 1, :, sl]], axis=0
                )
            right = jnp.concatenate([weighted_ref[s, rows, sl], entering], axis=0)
            mixed = mm(left, right).astype(BF16)
            gated = lift_ref[rows, sl] * mixed + skipped_ref[rows, sl]
            gated_ref[rows, sl] = gated
            power = gated * gated
            pair = sum(power[:, half:half + 128] for half in range(0, HALF, 128))
            squares = squares + pair.astype(F32)
        square_ref[k:k + 1] = jnp.sum(squares.T, axis=0, keepdims=True)
    unused = square_ref.shape[0] - blocks
    if unused:
        square_ref[blocks:] = jnp.zeros((unused, SPAN), F32)


def final(seq, weighted, near, far, left, rows, lift, skipped, incoming):
    length, channels = lift.shape
    return pl.pallas_call(
        final_kernel,
        in_specs=[pl.BlockSpec(memory_space=pltpu.SMEM)] + [WHOLE] * 8,
        out_specs=[WHOLE] * 2,
        out_shape=[
            pltpu.VMEM((length, channels), BF16),
            pltpu.VMEM((-(-length // SPAN // 8) * 8, SPAN), F32),
        ],
        compiler_params=PARAMS,
        cost_estimate=COST,
        name="final",
    )(
        seq, in_vmem(weighted), in_vmem(near), in_vmem(far), in_vmem(left), in_vmem(rows),
        in_vmem(lift), in_vmem(skipped), incoming,
    )


def norm_kernel(all_channels, seq_ref, square_ref, gain_ref, *refs):
    gated_refs, (out_hbm, staged, sems) = refs[:-3], refs[-3:]
    length, channels = gated_refs[0].shape
    blocks = length // SPAN
    stride = square_ref.shape[0] // len(gated_refs)
    copies = []
    for number, gated_ref in enumerate(gated_refs):
        s = lax.rem(seq_ref[0] + number, len(gated_refs))
        for k in range(blocks):
            rows = slice(k * SPAN, (k + 1) * SPAN)
            at = number * stride + k
            inverse = lax.rsqrt(square_ref[at:at + 1] / all_channels + 1e-05)
            column = jnp.broadcast_to(inverse, (128, SPAN)).T
            for lo in range(0, channels, 128):
                sl = slice(lo, lo + 128)
                staged[number, rows, sl] = (
                    gated_ref[rows, sl].astype(F32) * column * gain_ref[:, sl]
                ).astype(BF16)
            place = pl.ds(k * SPAN, SPAN)
            copies.append(
                pltpu.make_async_copy(
                    staged.at[number, place], out_hbm.at[s, place], sems.at[number * blocks + k]
                )
            )
            copies[-1].start(priority=k % 2)
    for copy in copies:
        copy.wait()


def normed(first, gated, squares, gain_row, all_channels):
    seqs = len(gated)
    length, channels = gated[0].shape
    return pl.pallas_call(
        functools.partial(norm_kernel, all_channels),
        in_specs=[pl.BlockSpec(memory_space=pltpu.SMEM)] + [WHOLE] * (2 + seqs),
        out_specs=ANYWHERE,
        out_shape=jax.ShapeDtypeStruct((seqs, length, channels), BF16),
        scratch_shapes=[
            pltpu.VMEM((seqs, length, channels), BF16),
            pltpu.SemaphoreType.DMA((seqs * (length // SPAN),)),
        ],
        compiler_params=STAGING_PARAMS,
        cost_estimate=COST,
        name="normed",
    )(first, squares, gain_row, *[in_vmem(one) for one in gated])


def from_partner(shard, axis, by):
    return lax.ppermute(shard, axis, [(i, i ^ by) for i in range(lax.axis_size(axis))])


def doubled(block, axis, by, behind=()):
    other = from_partner(block, axis, by)
    other, _ = lax.optimization_barrier((other, behind))
    return jnp.concatenate([block, other], axis=1)


def from_all(shard, axis):
    return [shard] + [from_partner(shard, axis, by) for by in range(1, lax.axis_size(axis))]


def as_parts(row):
    high = row.astype(BF16)
    low = (row - high.astype(F32)).astype(BF16)
    return jnp.concatenate([high, low, jnp.zeros((14, row.shape[1]), BF16)], axis=0)


def body(features, gate_in, state_proj, step_size, log_decay, skip_gain, norm_gain):
    seqs, length, channels = features.shape
    heads = step_size.shape[1]
    pair = np.repeat(np.concatenate([np.eye(heads)] * 2), channels // heads, axis=1)
    bands = jnp.asarray(np.concatenate([0 * pair, pair, 0 * pair]), BF16)
    until = np.tril(np.ones((SPAN, SPAN)))
    sums = jnp.asarray(np.concatenate([np.tile(until, 2), np.tile(np.eye(SPAN), 2)]), BF16)
    b_own, c_own = lax.optimization_barrier((state_proj[0], state_proj[1]))
    b_pieces = from_all(b_own, "head")
    b_near = jnp.concatenate(b_pieces[:2], axis=1)
    weighted, both, rows, bands = front(
        features, step_size, log_decay, skip_gain[None, :], sums, bands
    )

    place = lax.axis_index("ctx")
    even = place % 2 == 0
    mine = (place % 2).astype(jnp.int32)[None]
    devices = lax.axis_size("ctx")
    swap = [(i, i ^ 1) for i in range(devices)]
    total_at = TOTAL * (length // SPAN)
    decays = [rows[s, total_at:total_at + 1] for s in range(seqs)]
    decay = jnp.where(even, decays[0], decays[1])

    def past_chip(end, other, decay_other):
        return jnp.where(even, other + decay_other * end, end + decay * other)

    def across(past, entered, hop):
        sent = past if entered is None else past + decay_past * entered.astype(F32)
        sent = sent.astype(BF16)
        return sent, lax.ppermute(sent, "ctx", [(hop, hop + 2), (hop + 1, hop + 3)])

    near, near_ends = own_states(b_near, weighted, rows)
    near_rows = b_near.shape[1]
    other = lax.ppermute(
        jnp.concatenate([
            jnp.where(even, near_ends[1], near_ends[0]),
            as_parts(jnp.where(even, decays[1], decays[0])),
        ]),
        "ctx", swap,
    )
    near_other = other[:near_rows].astype(F32)
    decay_other = (
        other[near_rows:near_rows + 1].astype(F32) + other[near_rows + 1:near_rows + 2].astype(F32)
    )
    decay_past = decay_other * decay
    near_end = jnp.where(even, near_ends[0], near_ends[1]).astype(F32)
    near_past = past_chip(near_end, near_other, decay_other)
    near_sent, near_got = across(near_past, None, 0)
    b_far, _ = lax.optimization_barrier((b_pieces[2:], near_sent))
    b_far = jnp.concatenate(b_far, axis=1)
    far, far_ends = own_states(b_far, weighted, rows)
    far_other = lax.ppermute(jnp.where(even, far_ends[1], far_ends[0]), "ctx", swap).astype(F32)
    far_end = jnp.where(even, far_ends[0], far_ends[1]).astype(F32)
    far_past = past_chip(far_end, far_other, decay_other)
    far_sent, far_got = across(far_past, None, 0)
    c_own, _ = lax.optimization_barrier((c_own, near_ends))
    c = doubled(c_own, "head", 1, near_sent)
    both, _ = lax.optimization_barrier((both, far_sent))
    lifts = gates(mine, gate_in, features, both, bands, rows)
    for by in (1 << i for i in range(1, (lax.axis_size("head") - 1).bit_length())):
        c = doubled(c, "head", by, lifts)
    both, c = lax.optimization_barrier((both, c))
    lifts_next = gates(1 - mine, gate_in, features, both, bands, rows)
    left = left_of(jnp.concatenate([b_near, b_far], axis=1), c)
    left, lifts_next = lax.optimization_barrier((left, lifts_next))
    near_got, far_got, left = lax.optimization_barrier((near_got, far_got, left))
    for hop in range(2, devices - 2, 2):
        near_got = near_got + across(near_past, near_got, hop)[1]
        far_got = far_got + across(far_past, far_got, hop)[1]
    entered = jnp.concatenate([near_got, far_got])
    entered32 = entered.astype(F32)
    end = jnp.concatenate([near_end, far_end])
    end_other = jnp.concatenate([near_other, far_other])
    shared = lax.ppermute(
        jnp.where(even, end + decay * entered32, entered32).astype(BF16), "ctx", swap
    )
    incoming = jnp.where(even, entered32, end_other + decay_other * entered32).astype(BF16)
    operands = (weighted, near, far, left, rows)
    gated, squares = final(mine, *operands, *lifts, incoming)
    shared, _ = lax.optimization_barrier((shared, squares))
    gated_next, squares_next = final(1 - mine, *operands, *lifts_next, shared)
    squares = sum(from_all(jnp.concatenate([squares, squares_next]), "head"))
    return normed(
        mine, [gated, gated_next], squares, norm_gain[None, :],
        channels * lax.axis_size("head"),
    )


def solution(mesh):
    in_specs = (
        P("groups", "ctx", "head"),
        P("groups", "ctx", "head"),
        P(None, "groups", "head", "ctx"),
        P("groups", "head", "ctx"),
        P("groups", "head", "ctx"),
        P("head"),
        P("head"),
    )
    out_specs = P("groups", "ctx", "head")
    return jax.shard_map(body, mesh=mesh, in_specs=in_specs, out_specs=out_specs, check_vma=False)
```

```python
import functools

import jax
import jax.numpy as jnp
import numpy as np
from jax import lax
from jax.experimental import pallas as pl
from jax.experimental.pallas import tpu as pltpu
from jax.sharding import PartitionSpec as P

SPAN = 128
HALF = 256
F32 = jnp.float32
BF16 = jnp.bfloat16
MIB = 1024 * 1024
PARAMS = pltpu.CompilerParams(vmem_limit_bytes=4 * MIB)
COST = pl.CostEstimate(flops=1000, bytes_accessed=1000, transcendentals=0)
GATES_COST = pl.CostEstimate(flops=10**9, bytes_accessed=12 * 10**6, transcendentals=15 * 10**5)
LEFT_COST = pl.CostEstimate(flops=5 * 10**7, bytes_accessed=16 * 10**5, transcendentals=0)
STAGING_PARAMS = pltpu.CompilerParams(vmem_limit_bytes=10 * MIB)
ENTER, LEAVE, FIRST, TOTAL = range(4)
ROWS = 32
WHOLE = pl.BlockSpec(memory_space=pltpu.VMEM)
ANYWHERE = pl.BlockSpec(memory_space=pl.ANY)


def in_vmem(array):
    return pltpu.with_memory_space_constraint(array, pltpu.VMEM)


def in_hbm(array):
    return pltpu.with_memory_space_constraint(array, pltpu.HBM)


def mm(a, b):
    return jnp.dot(a, b, preferred_element_type=F32)


def mm_nt(a, b):
    return lax.dot_general(a, b, (((1,), (1,)), ((), ())), preferred_element_type=F32)


def iotas(shape):
    return (
        lax.broadcasted_iota(jnp.int32, shape, 0),
        lax.broadcasted_iota(jnp.int32, shape, 1),
    )


def two_parts(v):
    high = v.astype(BF16)
    return [high, (v - high.astype(F32)).astype(BF16)]


def fill_tables(step_ref, decay_ref, skip_ref, sums_ref, rise_band, both_ref, rows_ref):
    seqs, heads, length = decay_ref.shape
    blocks = length // SPAN
    _, lane = iotas((SPAN, 4 * heads))
    rising = lane < 2 * heads
    is_high = (lane < heads) | ((lane >= 2 * heads) & (lane < 3 * heads))
    until = sums_ref[:SPAN]
    same = sums_ref[SPAN:]

    def parts_of(v):
        high = v.astype(BF16).astype(F32)
        return jnp.where(is_high[:v.shape[0]], high, v - high).astype(BF16)

    skip = jnp.concatenate([skip_ref[...]] * 4, axis=1)
    for s in range(seqs):
        decays = two_parts(jnp.concatenate([decay_ref[s]] * 4, axis=0))
        steps = two_parts(jnp.concatenate([step_ref[s]] * 4, axis=0))
        enter, leave, first = [], [], []
        before = jnp.zeros((1, 4 * heads), F32)
        for k in range(blocks):
            sl = slice(k * SPAN, (k + 1) * SPAN)
            summed = mm_nt(until, jnp.concatenate([p[:, sl] for p in decays], axis=1))
            step = mm_nt(same, jnp.concatenate([p[:, sl] for p in steps], axis=1))
            middle = summed[SPAN // 2 - 1:SPAN // 2]
            last = summed[SPAN - 1:]
            above = summed - middle
            factor = jnp.exp(jnp.where(rising, above, -above))
            both_ref[s, sl, :] = parts_of(jnp.where(rising, factor, step * factor))
            enter.append(jnp.exp(middle))
            leave.append(jnp.exp(last - middle))
            first.append(jnp.exp(middle + before))
            before = before + last
        table = enter + leave + first + [jnp.exp(before)]
        table = table + [jnp.zeros_like(before)] * (ROWS - 1 - len(table)) + [skip]
        rows_ref[s] = mm(parts_of(jnp.concatenate(table, axis=0)), rise_band)


def front_kernel(
    x_hbm, step_hbm, decay_hbm, skip_hbm, sums_hbm, bands_hbm,
    weighted_ref, both_ref, rows_ref, bands, step, decay, skip, sums, sems,
):
    seqs, length, channels = weighted_ref.shape
    heads = decay.shape[1]
    pairs = [
        (decay_hbm, decay), (step_hbm, step), (sums_hbm, sums), (skip_hbm, skip), (bands_hbm, bands)
    ]
    small = len(pairs)
    pairs += [(x_hbm.at[s], weighted_ref.at[s]) for s in range(seqs)]
    copies = [
        pltpu.make_async_copy(source, target, sems.at[i])
        for i, (source, target) in enumerate(pairs)
    ]
    for copy in copies:
        copy.start()
    for copy in copies[:small]:
        copy.wait()
    fill_tables(step, decay, skip, sums, bands[2 * heads:], both_ref, rows_ref)
    for s in range(seqs):
        copies[small + s].wait()
        for k in range(length // SPAN):
            rows = slice(k * SPAN, (k + 1) * SPAN)
            both = both_ref[s, rows]
            for lo in range(0, channels, HALF):
                sl = slice(lo, lo + HALF)
                wide = mm(both, bands[:4 * heads, sl]).astype(BF16)
                weighted_ref[s, rows, sl] = weighted_ref[s, rows, sl] * wide


def front(features, step_size, log_decay, skip, sums, bands):
    seqs, length, channels = features.shape
    heads = step_size.shape[1]
    operands = [features, step_size, log_decay, skip, sums, bands]
    return pl.pallas_call(
        front_kernel,
        in_specs=[ANYWHERE] * 6,
        out_specs=[WHOLE] * 4,
        out_shape=[
            pltpu.VMEM(features.shape, BF16),
            pltpu.VMEM((seqs, length, 4 * heads), BF16),
            pltpu.VMEM((seqs, ROWS, channels), F32),
            pltpu.VMEM(bands.shape, BF16),
        ],
        scratch_shapes=[
            pltpu.VMEM(step_size.shape, F32),
            pltpu.VMEM(log_decay.shape, F32),
            pltpu.VMEM(skip.shape, F32),
            pltpu.VMEM(sums.shape, BF16),
            pltpu.SemaphoreType.DMA((seqs + 5,)),
        ],
        compiler_params=PARAMS,
        cost_estimate=COST,
        name="front",
    )(*[in_hbm(operand) for operand in operands])


def state_kernel(b_ref, weighted_ref, rows_ref, entering_ref, state_ref):
    seqs, length, channels = weighted_ref.shape
    blocks = length // SPAN
    for s in range(seqs):
        for lo in range(0, channels, HALF):
            sl = slice(lo, lo + HALF)
            state = None
            for k in range(blocks):
                rows = slice(k * SPAN, (k + 1) * SPAN)
                added = mm(b_ref[s, :, rows], weighted_ref[s, rows, sl])
                if k > 0:
                    at = ENTER * blocks + k
                    entering = rows_ref[s, at:at + 1, sl] * state
                    entering_ref[s, k - 1, :, sl] = entering.astype(BF16)
                    added = added + entering
                at = LEAVE * blocks + k
                state = rows_ref[s, at:at + 1, sl] * added
            state_ref[s, :, sl] = state.astype(BF16)


def own_states(b, weighted, rows):
    seqs, states, length = b.shape
    channels = weighted.shape[2]
    return pl.pallas_call(
        state_kernel,
        in_specs=[WHOLE] * 3,
        out_specs=[WHOLE] * 2,
        out_shape=[
            pltpu.VMEM((seqs, length // SPAN - 1, states, channels), BF16),
            pltpu.VMEM((seqs, states, channels), BF16),
        ],
        compiler_params=PARAMS,
        cost_estimate=COST,
        name="own_states",
    )(b, in_vmem(weighted), in_vmem(rows))


def gate_kernel(seq_ref, gate_ref, x_ref, both_ref, bands_ref, rows_ref, lift_ref, skipped_ref):
    length, channels = lift_ref.shape
    heads4 = both_ref.shape[2]
    band = slice(heads4 // 2, heads4 // 2 + heads4)
    seq = seq_ref[0]
    for k in range(length // SPAN):
        rows = slice(k * SPAN, (k + 1) * SPAN)
        both = both_ref[seq, rows]
        for lo in range(0, channels, HALF):
            sl = slice(lo, lo + HALF)
            half = 0.5 * gate_ref[seq, rows, sl].astype(F32)
            gate = (half * jnp.tanh(half) + half).astype(BF16)
            lift_ref[rows, sl] = mm(both, bands_ref[band, sl]).astype(BF16) * gate
            skip = rows_ref[seq, ROWS - 1:ROWS, sl].astype(BF16) * x_ref[seq, rows, sl]
            skipped_ref[rows, sl] = skip * gate


def gates(seq, gate_in, x, both, bands, rows):
    _, length, channels = gate_in.shape
    return pl.pallas_call(
        gate_kernel,
        in_specs=[pl.BlockSpec(memory_space=pltpu.SMEM)] + [WHOLE] * 5,
        out_specs=[WHOLE, WHOLE],
        out_shape=[pltpu.VMEM((length, channels), BF16)] * 2,
        compiler_params=PARAMS,
        cost_estimate=GATES_COST,
        name="gates",
    )(seq, in_vmem(gate_in), in_vmem(x), in_vmem(both), in_vmem(bands), in_vmem(rows))


def left_kernel(b_ref, c_ref, left_ref):
    seqs, states, length = b_ref.shape
    row, col = iotas((SPAN, SPAN))
    for s in range(seqs):
        for k in range(length // SPAN):
            rows = slice(k * SPAN, (k + 1) * SPAN)
            c_t = c_ref[s, :, rows].T
            affinity = mm(c_t, b_ref[s, :, rows])
            left_ref[s, rows, :SPAN] = jnp.where(row >= col, affinity, 0.0).astype(BF16)
            left_ref[s, rows, SPAN:] = c_t


def left_of(b, c):
    seqs, states, length = b.shape
    return pl.pallas_call(
        left_kernel,
        in_specs=[WHOLE] * 2,
        out_specs=WHOLE,
        out_shape=pltpu.VMEM((seqs, length, SPAN + states), BF16),
        compiler_params=PARAMS,
        cost_estimate=LEFT_COST,
        name="left",
    )(b, c)


def final_kernel(
    seq_ref, weighted_ref, near_ref, far_ref, left_ref, rows_ref, lift_ref, skipped_ref,
    incoming_ref, gated_ref, square_ref,
):
    length, channels = gated_ref.shape
    blocks = length // SPAN
    s = seq_ref[0]
    for k in range(blocks):
        rows = slice(k * SPAN, (k + 1) * SPAN)
        left = left_ref[s, rows]
        squares = jnp.zeros((SPAN, 128), F32)
        at = FIRST * blocks + k
        for lo in range(0, channels, HALF):
            sl = slice(lo, lo + HALF)
            entering = rows_ref[s, at:at + 1, sl].astype(BF16) * incoming_ref[:, sl]
            if k > 0:
                entering = entering + jnp.concatenate(
                    [near_ref[s, k - 1, :, sl], far_ref[s, k - 1, :, sl]], axis=0
                )
            right = jnp.concatenate([weighted_ref[s, rows, sl], entering], axis=0)
            mixed = mm(left, right).astype(BF16)
            gated = lift_ref[rows, sl] * mixed + skipped_ref[rows, sl]
            gated_ref[rows, sl] = gated
            power = gated * gated
            pair = sum(power[:, half:half + 128] for half in range(0, HALF, 128))
            squares = squares + pair.astype(F32)
        square_ref[k:k + 1] = jnp.sum(squares.T, axis=0, keepdims=True)
    unused = square_ref.shape[0] - blocks
    if unused:
        square_ref[blocks:] = jnp.zeros((unused, SPAN), F32)


def final(seq, weighted, near, far, left, rows, lift, skipped, incoming):
    length, channels = lift.shape
    return pl.pallas_call(
        final_kernel,
        in_specs=[pl.BlockSpec(memory_space=pltpu.SMEM)] + [WHOLE] * 8,
        out_specs=[WHOLE] * 2,
        out_shape=[
            pltpu.VMEM((length, channels), BF16),
            pltpu.VMEM((-(-length // SPAN // 8) * 8, SPAN), F32),
        ],
        compiler_params=PARAMS,
        cost_estimate=COST,
        name="final",
    )(
        seq, in_vmem(weighted), in_vmem(near), in_vmem(far), in_vmem(left), in_vmem(rows),
        in_vmem(lift), in_vmem(skipped), incoming,
    )


def norm_kernel(all_channels, seq_ref, square_ref, gain_ref, *refs):
    gated_refs, (out_hbm, staged, sems) = refs[:-3], refs[-3:]
    length, channels = gated_refs[0].shape
    blocks = length // SPAN
    stride = square_ref.shape[0] // len(gated_refs)
    copies = []
    for number, gated_ref in enumerate(gated_refs):
        s = lax.rem(seq_ref[0] + number, len(gated_refs))
        for k in range(blocks):
            rows = slice(k * SPAN, (k + 1) * SPAN)
            at = number * stride + k
            inverse = lax.rsqrt(square_ref[at:at + 1] / all_channels + 1e-05)
            column = jnp.broadcast_to(inverse, (128, SPAN)).T
            for lo in range(0, channels, 128):
                sl = slice(lo, lo + 128)
                staged[number, rows, sl] = (
                    gated_ref[rows, sl].astype(F32) * column * gain_ref[:, sl]
                ).astype(BF16)
            place = pl.ds(k * SPAN, SPAN)
            copies.append(
                pltpu.make_async_copy(
                    staged.at[number, place], out_hbm.at[s, place], sems.at[number * blocks + k]
                )
            )
            copies[-1].start(priority=k % 2)
    for copy in copies:
        copy.wait()


def normed(first, gated, squares, gain_row, all_channels):
    seqs = len(gated)
    length, channels = gated[0].shape
    return pl.pallas_call(
        functools.partial(norm_kernel, all_channels),
        in_specs=[pl.BlockSpec(memory_space=pltpu.SMEM)] + [WHOLE] * (2 + seqs),
        out_specs=ANYWHERE,
        out_shape=jax.ShapeDtypeStruct((seqs, length, channels), BF16),
        scratch_shapes=[
            pltpu.VMEM((seqs, length, channels), BF16),
            pltpu.SemaphoreType.DMA((seqs * (length // SPAN),)),
        ],
        compiler_params=STAGING_PARAMS,
        cost_estimate=COST,
        name="normed",
    )(first, squares, gain_row, *[in_vmem(one) for one in gated])


def from_partner(shard, axis, by):
    return lax.ppermute(shard, axis, [(i, i ^ by) for i in range(lax.axis_size(axis))])


def doubled(block, axis, by, behind=()):
    other = from_partner(block, axis, by)
    other, _ = lax.optimization_barrier((other, behind))
    return jnp.concatenate([block, other], axis=1)


def from_all(shard, axis):
    return [shard] + [from_partner(shard, axis, by) for by in range(1, lax.axis_size(axis))]


def as_parts(row):
    high = row.astype(BF16)
    low = (row - high.astype(F32)).astype(BF16)
    return jnp.concatenate([high, low, jnp.zeros((14, row.shape[1]), BF16)], axis=0)


def body(features, gate_in, state_proj, step_size, log_decay, skip_gain, norm_gain):
    seqs, length, channels = features.shape
    heads = step_size.shape[1]
    pair = np.repeat(np.concatenate([np.eye(heads)] * 2), channels // heads, axis=1)
    bands = jnp.asarray(np.concatenate([0 * pair, pair, 0 * pair]), BF16)
    until = np.tril(np.ones((SPAN, SPAN)))
    sums = jnp.asarray(np.concatenate([np.tile(until, 2), np.tile(np.eye(SPAN), 2)]), BF16)
    b_own, c_own = lax.optimization_barrier((state_proj[0], state_proj[1]))
    b_pieces = from_all(b_own, "head")
    b_near = jnp.concatenate(b_pieces[:2], axis=1)
    weighted, both, rows, bands = front(
        features, step_size, log_decay, skip_gain[None, :], sums, bands
    )

    place = lax.axis_index("ctx")
    even = place % 2 == 0
    mine = (place % 2).astype(jnp.int32)[None]
    devices = lax.axis_size("ctx")
    swap = [(i, i ^ 1) for i in range(devices)]
    total_at = TOTAL * (length // SPAN)
    decays = [rows[s, total_at:total_at + 1] for s in range(seqs)]
    decay = jnp.where(even, decays[0], decays[1])

    def past_chip(end, other, decay_other):
        return jnp.where(even, other + decay_other * end, end + decay * other)

    def across(past, entered, hop):
        sent = past if entered is None else past + decay_past * entered.astype(F32)
        sent = sent.astype(BF16)
        return sent, lax.ppermute(sent, "ctx", [(hop, hop + 2), (hop + 1, hop + 3)])

    near, near_ends = own_states(b_near, weighted, rows)
    near_rows = b_near.shape[1]
    other = lax.ppermute(
        jnp.concatenate([
            jnp.where(even, near_ends[1], near_ends[0]),
            as_parts(jnp.where(even, decays[1], decays[0])),
        ]),
        "ctx", swap,
    )
    near_other = other[:near_rows].astype(F32)
    decay_other = (
        other[near_rows:near_rows + 1].astype(F32) + other[near_rows + 1:near_rows + 2].astype(F32)
    )
    decay_past = decay_other * decay
    near_end = jnp.where(even, near_ends[0], near_ends[1]).astype(F32)
    near_past = past_chip(near_end, near_other, decay_other)
    near_sent, near_got = across(near_past, None, 0)
    b_far, _ = lax.optimization_barrier((b_pieces[2:], near_sent))
    b_far = jnp.concatenate(b_far, axis=1)
    far, far_ends = own_states(b_far, weighted, rows)
    far_swap = jnp.where(even, far_ends[1], far_ends[0])
    far_other = lax.ppermute(far_swap, "ctx", swap).astype(F32)
    far_end = jnp.where(even, far_ends[0], far_ends[1]).astype(F32)
    far_past = past_chip(far_end, far_other, decay_other)
    far_sent, far_got = across(far_past, None, 0)
    c_own, _ = lax.optimization_barrier((c_own, near_ends))
    c = doubled(c_own, "head", 1, far_swap)
    both, _ = lax.optimization_barrier((both, far_sent))
    lifts = gates(mine, gate_in, features, both, bands, rows)
    lifts_next = gates(1 - mine, gate_in, features, both, bands, rows)
    for by in (1 << i for i in range(1, (lax.axis_size("head") - 1).bit_length())):
        c = doubled(c, "head", by, (lifts, lifts_next))
    left = left_of(jnp.concatenate([b_near, b_far], axis=1), c)
    near_got, far_got, left = lax.optimization_barrier((near_got, far_got, left))
    for hop in range(2, devices - 2, 2):
        near_got = near_got + across(near_past, near_got, hop)[1]
        far_got = far_got + across(far_past, far_got, hop)[1]
    entered = jnp.concatenate([near_got, far_got])
    entered32 = entered.astype(F32)
    end = jnp.concatenate([near_end, far_end])
    end_other = jnp.concatenate([near_other, far_other])
    shared = lax.ppermute(
        jnp.where(even, end + decay * entered32, entered32).astype(BF16), "ctx", swap
    )
    incoming = jnp.where(even, entered32, end_other + decay_other * entered32).astype(BF16)
    operands = (weighted, near, far, left, rows)
    gated, squares = final(mine, *operands, *lifts, incoming)
    shared, _ = lax.optimization_barrier((shared, squares))
    gated_next, squares_next = final(1 - mine, *operands, *lifts_next, shared)
    squares = sum(from_all(jnp.concatenate([squares, squares_next]), "head"))
    return normed(
        mine, [gated, gated_next], squares, norm_gain[None, :],
        channels * lax.axis_size("head"),
    )


def solution(mesh):
    in_specs = (
        P("groups", "ctx", "head"),
        P("groups", "ctx", "head"),
        P(None, "groups", "head", "ctx"),
        P("groups", "head", "ctx"),
        P("groups", "head", "ctx"),
        P("head"),
        P("head"),
    )
    out_specs = P("groups", "ctx", "head")
    return jax.shard_map(body, mesh=mesh, in_specs=in_specs, out_specs=out_specs, check_vma=False)
```

```python
import functools

import jax
import jax.numpy as jnp
import numpy as np
from jax import lax
from jax.experimental import pallas as pl
from jax.experimental.pallas import tpu as pltpu
from jax.sharding import PartitionSpec as P

SPAN = 128
HALF = 256
F32 = jnp.float32
BF16 = jnp.bfloat16
MIB = 1024 * 1024
PARAMS = pltpu.CompilerParams(vmem_limit_bytes=4 * MIB)
COST = pl.CostEstimate(flops=1000, bytes_accessed=1000, transcendentals=0)
GATES_COST = pl.CostEstimate(flops=10**9, bytes_accessed=12 * 10**6, transcendentals=15 * 10**5)
LEFT_COST = pl.CostEstimate(flops=5 * 10**7, bytes_accessed=16 * 10**5, transcendentals=0)
STAGING_PARAMS = pltpu.CompilerParams(vmem_limit_bytes=10 * MIB)
ENTER, LEAVE, FIRST, TOTAL = range(4)
ROWS = 32
WHOLE = pl.BlockSpec(memory_space=pltpu.VMEM)
ANYWHERE = pl.BlockSpec(memory_space=pl.ANY)


def in_vmem(array):
    return pltpu.with_memory_space_constraint(array, pltpu.VMEM)


def in_hbm(array):
    return pltpu.with_memory_space_constraint(array, pltpu.HBM)


def mm(a, b):
    return jnp.dot(a, b, preferred_element_type=F32)


def mm_nt(a, b):
    return lax.dot_general(a, b, (((1,), (1,)), ((), ())), preferred_element_type=F32)


def iotas(shape):
    return (
        lax.broadcasted_iota(jnp.int32, shape, 0),
        lax.broadcasted_iota(jnp.int32, shape, 1),
    )


def two_parts(v):
    high = v.astype(BF16)
    return [high, (v - high.astype(F32)).astype(BF16)]


def fill_tables(step_ref, decay_ref, skip_ref, sums_ref, rise_band, both_ref, rows_ref):
    seqs, heads, length = decay_ref.shape
    blocks = length // SPAN
    _, lane = iotas((SPAN, 4 * heads))
    rising = lane < 2 * heads
    is_high = (lane < heads) | ((lane >= 2 * heads) & (lane < 3 * heads))
    until = sums_ref[:SPAN]
    same = sums_ref[SPAN:]

    def parts_of(v):
        high = v.astype(BF16).astype(F32)
        return jnp.where(is_high[:v.shape[0]], high, v - high).astype(BF16)

    skip = jnp.concatenate([skip_ref[...]] * 4, axis=1)
    for s in range(seqs):
        decays = two_parts(jnp.concatenate([decay_ref[s]] * 4, axis=0))
        steps = two_parts(jnp.concatenate([step_ref[s]] * 4, axis=0))
        enter, leave, first = [], [], []
        before = jnp.zeros((1, 4 * heads), F32)
        for k in range(blocks):
            sl = slice(k * SPAN, (k + 1) * SPAN)
            summed = mm_nt(until, jnp.concatenate([p[:, sl] for p in decays], axis=1))
            step = mm_nt(same, jnp.concatenate([p[:, sl] for p in steps], axis=1))
            middle = summed[SPAN // 2 - 1:SPAN // 2]
            last = summed[SPAN - 1:]
            above = summed - middle
            factor = jnp.exp(jnp.where(rising, above, -above))
            both_ref[s, sl, :] = parts_of(jnp.where(rising, factor, step * factor))
            enter.append(jnp.exp(middle))
            leave.append(jnp.exp(last - middle))
            first.append(jnp.exp(middle + before))
            before = before + last
        table = enter + leave + first + [jnp.exp(before)]
        table = table + [jnp.zeros_like(before)] * (ROWS - 1 - len(table)) + [skip]
        rows_ref[s] = mm(parts_of(jnp.concatenate(table, axis=0)), rise_band)


def front_kernel(
    x_hbm, step_hbm, decay_hbm, skip_hbm, sums_hbm, bands_hbm,
    weighted_ref, both_ref, rows_ref, bands, step, decay, skip, sums, sems,
):
    seqs, length, channels = weighted_ref.shape
    heads = decay.shape[1]
    pairs = [
        (decay_hbm, decay), (step_hbm, step), (sums_hbm, sums), (skip_hbm, skip), (bands_hbm, bands)
    ]
    small = len(pairs)
    pairs += [(x_hbm.at[s], weighted_ref.at[s]) for s in range(seqs)]
    copies = [
        pltpu.make_async_copy(source, target, sems.at[i])
        for i, (source, target) in enumerate(pairs)
    ]
    for copy in copies:
        copy.start()
    for copy in copies[:small]:
        copy.wait()
    fill_tables(step, decay, skip, sums, bands[2 * heads:], both_ref, rows_ref)
    for s in range(seqs):
        copies[small + s].wait()
        for k in range(length // SPAN):
            rows = slice(k * SPAN, (k + 1) * SPAN)
            both = both_ref[s, rows]
            for lo in range(0, channels, HALF):
                sl = slice(lo, lo + HALF)
                wide = mm(both, bands[:4 * heads, sl]).astype(BF16)
                weighted_ref[s, rows, sl] = weighted_ref[s, rows, sl] * wide


def front(features, step_size, log_decay, skip, sums, bands):
    seqs, length, channels = features.shape
    heads = step_size.shape[1]
    operands = [features, step_size, log_decay, skip, sums, bands]
    return pl.pallas_call(
        front_kernel,
        in_specs=[ANYWHERE] * 6,
        out_specs=[WHOLE] * 4,
        out_shape=[
            pltpu.VMEM(features.shape, BF16),
            pltpu.VMEM((seqs, length, 4 * heads), BF16),
            pltpu.VMEM((seqs, ROWS, channels), F32),
            pltpu.VMEM(bands.shape, BF16),
        ],
        scratch_shapes=[
            pltpu.VMEM(step_size.shape, F32),
            pltpu.VMEM(log_decay.shape, F32),
            pltpu.VMEM(skip.shape, F32),
            pltpu.VMEM(sums.shape, BF16),
            pltpu.SemaphoreType.DMA((seqs + 5,)),
        ],
        compiler_params=PARAMS,
        cost_estimate=COST,
        name="front",
    )(*[in_hbm(operand) for operand in operands])


def state_kernel(b_ref, weighted_ref, rows_ref, entering_ref, state_ref):
    seqs, length, channels = weighted_ref.shape
    blocks = length // SPAN
    for s in range(seqs):
        for lo in range(0, channels, HALF):
            sl = slice(lo, lo + HALF)
            state = None
            for k in range(blocks):
                rows = slice(k * SPAN, (k + 1) * SPAN)
                added = mm(b_ref[s, :, rows], weighted_ref[s, rows, sl])
                if k > 0:
                    at = ENTER * blocks + k
                    entering = rows_ref[s, at:at + 1, sl] * state
                    entering_ref[s, k - 1, :, sl] = entering.astype(BF16)
                    added = added + entering
                at = LEAVE * blocks + k
                state = rows_ref[s, at:at + 1, sl] * added
            state_ref[s, :, sl] = state.astype(BF16)


def own_states(b, weighted, rows):
    seqs, states, length = b.shape
    channels = weighted.shape[2]
    return pl.pallas_call(
        state_kernel,
        in_specs=[WHOLE] * 3,
        out_specs=[WHOLE] * 2,
        out_shape=[
            pltpu.VMEM((seqs, length // SPAN - 1, states, channels), BF16),
            pltpu.VMEM((seqs, states, channels), BF16),
        ],
        compiler_params=PARAMS,
        cost_estimate=COST,
        name="own_states",
    )(b, in_vmem(weighted), in_vmem(rows))


def gate_kernel(seq_ref, gate_ref, x_ref, both_ref, bands_ref, rows_ref, lift_ref, skipped_ref):
    length, channels = lift_ref.shape
    heads4 = both_ref.shape[2]
    band = slice(heads4 // 2, heads4 // 2 + heads4)
    seq = seq_ref[0]
    for k in range(length // SPAN):
        rows = slice(k * SPAN, (k + 1) * SPAN)
        both = both_ref[seq, rows]
        for lo in range(0, channels, HALF):
            sl = slice(lo, lo + HALF)
            half = 0.5 * gate_ref[seq, rows, sl].astype(F32)
            gate = (half * jnp.tanh(half) + half).astype(BF16)
            lift_ref[rows, sl] = mm(both, bands_ref[band, sl]).astype(BF16) * gate
            skip = rows_ref[seq, ROWS - 1:ROWS, sl].astype(BF16) * x_ref[seq, rows, sl]
            skipped_ref[rows, sl] = skip * gate


def gates(seq, gate_in, x, both, bands, rows):
    _, length, channels = gate_in.shape
    return pl.pallas_call(
        gate_kernel,
        in_specs=[pl.BlockSpec(memory_space=pltpu.SMEM)] + [WHOLE] * 5,
        out_specs=[WHOLE, WHOLE],
        out_shape=[pltpu.VMEM((length, channels), BF16)] * 2,
        compiler_params=PARAMS,
        cost_estimate=GATES_COST,
        name="gates",
    )(seq, in_vmem(gate_in), in_vmem(x), in_vmem(both), in_vmem(bands), in_vmem(rows))


def local_kernel(
    seq_ref, weighted_ref, near_ref, far_ref, lift_ref, skipped_ref, b_ref, c_ref, rows_ref,
    own_ref, factor_ref, c_t_ref,
):
    length, channels = own_ref.shape
    blocks = length // SPAN
    s = seq_ref[0]
    row, col = iotas((SPAN, SPAN))
    for k in range(blocks):
        rows = slice(k * SPAN, (k + 1) * SPAN)
        c_t = c_ref[s, :, rows].T
        c_t_ref[rows] = c_t
        affinity = mm(c_t, b_ref[s, :, rows])
        left = jnp.where(row >= col, affinity, 0.0).astype(BF16)
        if k > 0:
            left = jnp.concatenate([left, c_t], axis=1)
        at = FIRST * blocks + k
        for lo in range(0, channels, HALF):
            sl = slice(lo, lo + HALF)
            right = weighted_ref[s, rows, sl]
            if k > 0:
                right = jnp.concatenate(
                    [right, near_ref[s, k - 1, :, sl], far_ref[s, k - 1, :, sl]], axis=0
                )
            lift = lift_ref[rows, sl]
            own_ref[rows, sl] = lift * mm(left, right).astype(BF16) + skipped_ref[rows, sl]
            factor_ref[rows, sl] = lift * rows_ref[s, at:at + 1, sl].astype(BF16)


def local_terms(seq, weighted, near, far, lift, skipped, b, c, rows):
    length, channels = lift.shape
    states = b.shape[1]
    return pl.pallas_call(
        local_kernel,
        in_specs=[pl.BlockSpec(memory_space=pltpu.SMEM)] + [WHOLE] * 8,
        out_specs=[WHOLE] * 3,
        out_shape=[
            pltpu.VMEM(lift.shape, BF16),
            pltpu.VMEM(lift.shape, BF16),
            pltpu.VMEM((length, states), BF16),
        ],
        compiler_params=PARAMS,
        cost_estimate=LEFT_COST,
        name="local_terms",
    )(
        seq, in_vmem(weighted), in_vmem(near), in_vmem(far), in_vmem(lift), in_vmem(skipped),
        b, c, in_vmem(rows),
    )


def joined_kernel(own_ref, factor_ref, c_t_ref, incoming_ref, gated_ref, square_ref):
    length, channels = own_ref.shape
    blocks = length // SPAN
    for k in range(blocks):
        rows = slice(k * SPAN, (k + 1) * SPAN)
        c_t = c_t_ref[rows]
        squares = jnp.zeros((SPAN, 128), F32)
        for lo in range(0, channels, HALF):
            sl = slice(lo, lo + HALF)
            carried = mm(c_t, incoming_ref[:, sl]).astype(BF16)
            gated = own_ref[rows, sl] + factor_ref[rows, sl] * carried
            gated_ref[rows, sl] = gated
            power = gated * gated
            pair = sum(power[:, half:half + 128] for half in range(0, HALF, 128))
            squares = squares + pair.astype(F32)
        square_ref[k:k + 1] = jnp.sum(squares.T, axis=0, keepdims=True)
    unused = square_ref.shape[0] - blocks
    if unused:
        square_ref[blocks:] = jnp.zeros((unused, SPAN), F32)


def joined(own, factor, c_t, incoming):
    length, channels = own.shape
    return pl.pallas_call(
        joined_kernel,
        in_specs=[WHOLE] * 4,
        out_specs=[WHOLE] * 2,
        out_shape=[
            pltpu.VMEM((length, channels), BF16),
            pltpu.VMEM((-(-length // SPAN // 8) * 8, SPAN), F32),
        ],
        compiler_params=PARAMS,
        cost_estimate=COST,
        name="joined",
    )(in_vmem(own), in_vmem(factor), in_vmem(c_t), incoming)


def norm_kernel(all_channels, seq_ref, square_ref, gain_ref, *refs):
    gated_refs, (out_hbm, staged, sems) = refs[:-3], refs[-3:]
    length, channels = gated_refs[0].shape
    blocks = length // SPAN
    stride = square_ref.shape[0] // len(gated_refs)
    copies = []
    for number, gated_ref in enumerate(gated_refs):
        s = lax.rem(seq_ref[0] + number, len(gated_refs))
        for k in range(blocks):
            rows = slice(k * SPAN, (k + 1) * SPAN)
            at = number * stride + k
            inverse = lax.rsqrt(square_ref[at:at + 1] / all_channels + 1e-05)
            column = jnp.broadcast_to(inverse, (128, SPAN)).T
            for lo in range(0, channels, 128):
                sl = slice(lo, lo + 128)
                staged[number, rows, sl] = (
                    gated_ref[rows, sl].astype(F32) * column * gain_ref[:, sl]
                ).astype(BF16)
            place = pl.ds(k * SPAN, SPAN)
            copies.append(
                pltpu.make_async_copy(
                    staged.at[number, place], out_hbm.at[s, place], sems.at[number * blocks + k]
                )
            )
            copies[-1].start(priority=k % 2)
    for copy in copies:
        copy.wait()


def normed(first, gated, squares, gain_row, all_channels):
    seqs = len(gated)
    length, channels = gated[0].shape
    return pl.pallas_call(
        functools.partial(norm_kernel, all_channels),
        in_specs=[pl.BlockSpec(memory_space=pltpu.SMEM)] + [WHOLE] * (2 + seqs),
        out_specs=ANYWHERE,
        out_shape=jax.ShapeDtypeStruct((seqs, length, channels), BF16),
        scratch_shapes=[
            pltpu.VMEM((seqs, length, channels), BF16),
            pltpu.SemaphoreType.DMA((seqs * (length // SPAN),)),
        ],
        compiler_params=STAGING_PARAMS,
        cost_estimate=COST,
        name="normed",
    )(first, squares, gain_row, *[in_vmem(one) for one in gated])


def from_partner(shard, axis, by):
    return lax.ppermute(shard, axis, [(i, i ^ by) for i in range(lax.axis_size(axis))])


def from_all(shard, axis):
    return [shard] + [from_partner(shard, axis, by) for by in range(1, lax.axis_size(axis))]


def as_parts(row):
    high = row.astype(BF16)
    low = (row - high.astype(F32)).astype(BF16)
    return jnp.concatenate([high, low, jnp.zeros((14, row.shape[1]), BF16)], axis=0)


def body(features, gate_in, state_proj, step_size, log_decay, skip_gain, norm_gain):
    seqs, length, channels = features.shape
    heads = step_size.shape[1]
    pair = np.repeat(np.concatenate([np.eye(heads)] * 2), channels // heads, axis=1)
    bands = jnp.asarray(np.concatenate([0 * pair, pair, 0 * pair]), BF16)
    until = np.tril(np.ones((SPAN, SPAN)))
    sums = jnp.asarray(np.concatenate([np.tile(until, 2), np.tile(np.eye(SPAN), 2)]), BF16)
    b_own, c_own = lax.optimization_barrier((state_proj[0], state_proj[1]))
    b_pieces = from_all(b_own, "head")
    b_near = jnp.concatenate(b_pieces[:2], axis=1)
    weighted, both, rows, bands = front(
        features, step_size, log_decay, skip_gain[None, :], sums, bands
    )

    place = lax.axis_index("ctx")
    even = place % 2 == 0
    mine = (place % 2).astype(jnp.int32)[None]
    devices = lax.axis_size("ctx")
    swap = [(i, i ^ 1) for i in range(devices)]
    total_at = TOTAL * (length // SPAN)
    decays = [rows[s, total_at:total_at + 1] for s in range(seqs)]
    decay = jnp.where(even, decays[0], decays[1])

    def past_chip(end, other, decay_other):
        return jnp.where(even, other + decay_other * end, end + decay * other)

    def across(past, entered, hop):
        sent = past if entered is None else past + decay_past * entered.astype(F32)
        sent = sent.astype(BF16)
        return sent, lax.ppermute(sent, "ctx", [(hop, hop + 2), (hop + 1, hop + 3)])

    near, near_ends = own_states(b_near, weighted, rows)
    near_rows = b_near.shape[1]
    other = lax.ppermute(
        jnp.concatenate([
            jnp.where(even, near_ends[1], near_ends[0]),
            as_parts(jnp.where(even, decays[1], decays[0])),
        ]),
        "ctx", swap,
    )
    near_other = other[:near_rows].astype(F32)
    decay_other = (
        other[near_rows:near_rows + 1].astype(F32) + other[near_rows + 1:near_rows + 2].astype(F32)
    )
    decay_past = decay_other * decay
    near_end = jnp.where(even, near_ends[0], near_ends[1]).astype(F32)
    near_past = past_chip(near_end, near_other, decay_other)
    near_sent, near_got = across(near_past, None, 0)
    b_far, _ = lax.optimization_barrier((b_pieces[2:], near_sent))
    b_far = jnp.concatenate(b_far, axis=1)
    far, far_ends = own_states(b_far, weighted, rows)
    far_other = lax.ppermute(jnp.where(even, far_ends[1], far_ends[0]), "ctx", swap).astype(F32)
    far_end = jnp.where(even, far_ends[0], far_ends[1]).astype(F32)
    far_past = past_chip(far_end, far_other, decay_other)
    far_sent, far_got = across(far_past, None, 0)
    c_own, _ = lax.optimization_barrier((c_own, near_ends))
    c = from_all(c_own, "head")
    both, _ = lax.optimization_barrier((both, far_sent))
    lifts = gates(mine, gate_in, features, both, bands, rows)
    both, lifts, c = lax.optimization_barrier((both, lifts, c))
    lifts_next = gates(1 - mine, gate_in, features, both, bands, rows)
    c, lifts_next = lax.optimization_barrier((c, lifts_next))
    b = jnp.concatenate([b_near, b_far], axis=1)
    c = jnp.concatenate(c, axis=1)
    terms = local_terms(mine, weighted, near, far, *lifts, b, c, rows)
    terms_next = local_terms(1 - mine, weighted, near, far, *lifts_next, b, c, rows)
    near_got, far_got, terms, terms_next = lax.optimization_barrier(
        (near_got, far_got, terms, terms_next)
    )
    for hop in range(2, devices - 2, 2):
        near_got = near_got + across(near_past, near_got, hop)[1]
        far_got = far_got + across(far_past, far_got, hop)[1]
    entered = jnp.concatenate([near_got, far_got])
    entered32 = entered.astype(F32)
    end = jnp.concatenate([near_end, far_end])
    end_other = jnp.concatenate([near_other, far_other])
    shared = lax.ppermute(
        jnp.where(even, end + decay * entered32, entered32).astype(BF16), "ctx", swap
    )
    incoming = jnp.where(even, entered32, end_other + decay_other * entered32).astype(BF16)
    gated, squares = joined(*terms, incoming)
    shared, _ = lax.optimization_barrier((shared, squares))
    gated_next, squares_next = joined(*terms_next, shared)
    squares = sum(from_all(jnp.concatenate([squares, squares_next]), "head"))
    return normed(
        mine, [gated, gated_next], squares, norm_gain[None, :],
        channels * lax.axis_size("head"),
    )


def solution(mesh):
    in_specs = (
        P("groups", "ctx", "head"),
        P("groups", "ctx", "head"),
        P(None, "groups", "head", "ctx"),
        P("groups", "head", "ctx"),
        P("groups", "head", "ctx"),
        P("head"),
        P("head"),
    )
    out_specs = P("groups", "ctx", "head")
    return jax.shard_map(body, mesh=mesh, in_specs=in_specs, out_specs=out_specs, check_vma=False)
```
